128 devices in a mesh: seq: 32 (over y, z, core), head: 4 (over x).
Axes of the slice: x: 4, y: 4, z: 4, core: 2. Of those that a mesh axis runs over, the one named last changes fastest.
Arguments:
- query: bfloat16 [8192, 2048], P('seq', 'head'), may hold values from -6 to 6
- key: bfloat16 [8192, 2048], P('seq', 'head'), may hold values from -6 to 6
- value: bfloat16 [8192, 4096], P('seq', 'head'), may hold values from -6 to 6
- beta: float32 [32, 8192], P('head', 'seq'), may hold values from 0 to 1, as said below
- decay: float32 [32, 8192], P('head', 'seq'), may hold values from -1 to 0, as said below
- wo_start: bfloat16 [2048, 4096], P('seq', 'head'), may hold values from -0.09375 to 0.09375
- wo_end: bfloat16 [2048, 4096], P('seq', 'head'), may hold values from -0.09375 to 0.09375
- curve_index: int32 [1], replicated, may hold values from 0 to 256
- cotangent: bfloat16 [8192, 2048], P('seq', 'head'), may hold values from -6 to 6
Outputs:
- mixed: bfloat16 [8192, 2048], P('seq', 'head')
- grad_query: float32 [8192, 2048], P('seq', 'head')
- grad_key: float32 [8192, 2048], P('seq', 'head')
- grad_value: float32 [8192, 4096], P('seq', 'head')
- grad_beta: float32 [32, 8192], P('head', 'seq')
- grad_decay: float32 [32, 8192], P('head', 'seq')
- grad_wo_start: float32 [2048, 4096], P('seq', 'head')
- grad_wo_end: float32 [2048, 4096], P('seq', 'head')
The draws below stay inside these ranges and needn't reach their ends.
Inputs may be any that keep to these rules, and one draw needn't show every extreme that they name: beta lies strictly between 0 and 1. decay is negative: each token's gate exp(decay) lies strictly between 0 and 1.
All inputs are finite; a program needn't handle non-finite values.
Results may differ from the reference program's by a relative error of at most 0.02.
Values may be sent and summed in bfloat16 or wider, within the bound.
No kernel may reach another device: no remote copies, remote signals or barrier semaphores. Data moves between devices by JAX's collectives and lax.ppermute only.
A program may use at most 192 MiB of HBM per device.

```python
import math
import jax
import jax.numpy as jnp
from jax import lax

D = 2048
HV = 32
HK = 16
DK = 128
DV = 128
TOK_DEV = 256
CURVE_POINTS = 257
SPAN = 128
TOKEN_TOTAL = 8192


def head_plan(key, slow_share):
    picks = jax.random.uniform(jax.random.fold_in(key, 101), (HV,))
    slow = picks < slow_share
    blocks = TOKEN_TOTAL // TOK_DEV
    spread = jnp.exp(jax.random.uniform(jax.random.fold_in(key, 102), (HV, blocks), minval=-0.7, maxval=0.7))
    spread = jnp.repeat(spread, TOK_DEV, axis=1)
    return (slow, spread)


def draw_decay(key, part):
    share = 0.5
    slow, spread = head_plan(key, share)
    key = jax.random.fold_in(key, 7)
    fast_rate = jnp.exp(jax.random.uniform(jax.random.fold_in(key, 1), (HV, 1), minval=math.log(1.0 / 50.0), maxval=math.log(1.0 / 30.0)))
    slow_rate = 0.3 / TOKEN_TOTAL
    jitter = jax.random.uniform(jax.random.fold_in(key, 2), (HV, TOKEN_TOTAL), minval=0.5, maxval=1.5)
    decay_speed = jnp.where(slow[:, None], slow_rate, fast_rate) * spread * jitter
    position_list = jax.random.randint(jax.random.fold_in(key, 3), (HV, 3), 0, TOKEN_TOTAL)
    sudden_jump = jnp.any(position_list[:, :, None] == jnp.arange(TOKEN_TOTAL, dtype=jnp.int32)[None, None, :], axis=1)
    value_fall = jnp.log(jax.random.uniform(jax.random.fold_in(key, 4), (HV, TOKEN_TOTAL), minval=0.5, maxval=0.8))
    return jnp.where(sudden_jump, value_fall, -decay_speed).astype(jnp.float32)


def draw_beta(key, part):
    share = 0.5
    slow, spread = head_plan(key, share)
    key = jax.random.fold_in(key, 9)
    fast_value = jax.random.uniform(jax.random.fold_in(key, 1), (HV, TOKEN_TOTAL), minval=0.2, maxval=0.9)
    slow_value = jax.random.uniform(jax.random.fold_in(key, 2), (HV, TOKEN_TOTAL), minval=0.2, maxval=0.6) * spread * (DK / TOKEN_TOTAL)
    return jnp.where(slow[:, None], slow_value, fast_value).astype(jnp.float32)


def raised(drawn, rng, source, target, parts, factor):
    def block_of(dim):
        return (jnp.arange(drawn.shape[dim]) // (drawn.shape[dim] // parts)).reshape((-1,) + (1,) * (drawn.ndim - 1 - dim))

    near = jax.random.permutation(rng, parts)[block_of(target)]
    far = (block_of(target) + parts // 2) % parts
    return jnp.where((block_of(source) == near) | (block_of(source) == far), factor * drawn, drawn)


def level_of(stream_key, dims, cuts, low, largest):
    loudness, own = 1.0, jax.random.fold_in(stream_key, 6)
    for dim, blocks in cuts:
        heights = jnp.exp(jax.random.uniform(jax.random.fold_in(own, dim), (blocks,), jnp.float32, low / len(cuts), largest / len(cuts)))
        loudness = loudness * jnp.repeat(heights, dims[dim] // blocks).reshape([-1 if axis == dim else 1 for axis in range(len(dims))])
    return loudness


def centred(key, extent, deviation, reach, cuts=(), kind=jnp.bfloat16):
    values = deviation * jax.random.normal(key, extent, jnp.float32)
    if cuts:
        values = values * level_of(key, extent, cuts, -0.22, 0.18)
    return jnp.clip(values, -reach, reach).astype(kind)


def gaussian_with(stream_key, extent, scale, most, split, heavy, kind=jnp.bfloat16):
    entries = scale * jax.random.normal(stream_key, extent, jnp.float32)
    if split:
        entries = entries * level_of(stream_key, extent, split, -0.22, 0.18)
    return jnp.clip(raised(entries, jax.random.fold_in(stream_key, 3), *heavy), -most, most).astype(kind)


def setup_inputs(seed: int = 0) -> dict:
    key_of = jax.random.split(jax.random.key(seed), 10)
    query = centred(key_of[0], (TOKEN_TOTAL, HK * DK), 1.0, 6.0, ((0, 32), (1, 4)))
    key = centred(key_of[1], (TOKEN_TOTAL, HK * DK), 1.0, 6.0, ((0, 32), (1, 4)))
    value = centred(key_of[2], (TOKEN_TOTAL, HV * DV), 1.0, 6.0, ((0, 32), (1, 4)))
    beta = draw_beta(jax.random.fold_in(key_of[9], 71), 0)
    decay = draw_decay(jax.random.fold_in(key_of[9], 71), 0)
    wo_start = centred(key_of[5], (D, HV * DV), (HV * DV) ** -0.5, 0.09375, ((0, 32), (1, 4)))
    wo_end = centred(key_of[6], (D, HV * DV), (HV * DV) ** -0.5, 0.09375, ((0, 32), (1, 4)))
    curve_index = jax.random.randint(key_of[7], (1,), 0, CURVE_POINTS).astype(jnp.int32)
    cotangent = gaussian_with(key_of[8], (TOKEN_TOTAL, D), 1.0, 6.0, ((0, 32), (1, 4)), (0, 1, 32, 2.75))
    return dict(query=query, key=key, value=value, beta=beta, decay=decay, wo_start=wo_start, wo_end=wo_end, curve_index=curve_index, cotangent=cotangent)


norm_eps = 1e-06

def matmul_high(left, right):
    return jnp.matmul(left, right, precision=lax.Precision.HIGHEST)

def flip_last(matrix):
    return jnp.swapaxes(matrix, -1, -2)

def gram_low(left, right):
    return lax.dot_general(left.astype(jnp.bfloat16), right.astype(jnp.bfloat16), (((2,), (2,)), ((0,), (0,))), preferred_element_type=jnp.float32)

def unit_inverse(lower):
    size = lower.shape[-1]
    negated = -lower
    result = jnp.eye(size, dtype=lower.dtype) + negated
    power = negated
    for level in range(size.bit_length() - 2):
        power = matmul_high(power, power)
        result = result + matmul_high(result, power)
    return result

def span_parts(queries, keys, values, betas, decays):
    size = queries.shape[1]
    cumulative = jnp.cumsum(decays, axis=-1)
    growth = jnp.exp(cumulative)
    row_ids = lax.broadcasted_iota(jnp.int32, (size, size), 0)
    col_ids = lax.broadcasted_iota(jnp.int32, (size, size), 1)
    inclusive = row_ids >= col_ids
    strict = row_ids > col_ids
    spread = cumulative[:, :, None] - cumulative[:, None, :]
    ratio = jnp.where(inclusive, jnp.exp(jnp.minimum(spread, 0.0)), 0.0)
    lower = jnp.where(strict, betas[:, :, None] * gram_low(keys, keys) * ratio, 0.0)
    inverse = unit_inverse(lower)
    weights = matmul_high(inverse, (betas * growth)[:, :, None] * keys)
    written = matmul_high(inverse, betas[:, :, None] * values)
    attend = jnp.where(inclusive, gram_low(queries, keys) * ratio, 0.0)
    tail = jnp.exp(cumulative[:, -1:] - cumulative)[:, :, None] * keys
    return (growth, attend, weights, written, tail)

def span_step(state, pieces):
    queries, keys, values, betas, decays = pieces
    growth, attend, weights, written, tail = span_parts(queries, keys, values, betas, decays)
    update = written - matmul_high(weights, flip_last(state))
    output = growth[:, :, None] * matmul_high(queries, flip_last(state)) + matmul_high(attend, update)
    last_growth = growth[:, -1][:, None, None]
    new_state = last_growth * state + matmul_high(flip_last(update), tail)
    return (new_state, output)

def recurrence(query, key, value, beta, decay):
    tokens = query.shape[0]
    group = HV // HK
    keyed = key.reshape(tokens, HK, DK)
    keyed = keyed * lax.rsqrt(lax.optimization_barrier(jnp.sum(keyed * keyed, axis=-1, keepdims=True)) + norm_eps)
    key_full = jnp.repeat(keyed, group, axis=1)
    query_full = jnp.repeat(query.reshape(tokens, HK, DK), group, axis=1)
    value_full = value.reshape(tokens, HV, DV)
    blocks = tokens // SPAN

    def arrange(array):
        return array.reshape(blocks, SPAN, HV, array.shape[-1]).transpose(0, 2, 1, 3)

    def arrange_rates(array):
        return array.reshape(HV, blocks, SPAN).transpose(1, 0, 2)
    advance = jax.checkpoint(span_step)
    initial = jnp.zeros((HV, DV, DK), jnp.float32)
    final, outputs = lax.scan(advance, initial, (arrange(query_full), arrange(key_full), arrange(value_full), arrange_rates(beta), arrange_rates(decay)))
    return outputs.transpose(0, 2, 1, 3).reshape(tokens, HV * DV)

def reference(query, key, value, beta, decay, wo_start, wo_end, curve_index, cotangent):
    position = curve_index[0].astype(jnp.float32) / (CURVE_POINTS - 1)
    weight_point = ((1.0 - position) * wo_start.astype(jnp.float32) + position * wo_end.astype(jnp.float32)).astype(jnp.bfloat16)
    inputs = (query.astype(jnp.float32), key.astype(jnp.float32), value.astype(jnp.float32), beta, decay)
    heads_out, pullback = jax.vjp(recurrence, *inputs)
    tokens = heads_out.shape[0]
    grouped = heads_out.reshape(tokens, HV, DV)
    scale = lax.rsqrt(lax.optimization_barrier(jnp.mean(grouped * grouped, axis=-1, keepdims=True)) + norm_eps)
    normalized_rows = (grouped * scale).reshape(tokens, HV * DV).astype(jnp.bfloat16)
    mixed = lax.dot_general(normalized_rows, weight_point, (((1,), (1,)), ((), ())), preferred_element_type=jnp.float32).astype(jnp.bfloat16)
    grad_normed = jnp.dot(cotangent, weight_point, preferred_element_type=jnp.float32)
    grad_weight = lax.dot_general(cotangent, normalized_rows, (((0,), (0,)), ((), ())), preferred_element_type=jnp.float32)
    grad_grouped = grad_normed.reshape(tokens, HV, DV)
    inner = lax.optimization_barrier(jnp.mean(grad_grouped * grouped, axis=-1, keepdims=True))
    grad_heads = scale * grad_grouped - scale * scale * scale * grouped * inner
    grad_query, grad_key, grad_value, grad_beta, grad_decay = pullback(grad_heads.reshape(tokens, HV * DV))
    return (mixed, grad_query, grad_key, grad_value, grad_beta, grad_decay, (1.0 - position) * grad_weight, position * grad_weight)
```

```python
import jax
import jax.numpy as jnp
from jax import lax
from jax.experimental import pallas as pl
from jax.experimental.pallas import tpu as pltpu
from jax.sharding import Mesh, PartitionSpec as P

DK = 128
CURVE_POINTS = 257
EPS = 1e-06
NY, NZ, NC, NH = 4, 4, 2, 4
SEG = NZ * NC
TOK = 256
HALF = 128
KEYS = 4
ROWS = 272
BF = jnp.bfloat16
F32 = jnp.float32
RING = ("y", "z", "c")
INTERPRET = False


def dot(left, right, dims):
    return lax.dot_general(
        left.astype(BF), right.astype(BF), (dims, ((), ())), preferred_element_type=F32
    )


def mm(left, right):
    return dot(left, right, ((1,), (0,)))


def mm_nt(left, right):
    return dot(left, right, ((1,), (1,)))


def mm_tn(left, right):
    return dot(left, right, ((0,), (0,)))


def iota(shape, dim):
    return lax.broadcasted_iota(jnp.int32, shape, dim)


def lane_sum(array):
    return jnp.sum(array, axis=1, keepdims=True)


def call(kernel, out_shape, grid, in_specs, out_specs, args, flops, scratch=(), prefetch=None):
    bytes_moved = sum(a.size * a.dtype.itemsize for a in (*args, *out_shape))
    spec = dict(grid=grid, in_specs=in_specs, out_specs=out_specs, scratch_shapes=list(scratch))
    extra = {}
    if prefetch is None:
        extra = spec
    else:
        extra = dict(grid_spec=pltpu.PrefetchScalarGridSpec(num_scalar_prefetch=1, **spec))
        args = (prefetch, *args)
    return pl.pallas_call(
        kernel,
        out_shape=out_shape,
        compiler_params=pltpu.CompilerParams(vmem_limit_bytes=48 * 2**20),
        cost_estimate=pl.CostEstimate(
            flops=flops, bytes_accessed=bytes_moved, transcendentals=0
        ),
        interpret=INTERPRET,
        **extra,
    )(*args)


def shape(*dims, dtype=F32):
    return jax.ShapeDtypeStruct(dims, dtype)


def whole(array):
    return pl.BlockSpec(array.shape, lambda *_: (0,) * len(array.shape))


def heads_spec(rows, cols):
    return pl.BlockSpec((2, rows, cols), lambda j: (j, 0, 0))


def lead_spec(rows, cols):
    return pl.BlockSpec((1, rows, cols), lambda j: (j, 0, 0))


def wide_spec(cols):
    return pl.BlockSpec((TOK, cols), lambda j: (0, j))


def unit_keys(key_block):
    raw = key_block.astype(F32)
    rate = lax.rsqrt(lane_sum(raw * raw) + EPS)
    return raw * rate, rate


def prefix_lanes(array):
    size = array.shape[1]
    lane = iota(array.shape, 1)
    step = 1
    while step < size:
        array = array + jnp.where(lane >= step, pltpu.roll(array, step, 1), 0.0)
        step *= 2
    return array


def suffix_lanes(array):
    size = array.shape[1]
    lane = iota(array.shape, 1)
    step = 1
    while step < size:
        array = array + jnp.where(lane < size - step, pltpu.roll(array, size - step, 1), 0.0)
        step *= 2
    return array


def invert_blocks(lowers):
    row, col = iota((HALF, HALF), 0), iota((HALF, HALF), 1)
    apart = row ^ col
    eye = jnp.where(row == col, 1.0, 0.0)
    found = [eye - jnp.where(apart < 2, low, 0.0) for low in lowers]
    size = 2
    while size < HALF:
        mask = (apart >= size) & (apart < 2 * size)
        offs = [jnp.where(mask, low, 0.0).astype(BF) for low in lowers]
        lows = [x.astype(BF) for x in found]
        halfway = [mm(x, off) for x, off in zip(lows, offs)]
        found = [f - mm(m, x) for f, m, x in zip(found, halfway, lows)]
        size *= 2
    return found


def pre_kernel(k_ref, v_ref, beta_ref, decay_ref, pay_ref, x_ref, wu_ref, c_ref, cols_ref):
    j = pl.program_id(0)

    @pl.when(j == 0)
    def _():
        c_ref[...] = prefix_lanes(decay_ref[...])

    unit, _ = unit_keys(k_ref[...])
    low = unit.astype(BF)
    gram = mm_nt(low, low)
    rows = [c_ref[pl.ds(2 * j + a, 1), :] for a in range(2)]
    rates = [beta_ref[pl.ds(2 * j + a, 1), :] for a in range(2)]
    sub = iota((8, TOK), 0)
    packed = jnp.zeros((8, TOK), F32)
    for place, line in enumerate((*rows, *rates)):
        packed = jnp.where(sub == place, line, packed)
    cols = jnp.transpose(jnp.concatenate([packed, jnp.zeros((HALF - 8, TOK), F32)], axis=0))
    cols_ref[0] = cols
    strict = iota((TOK, TOK), 0) > iota((TOK, TOK), 1)
    lowers = []
    for a in range(2):
        ratio = jnp.exp(jnp.minimum(cols[:, a : a + 1] - rows[a], 0.0))
        lowers.append(jnp.where(strict, cols[:, 2 + a : 3 + a] * gram * ratio, 0.0))
    found = invert_blocks(
        [low[b * HALF : (b + 1) * HALF, b * HALF : (b + 1) * HALF] for low in lowers for b in (0, 1)]
    )
    for a in range(2):
        first, second = found[2 * a].astype(BF), found[2 * a + 1].astype(BF)
        corner = -mm(mm(second, lowers[a][HALF:, :HALF]), first)
        inverse = jnp.concatenate(
            [
                jnp.concatenate([first, jnp.zeros((HALF, HALF), BF)], axis=1),
                jnp.concatenate([corner.astype(BF), second], axis=1),
            ],
            axis=0,
        )
        x_ref[a] = inverse
        c_col, beta_col = cols[:, a : a + 1], cols[:, 2 + a : 3 + a]
        value = v_ref[:, a * DK : (a + 1) * DK].astype(F32)
        right = jnp.concatenate(
            [(beta_col * jnp.exp(c_col) * unit).astype(BF), (beta_col * value).astype(BF)], axis=1
        )
        wu = mm(inverse, right).astype(BF)
        wu_ref[a] = wu
        end = c_col[TOK - 1 : TOK, :]
        tail = (jnp.exp(end - c_col) * unit).astype(BF)
        pay_ref[a, : 2 * DK, :] = mm_tn(wu, tail).astype(BF)
        gate = jnp.broadcast_to(jnp.exp(end), (16, DK))
        one = gate.astype(BF)
        two = (gate - one.astype(F32)).astype(BF)
        three = (gate - one.astype(F32) - two.astype(F32)).astype(BF)
        place = iota((16, DK), 0)
        pay_ref[a, 2 * DK :, :] = jnp.where(
            place == 0,
            one.astype(F32),
            jnp.where(
                place == 1, two.astype(F32), jnp.where(place == 2, three.astype(F32), 0.0)
            ),
        ).astype(BF)


def gate_of(block):
    return jnp.sum(block[2 * DK :, :].astype(F32), axis=0, keepdims=True)


def pre_pass(key, value, beta, decay):
    heads = 2 * KEYS
    return call(
        pre_kernel,
        (
            shape(heads, ROWS, DK, dtype=BF),
            shape(heads, TOK, TOK, dtype=BF),
            shape(heads, TOK, 2 * DK, dtype=BF),
            shape(heads, TOK),
            shape(KEYS, TOK, DK),
        ),
        (KEYS,),
        [wide_spec(DK), wide_spec(2 * DK), whole(beta), whole(decay)],
        (
            heads_spec(ROWS, DK),
            heads_spec(TOK, TOK),
            heads_spec(TOK, 2 * DK),
            whole(decay),
            lead_spec(TOK, DK),
        ),
        (key, value, beta, decay),
        2 * 10**9,
    )


def attend_kernel(q_ref, k_ref, c_ref, cols_ref, x_ref, wu_ref, p_ref, car_ref, out_ref, xz_ref):
    j = pl.program_id(0)
    unit, _ = unit_keys(k_ref[...])
    query = q_ref[...]
    gram = mm_nt(query, unit)
    cols = cols_ref[0]
    inclusive = iota((TOK, TOK), 0) >= iota((TOK, TOK), 1)
    for a in range(2):
        c_col = cols[:, a : a + 1]
        ratio = jnp.exp(jnp.minimum(c_col - c_ref[pl.ds(2 * j + a, 1), :], 0.0))
        attend = jnp.where(inclusive, gram * ratio, 0.0).astype(BF)
        p_ref[a] = attend
        both = mm(attend, wu_ref[a])
        car_ref[a] = (jnp.exp(c_col) * query.astype(F32) - both[:, :DK]).astype(BF)
        out_ref[a] = both[:, DK:]
        tail = jnp.exp(c_col[TOK - 1 : TOK, :] - c_col) * unit
        xz_ref[a] = mm_tn(x_ref[a], tail).astype(BF)


def attend_pass(query, key, cums, cols, inverse, wu):
    heads = 2 * KEYS
    return call(
        attend_kernel,
        (
            shape(heads, TOK, TOK, dtype=BF),
            shape(heads, TOK, DK, dtype=BF),
            shape(heads, TOK, DK),
            shape(heads, TOK, DK, dtype=BF),
        ),
        (KEYS,),
        [
            wide_spec(DK),
            wide_spec(DK),
            whole(cums),
            lead_spec(TOK, DK),
            heads_spec(TOK, TOK),
            heads_spec(TOK, 2 * DK),
        ],
        (
            heads_spec(TOK, TOK),
            heads_spec(TOK, DK),
            heads_spec(TOK, DK),
            heads_spec(TOK, DK),
        ),
        (query, key, cums, cols, inverse, wu),
        10**9,
    )


def prefix_kernel(pay_ref, nx_ref, bx_ref, gx_ref, tot_ref):
    both = jnp.zeros((2 * DK, DK), F32)
    gate = jnp.ones((1, DK), F32)
    for i in range(SEG):
        nx_ref[i] = both[:DK].astype(BF)
        bx_ref[i] = both[DK:]
        gx_ref[i : i + 1, :] = gate
        block = pay_ref[i]
        step_gate = gate_of(block)
        moved = block[:DK].astype(F32)
        both = (
            step_gate * both
            - mm(both, block[:DK])
            + jnp.concatenate([gate * moved, block[DK : 2 * DK].astype(F32)], axis=0)
        )
        gate = gate * step_gate
    tot_ref[: 2 * DK, :] = both.astype(BF)
    full = jnp.broadcast_to(gate, (16, DK))
    one = full.astype(BF)
    two = (full - one.astype(F32)).astype(BF)
    three = (full - one.astype(F32) - two.astype(F32)).astype(BF)
    place = iota((16, DK), 0)
    tot_ref[2 * DK :, :] = jnp.where(
        place == 0,
        one.astype(F32),
        jnp.where(place == 1, two.astype(F32), jnp.where(place == 2, three.astype(F32), 0.0)),
    ).astype(BF)


def prefix_pass(pay):
    outs = (
        shape(SEG, DK, DK, dtype=BF),
        shape(SEG, DK, DK),
        shape(SEG, DK),
        shape(ROWS, DK, dtype=BF),
    )
    return call(
        prefix_kernel, outs, (1,), [whole(pay)], tuple(whole(o) for o in outs), (pay,), 10**8
    )


def suffix_kernel(pay_ref, ns_ref, gs_ref):
    later = jnp.zeros((DK, DK), F32)
    gate = jnp.ones((1, DK), F32)
    for i in reversed(range(SEG)):
        ns_ref[i] = later.astype(BF)
        gs_ref[i : i + 1, :] = gate
        block = pay_ref[i]
        step_gate = gate_of(block)
        moved = block[:DK]
        later = step_gate * later + gate * moved.astype(F32) - mm(moved, later)
        gate = gate * step_gate


def suffix_pass(pay):
    outs = (shape(SEG, DK, DK, dtype=BF), shape(SEG, DK))
    return call(
        suffix_kernel, outs, (1,), [whole(pay)], tuple(whole(o) for o in outs), (pay,), 10**8
    )


def enter_kernel(place_ref, one_ref, two_ref, three_ref, nx_ref, bx_ref, gx_ref, s_ref):
    here = place_ref[1]
    state = jnp.zeros((DK, DK), F32)
    for back, ref in ((3, three_ref), (2, two_ref), (1, one_ref)):
        block = ref[...]
        moved = (
            gate_of(block) * state - mm(state, block[:DK]) + block[DK : 2 * DK].astype(F32)
        )
        state = jnp.where(here >= back, moved, state)
    for i in range(SEG):
        s_ref[i] = (gx_ref[i : i + 1, :] * state - mm(state, nx_ref[i]) + bx_ref[i]).astype(BF)


def enter_pass(place, totals, nx, bx, gx):
    out = shape(SEG, DK, DK, dtype=BF)
    args = (*totals, nx, bx, gx)
    return call(
        enter_kernel,
        (out,),
        (1,),
        [whole(a) for a in args],
        (whole(out),),
        args,
        10**8,
        prefetch=place,
    )[0]


def norm_kernel(s_ref, car_ref, loc_ref, gn_ref, norm_ref, do_ref, dir_ref):
    for a in range(2):
        carried = car_ref[a]
        head = loc_ref[a] + mm_nt(carried, s_ref[a])
        scale = lax.rsqrt(lane_sum(head * head) * (1.0 / DK) + EPS)
        normed = head * scale
        norm_ref[:, a * DK : (a + 1) * DK] = normed.astype(BF)
        grad = gn_ref[:, a * DK : (a + 1) * DK]
        inner = lane_sum(grad * normed) * (1.0 / DK)
        back = (scale * (grad - normed * inner)).astype(BF)
        do_ref[a] = back
        dir_ref[a] = mm_tn(back, carried).astype(BF)


def norm_pass(state, carried, local, grad_normed):
    heads = 2 * KEYS
    return call(
        norm_kernel,
        (
            shape(TOK, heads * DK, dtype=BF),
            shape(heads, TOK, DK, dtype=BF),
            shape(heads, DK, DK, dtype=BF),
        ),
        (KEYS,),
        [heads_spec(DK, DK), heads_spec(TOK, DK), heads_spec(TOK, DK), wide_spec(2 * DK)],
        (wide_spec(2 * DK), heads_spec(TOK, DK), heads_spec(DK, DK)),
        (state, carried, local, grad_normed),
        10**8,
    )


def middle_kernel(
    q_ref, k_ref, v_ref, c_ref, cols_ref, s_ref, do_ref, p_ref, x_ref, wu_ref,
    dq_ref, u_ref, dk_ref, e_ref, y_ref, dcc_ref, dcr_ref,
):
    j = pl.program_id(0)
    unit, _ = unit_keys(k_ref[...])
    low = unit.astype(BF)
    query = q_ref[...]
    wide = query.astype(F32)
    cols = cols_ref[0]
    inclusive = iota((TOK, TOK), 0) >= iota((TOK, TOK), 1)
    lane = iota((TOK, DK), 1)
    sub = iota((8, TOK), 0)
    down = jnp.zeros((TOK, DK), F32)
    across = jnp.zeros((8, TOK), F32)
    pair_sum = jnp.zeros((TOK, TOK), F32)
    grad_query = jnp.zeros((TOK, DK), F32)
    for a in range(2):
        c_col = cols[:, a : a + 1]
        growth = jnp.exp(c_col)
        state, back, attend = s_ref[a], do_ref[a], p_ref[a]
        update = (wu_ref[a, :, DK:].astype(F32) - mm_nt(wu_ref[a, :, :DK], state)).astype(BF)
        u_ref[a] = update
        pairs = mm_nt(back, update)
        ratio = jnp.exp(jnp.minimum(c_col - c_ref[pl.ds(2 * j + a, 1), :], 0.0))
        pair_sum += jnp.where(inclusive, pairs * ratio, 0.0)
        shares = pairs * attend.astype(F32)
        reached = growth * mm(back, state)
        grad_query += reached
        down = jnp.where(lane == a, lane_sum(shares) + lane_sum(reached * wide), down)
        across = jnp.where(sub == a, -jnp.sum(shares, axis=0, keepdims=True), across)
        e_ref[a] = mm_tn(x_ref[a], mm_tn(attend, back))
        value = v_ref[:, a * DK : (a + 1) * DK].astype(F32)
        y_ref[a] = (value - growth * mm_nt(low, state)).astype(BF)
    pair_low = pair_sum.astype(BF)
    dq_ref[...] = grad_query + mm(pair_low, low)
    dk_ref[...] = mm_tn(pair_low, query)
    dcc_ref[0] = down
    dcr_ref[0] = across


def middle_pass(query, key, value, cums, cols, state, back, attend, inverse, wu):
    heads = 2 * KEYS
    return call(
        middle_kernel,
        (
            shape(TOK, KEYS * DK),
            shape(heads, TOK, DK, dtype=BF),
            shape(TOK, KEYS * DK),
            shape(heads, TOK, DK),
            shape(heads, TOK, DK, dtype=BF),
            shape(KEYS, TOK, DK),
            shape(KEYS, 8, TOK),
        ),
        (KEYS,),
        [
            wide_spec(DK),
            wide_spec(DK),
            wide_spec(2 * DK),
            whole(cums),
            lead_spec(TOK, DK),
            heads_spec(DK, DK),
            heads_spec(TOK, DK),
            heads_spec(TOK, TOK),
            heads_spec(TOK, TOK),
            heads_spec(TOK, 2 * DK),
        ],
        (
            wide_spec(DK),
            heads_spec(TOK, DK),
            wide_spec(DK),
            heads_spec(TOK, DK),
            heads_spec(TOK, DK),
            lead_spec(TOK, DK),
            lead_spec(8, TOK),
        ),
        (query, key, value, cums, cols, state, back, attend, inverse, wu),
        2 * 10**9,
    )


def later_kernel(pay_ref, dir_ref, d_ref, tot_ref):
    total = jnp.zeros((DK, DK), F32)
    for i in reversed(range(SEG)):
        d_ref[i] = total
        block = pay_ref[i]
        total = gate_of(block) * total - mm_nt(total, block[:DK]) + dir_ref[i].astype(F32)
    tot_ref[...] = total.astype(BF)


def later_pass(pay, direct):
    outs = (shape(SEG, DK, DK), shape(DK, DK, dtype=BF))
    args = (pay, direct)
    return call(
        later_kernel,
        outs,
        (1,),
        [whole(a) for a in args],
        tuple(whole(o) for o in outs),
        args,
        10**8,
    )


def leave_kernel(
    place_ref, one_ref, two_ref, three_ref, g1_ref, g2_ref, g3_ref, ns_ref, gs_ref, d_ref, g_ref
):
    here = place_ref[1]
    total = jnp.zeros((DK, DK), F32)
    for ahead, ref, grad in ((3, one_ref, g3_ref), (2, two_ref, g2_ref), (1, three_ref, g1_ref)):
        block = ref[...]
        moved = gate_of(block) * total - mm_nt(total, block[:DK]) + grad[...].astype(F32)
        total = jnp.where(here + ahead < NY, moved, total)
    for i in range(SEG):
        g_ref[i] = (gs_ref[i : i + 1, :] * total - mm_nt(total, ns_ref[i]) + d_ref[i]).astype(BF)


def leave_pass(place, totals, grads, ns, gs, directs):
    out = shape(SEG, DK, DK, dtype=BF)
    args = (*totals, *grads, ns, gs, directs)
    return call(
        leave_kernel,
        (out,),
        (1,),
        [whole(a) for a in args],
        (whole(out),),
        args,
        10**8,
        prefetch=place,
    )[0]


def last_kernel(
    k_ref, c_ref, cols_ref, s_ref, g_ref, e_ref, y_ref, u_ref, xz_ref, dk0_ref, dcc_ref, dcr_ref,
    dv_ref, dk_ref, db_ref, dd_ref,
):
    j = pl.program_id(0)
    unit, rate = unit_keys(k_ref[...])
    low = unit.astype(BF)
    gram = mm_nt(low, low)
    cols = cols_ref[0]
    strict = iota((TOK, TOK), 0) > iota((TOK, TOK), 1)
    last = iota((TOK, 1), 0) == TOK - 1
    lane = iota((TOK, DK), 1)
    down = jnp.zeros((TOK, DK), F32)
    pair_sum = jnp.zeros((TOK, TOK), F32)
    grad_key = dk0_ref[...]
    across = []
    for a in range(2):
        c_col, beta_col = cols[:, a : a + 1], cols[:, 2 + a : 3 + a]
        growth = jnp.exp(c_col)
        end = c_col[TOK - 1 : TOK, :]
        state, later, update = s_ref[a], g_ref[a], u_ref[a]
        error = e_ref[a] + mm_nt(xz_ref[a], later)
        ratio = jnp.exp(jnp.minimum(c_col - c_ref[pl.ds(2 * j + a, 1), :], 0.0))
        pairs = jnp.where(strict, -mm_nt(error, update) * ratio, 0.0)
        shares = pairs * gram
        row_share = lane_sum(shares)
        across.append(jnp.sum(beta_col * shares, axis=0, keepdims=True))
        pair_sum += beta_col * pairs
        grad_value = beta_col * error
        dv_ref[:, a * DK : (a + 1) * DK] = grad_value
        reached = growth * mm(grad_value, state)
        tail = jnp.exp(end - c_col) * mm(update, later)
        grad_key += tail - reached
        tail_share = lane_sum(tail * unit)
        gate_share = jnp.exp(end) * jnp.sum(
            lane_sum(state.astype(F32) * later.astype(F32)), axis=0, keepdims=True
        )
        total = jnp.sum(tail_share, axis=0, keepdims=True) + gate_share
        grad_cum = beta_col * row_share - lane_sum(reached * unit) - tail_share
        grad_cum += jnp.where(last, total, 0.0)
        grad_beta = row_share + lane_sum(error * y_ref[a].astype(F32))
        down = jnp.where(lane == a, grad_cum, jnp.where(lane == 2 + a, grad_beta, down))
    pair_low = pair_sum.astype(BF)
    grad_key += mm(pair_low, low) + mm_tn(pair_low, low)
    dk_ref[...] = rate * (grad_key - unit * lane_sum(unit * grad_key))
    turned = jnp.transpose(down + jnp.where(lane < 2, dcc_ref[0], 0.0))[:8]
    sub = iota((8, TOK), 0)
    cum = turned + dcr_ref[0]
    for a in range(2):
        cum = jnp.where(sub == a, cum - across[a], cum)
    decayed = suffix_lanes(cum)
    for a in range(2):
        mine = sub == 2 * j + a
        dd_ref[...] = jnp.where(mine, decayed[a : a + 1], dd_ref[...])
        db_ref[...] = jnp.where(mine, turned[2 + a : 3 + a], db_ref[...])


def last_pass(key, cums, cols, state, later, error, y, update, xz, dk0, dcc, dcr):
    heads = 2 * KEYS
    return call(
        last_kernel,
        (
            shape(TOK, heads * DK),
            shape(TOK, KEYS * DK),
            shape(heads, TOK),
            shape(heads, TOK),
        ),
        (KEYS,),
        [
            wide_spec(DK),
            whole(cums),
            lead_spec(TOK, DK),
            heads_spec(DK, DK),
            heads_spec(DK, DK),
            heads_spec(TOK, DK),
            heads_spec(TOK, DK),
            heads_spec(TOK, DK),
            heads_spec(TOK, DK),
            wide_spec(DK),
            lead_spec(TOK, DK),
            lead_spec(8, TOK),
        ],
        (wide_spec(2 * DK), wide_spec(DK), whole(cums), whole(cums)),
        (key, cums, cols, state, later, error, y, update, xz, dk0, dcc, dcr),
        2 * 10**9,
    )


def back_kernel(place_ref, cot_ref, w_ref, out_ref):
    part = mm(cot_ref[0], w_ref[...])

    @pl.when(pl.program_id(0) == 0)
    def _():
        out_ref[...] = part

    @pl.when(pl.program_id(0) > 0)
    def _():
        out_ref[...] += part


def back_pass(place, cot, weight):
    depth, wide = cot.shape[2], weight.shape[1]
    out = shape(TOK, wide)
    return call(
        back_kernel,
        (out,),
        (NH,),
        [
            pl.BlockSpec((1, TOK, depth), lambda k, place: (k, 0, 0)),
            pl.BlockSpec((depth, wide), lambda k, place: ((place[0] + k) % NH, 0)),
        ],
        (whole(out),),
        (cot, weight),
        2 * TOK * NH * depth * wide,
        prefetch=place,
    )[0]


def mix_kernel(place_ref, norm_ref, w_ref, out_ref):
    out_ref[0] = mm_nt(norm_ref[...], w_ref[...]).astype(BF)


def mix_pass(place, normed, weight):
    depth = weight.shape[0] // NH
    out = shape(NH, TOK, depth, dtype=BF)
    return call(
        mix_kernel,
        (out,),
        (NH,),
        [
            whole(normed),
            pl.BlockSpec((depth, weight.shape[1]), lambda k, place: ((place[0] + k) % NH, 0)),
        ],
        (pl.BlockSpec((1, TOK, depth), lambda k, place: (k, 0, 0)),),
        (normed, weight),
        2 * TOK * weight.size,
        prefetch=place,
    )[0]


def outer_kernel(place_ref, cot_ref, norm_ref, mine_ref, other_ref):
    here, core = place_ref[2], place_ref[3]
    rows = mine_ref.shape[2]
    for k in range(NZ):
        start = pl.multiple_of(((here + k) % NZ) * 2 * rows, 2 * rows)
        part = mm_tn(cot_ref[0, :, pl.ds(start, 2 * rows)], norm_ref[...]).astype(BF)
        first = core == 0
        mine_ref[0, k] = jnp.where(first, part[:rows], part[rows:])
        other_ref[0, k] = jnp.where(first, part[rows:], part[:rows])


def outer_pass(place, cot, normed):
    rows = cot.shape[2] // (NZ * NC)
    out = shape(NY, NZ, rows, normed.shape[1], dtype=BF)
    spec = pl.BlockSpec((1, NZ, rows, normed.shape[1]), lambda k, place: (k, 0, 0, 0))
    return call(
        outer_kernel,
        (out, out),
        (NY,),
        [
            pl.BlockSpec(
                (1, TOK, cot.shape[2]), lambda k, place: ((place[1] + k - place[0] + NH) % NH, 0, 0)
            ),
            whole(normed),
        ],
        (spec, spec),
        (cot, normed),
        2 * cot.size * normed.shape[1],
        prefetch=place,
    )


def shift(array, axis, count, step):
    return lax.ppermute(array, axis, [(i, (i + step) % count) for i in range(count)])


def scatter_stage(parts, axis, count):
    total = parts[0].astype(F32)
    moved = [shift(parts[k].astype(BF), axis, count, k) for k in range(1, count)]
    for part in moved:
        total = total + part.astype(F32)
    return total


def body(query, key, value, beta, decay, wo_start, wo_end, curve_index, cotangent):
    place = jnp.stack([lax.axis_index(a) for a in ("head", "y", "z", "c")]).astype(jnp.int32)
    position = curve_index[0].astype(F32) / (CURVE_POINTS - 1)
    weight_local = (
        (1.0 - position) * wo_start.astype(F32) + position * wo_end.astype(F32)
    ).astype(BF)
    weight = lax.all_gather(weight_local, RING, axis=0, tiled=True)
    cot = jnp.stack([cotangent] + [shift(cotangent, "head", NH, -k) for k in range(1, NH)])

    pay, inverse, wu, cums, cols = pre_pass(key, value, beta, decay)
    pays = lax.all_to_all(pay, ("z", "c"), 0, 0, tiled=True)
    attend, carried, local, xz = attend_pass(query, key, cums, cols, inverse, wu)
    nx, bx, gx, total = prefix_pass(pays)
    totals = [shift(total, "y", NY, k) for k in range(1, NY)]
    ns, gs = suffix_pass(pays)
    states = enter_pass(place, totals, nx, bx, gx)
    state = lax.all_to_all(states, ("z", "c"), 0, 0, tiled=True)
    grad_normed = back_pass(place, cot, weight)
    normed, back, direct = norm_pass(state, carried, local, grad_normed)

    directs = lax.all_to_all(direct, ("z", "c"), 0, 0, tiled=True)
    mine, other = outer_pass(place, cot, normed)
    got = lax.ppermute(other, "c", [(0, 1), (1, 0)])
    grad_query, update, dk0, error, y, dcc, dcr = middle_pass(
        query, key, value, cums, cols, state, back, attend, inverse, wu
    )
    mixes = mix_pass(place, normed, weight)
    mixed = scatter_stage([mixes[k] for k in range(NH)], "head", NH).astype(BF)
    suffixes, grad_total = later_pass(pays, directs)
    grads = [shift(grad_total, "y", NY, -k) for k in range(1, NY)]
    laters = leave_pass(place, totals, grads, ns, gs, suffixes)
    later = lax.all_to_all(laters, ("z", "c"), 0, 0, tiled=True)

    pair = mine.astype(F32) + got.astype(F32)
    wide = pair.shape[-1] // 2
    left, right = pair[..., :wide], pair[..., wide:]
    left = scatter_stage([left[:, k] for k in range(NZ)], "z", NZ)
    right = scatter_stage([right[k] for k in range(NY)], "y", NY)
    left = scatter_stage([left[k] for k in range(NY)], "y", NY)
    right = scatter_stage([right[k] for k in range(NZ)], "z", NZ)
    grad_weight = jnp.concatenate([left, right], axis=-1)

    grad_value, grad_key, grad_beta, grad_decay = last_pass(
        key, cums, cols, state, later, error, y, update, xz, dk0, dcc, dcr
    )
    return (
        mixed,
        grad_query,
        grad_key,
        grad_value,
        grad_beta,
        grad_decay,
        (1.0 - position) * grad_weight,
        position * grad_weight,
    )


def solution(mesh):
    fine = Mesh(mesh.devices.reshape(NY, NZ, NC, NH), ("y", "z", "c", "head"))
    rows, flipped = P(RING, "head"), P("head", RING)
    return jax.shard_map(
        body,
        mesh=fine,
        in_specs=(rows, rows, rows, flipped, flipped, rows, rows, P(), rows),
        out_specs=(rows, rows, rows, rows, flipped, flipped, rows, rows),
        check_vma=False,
    )
```

```python
import jax
import jax.numpy as jnp
from jax import lax
from jax.experimental import pallas as pl
from jax.experimental.pallas import tpu as pltpu
from jax.sharding import Mesh, PartitionSpec as P

DK = 128
CURVE_POINTS = 257
EPS = 1e-06
NY, NZ, NC, NH = 4, 4, 2, 4
SEG = NZ * NC
TOK = 256
HALF = 128
KEYS = 4
ROWS = 272
BF = jnp.bfloat16
F32 = jnp.float32
RING = ("y", "z", "c")
INTERPRET = False


def dot(left, right, dims):
    return lax.dot_general(
        left.astype(BF), right.astype(BF), (dims, ((), ())), preferred_element_type=F32
    )


def mm(left, right):
    return dot(left, right, ((1,), (0,)))


def mm_nt(left, right):
    return dot(left, right, ((1,), (1,)))


def mm_tn(left, right):
    return dot(left, right, ((0,), (0,)))


def iota(shape, dim):
    return lax.broadcasted_iota(jnp.int32, shape, dim)


def lane_sum(array):
    return jnp.sum(array, axis=1, keepdims=True)


def call(kernel, out_shape, grid, in_specs, out_specs, args, flops, prefetch=None, after=()):
    count = len(args) + (prefetch is not None)

    def run(*refs):
        kernel(*refs[:count], *refs[count + len(after) :])

    in_specs = [*in_specs, *(pl.BlockSpec(memory_space=pl.ANY) for _ in after)]
    bytes_moved = sum(a.size * a.dtype.itemsize for a in (*args, *out_shape))
    args = (*args, *after)
    spec = dict(grid=grid, in_specs=in_specs, out_specs=out_specs)
    extra = {}
    if prefetch is None:
        extra = spec
    else:
        extra = dict(grid_spec=pltpu.PrefetchScalarGridSpec(num_scalar_prefetch=1, **spec))
        args = (prefetch, *args)
    return pl.pallas_call(
        run,
        out_shape=out_shape,
        compiler_params=pltpu.CompilerParams(vmem_limit_bytes=60 * 2**20),
        cost_estimate=pl.CostEstimate(
            flops=flops, bytes_accessed=bytes_moved, transcendentals=0
        ),
        interpret=INTERPRET,
        name=kernel.__name__,
        **extra,
    )(*args)


def shape(*dims, dtype=F32):
    return jax.ShapeDtypeStruct(dims, dtype)


def whole(array):
    return pl.BlockSpec(array.shape, lambda *_: (0,) * len(array.shape))


def heads_spec(rows, cols):
    return pl.BlockSpec((2, rows, cols), lambda j: (j, 0, 0))


def lead_spec(rows, cols):
    return pl.BlockSpec((1, rows, cols), lambda j: (j, 0, 0))


def wide_spec(cols):
    return pl.BlockSpec((TOK, cols), lambda j: (0, j))


def unit_keys(key_block):
    raw = key_block.astype(F32)
    rate = lax.rsqrt(lane_sum(raw * raw) + EPS)
    return raw * rate, rate


def prefix_lanes(array):
    size = array.shape[1]
    lane = iota(array.shape, 1)
    step = 1
    while step < size:
        array = array + jnp.where(lane >= step, pltpu.roll(array, step, 1), 0.0)
        step *= 2
    return array


def suffix_lanes(array):
    size = array.shape[1]
    lane = iota(array.shape, 1)
    step = 1
    while step < size:
        array = array + jnp.where(lane < size - step, pltpu.roll(array, size - step, 1), 0.0)
        step *= 2
    return array


def invert_blocks(lowers):
    row, col = iota((HALF, HALF), 0), iota((HALF, HALF), 1)
    apart = row ^ col
    eye = jnp.where(row == col, 1.0, 0.0)
    found = [eye - jnp.where(apart < 2, low, 0.0) for low in lowers]
    size = 2
    while size < HALF:
        mask = (apart >= size) & (apart < 2 * size)
        offs = [jnp.where(mask, low, 0.0).astype(BF) for low in lowers]
        lows = [x.astype(BF) for x in found]
        halfway = [mm(x, off) for x, off in zip(lows, offs)]
        found = [f - mm(m, x) for f, m, x in zip(found, halfway, lows)]
        size *= 2
    return found


def pre_kernel(k_ref, v_ref, beta_ref, decay_ref, pay_ref, x_ref, wu_ref, c_ref, cols_ref):
    j = pl.program_id(0)

    @pl.when(j == 0)
    def _():
        c_ref[...] = prefix_lanes(decay_ref[...])

    unit, _ = unit_keys(k_ref[...])
    low = unit.astype(BF)
    gram = mm_nt(low, low)
    rows = [c_ref[pl.ds(2 * j + a, 1), :] for a in range(2)]
    rates = [beta_ref[pl.ds(2 * j + a, 1), :] for a in range(2)]
    sub = iota((8, TOK), 0)
    packed = jnp.zeros((8, TOK), F32)
    for place, line in enumerate((*rows, *rates)):
        packed = jnp.where(sub == place, line, packed)
    cols = jnp.transpose(jnp.concatenate([packed, jnp.zeros((HALF - 8, TOK), F32)], axis=0))
    cols_ref[0] = cols
    strict = iota((TOK, TOK), 0) > iota((TOK, TOK), 1)
    lowers = []
    for a in range(2):
        ratio = jnp.exp(jnp.minimum(cols[:, a : a + 1] - rows[a], 0.0))
        lowers.append(jnp.where(strict, cols[:, 2 + a : 3 + a] * gram * ratio, 0.0))
    found = invert_blocks(
        [low[b * HALF : (b + 1) * HALF, b * HALF : (b + 1) * HALF] for low in lowers for b in (0, 1)]
    )
    for a in range(2):
        first, second = found[2 * a].astype(BF), found[2 * a + 1].astype(BF)
        corner = -mm(mm(second, lowers[a][HALF:, :HALF]), first)
        inverse = jnp.concatenate(
            [
                jnp.concatenate([first, jnp.zeros((HALF, HALF), BF)], axis=1),
                jnp.concatenate([corner.astype(BF), second], axis=1),
            ],
            axis=0,
        )
        x_ref[a] = inverse
        c_col, beta_col = cols[:, a : a + 1], cols[:, 2 + a : 3 + a]
        value = v_ref[:, a * DK : (a + 1) * DK].astype(F32)
        right = jnp.concatenate(
            [(beta_col * jnp.exp(c_col) * unit).astype(BF), (beta_col * value).astype(BF)], axis=1
        )
        wu = mm(inverse, right).astype(BF)
        wu_ref[a] = wu
        end = c_col[TOK - 1 : TOK, :]
        tail = (jnp.exp(end - c_col) * unit).astype(BF)
        pay_ref[a, : 2 * DK, :] = mm_tn(wu, tail).astype(BF)
        gate = jnp.broadcast_to(jnp.exp(end), (16, DK))
        one = gate.astype(BF)
        two = (gate - one.astype(F32)).astype(BF)
        three = (gate - one.astype(F32) - two.astype(F32)).astype(BF)
        place = iota((16, DK), 0)
        pay_ref[a, 2 * DK :, :] = jnp.where(
            place == 0,
            one.astype(F32),
            jnp.where(
                place == 1, two.astype(F32), jnp.where(place == 2, three.astype(F32), 0.0)
            ),
        ).astype(BF)


def gate_of(block):
    return jnp.sum(block[2 * DK :, :].astype(F32), axis=0, keepdims=True)


def pre_pass(key, value, beta, decay):
    heads = 2 * KEYS
    return call(
        pre_kernel,
        (
            shape(heads, ROWS, DK, dtype=BF),
            shape(heads, TOK, TOK, dtype=BF),
            shape(heads, TOK, 2 * DK, dtype=BF),
            shape(heads, TOK),
            shape(KEYS, TOK, DK),
        ),
        (KEYS,),
        [wide_spec(DK), wide_spec(2 * DK), whole(beta), whole(decay)],
        (
            heads_spec(ROWS, DK),
            heads_spec(TOK, TOK),
            heads_spec(TOK, 2 * DK),
            whole(decay),
            lead_spec(TOK, DK),
        ),
        (key, value, beta, decay),
        2 * 10**9,
    )


def attend_kernel(q_ref, k_ref, c_ref, cols_ref, x_ref, wu_ref, p_ref, car_ref, out_ref, xz_ref):
    j = pl.program_id(0)
    unit, _ = unit_keys(k_ref[...])
    query = q_ref[...]
    gram = mm_nt(query, unit)
    cols = cols_ref[0]
    inclusive = iota((TOK, TOK), 0) >= iota((TOK, TOK), 1)
    for a in range(2):
        c_col = cols[:, a : a + 1]
        ratio = jnp.exp(jnp.minimum(c_col - c_ref[pl.ds(2 * j + a, 1), :], 0.0))
        attend = jnp.where(inclusive, gram * ratio, 0.0).astype(BF)
        p_ref[a] = attend
        both = mm(attend, wu_ref[a])
        car_ref[a] = (jnp.exp(c_col) * query.astype(F32) - both[:, :DK]).astype(BF)
        out_ref[a] = both[:, DK:]
        tail = jnp.exp(c_col[TOK - 1 : TOK, :] - c_col) * unit
        xz_ref[a] = mm_tn(x_ref[a], tail).astype(BF)


def attend_pass(query, key, cums, cols, inverse, wu):
    heads = 2 * KEYS
    return call(
        attend_kernel,
        (
            shape(heads, TOK, TOK, dtype=BF),
            shape(heads, TOK, DK, dtype=BF),
            shape(heads, TOK, DK),
            shape(heads, TOK, DK, dtype=BF),
        ),
        (KEYS,),
        [
            wide_spec(DK),
            wide_spec(DK),
            whole(cums),
            lead_spec(TOK, DK),
            heads_spec(TOK, TOK),
            heads_spec(TOK, 2 * DK),
        ],
        (
            heads_spec(TOK, TOK),
            heads_spec(TOK, DK),
            heads_spec(TOK, DK),
            heads_spec(TOK, DK),
        ),
        (query, key, cums, cols, inverse, wu),
        10**9,
    )


def prefix_kernel(pay_ref, nx_ref, bx_ref, gx_ref, tot_ref):
    both = jnp.zeros((2 * DK, DK), F32)
    gate = jnp.ones((1, DK), F32)
    for i in range(SEG):
        nx_ref[i] = both[:DK].astype(BF)
        bx_ref[i] = both[DK:]
        gx_ref[i : i + 1, :] = gate
        block = pay_ref[i]
        step_gate = gate_of(block)
        moved = block[:DK].astype(F32)
        both = (
            step_gate * both
            - mm(both, block[:DK])
            + jnp.concatenate([gate * moved, block[DK : 2 * DK].astype(F32)], axis=0)
        )
        gate = gate * step_gate
    tot_ref[: 2 * DK, :] = both.astype(BF)
    full = jnp.broadcast_to(gate, (16, DK))
    one = full.astype(BF)
    two = (full - one.astype(F32)).astype(BF)
    three = (full - one.astype(F32) - two.astype(F32)).astype(BF)
    place = iota((16, DK), 0)
    tot_ref[2 * DK :, :] = jnp.where(
        place == 0,
        one.astype(F32),
        jnp.where(place == 1, two.astype(F32), jnp.where(place == 2, three.astype(F32), 0.0)),
    ).astype(BF)


def prefix_pass(pay):
    outs = (
        shape(SEG, DK, DK, dtype=BF),
        shape(SEG, DK, DK),
        shape(SEG, DK),
        shape(ROWS, DK, dtype=BF),
    )
    return call(
        prefix_kernel, outs, (1,), [whole(pay)], tuple(whole(o) for o in outs), (pay,), 10**8
    )


def suffix_kernel(pay_ref, ns_ref, gs_ref):
    later = jnp.zeros((DK, DK), F32)
    gate = jnp.ones((1, DK), F32)
    for i in reversed(range(SEG)):
        ns_ref[i] = later.astype(BF)
        gs_ref[i : i + 1, :] = gate
        block = pay_ref[i]
        step_gate = gate_of(block)
        moved = block[:DK]
        later = step_gate * later + gate * moved.astype(F32) - mm(moved, later)
        gate = gate * step_gate


def suffix_pass(pay):
    outs = (shape(SEG, DK, DK, dtype=BF), shape(SEG, DK))
    return call(
        suffix_kernel, outs, (1,), [whole(pay)], tuple(whole(o) for o in outs), (pay,), 10**8
    )


def enter_kernel(place_ref, one_ref, two_ref, three_ref, nx_ref, bx_ref, gx_ref, s_ref):
    here = place_ref[1]
    state = jnp.zeros((DK, DK), F32)
    for back, ref in ((3, three_ref), (2, two_ref), (1, one_ref)):
        block = ref[...]
        moved = (
            gate_of(block) * state - mm(state, block[:DK]) + block[DK : 2 * DK].astype(F32)
        )
        state = jnp.where(here >= back, moved, state)
    for i in range(SEG):
        s_ref[i] = (gx_ref[i : i + 1, :] * state - mm(state, nx_ref[i]) + bx_ref[i]).astype(BF)


def enter_pass(place, totals, nx, bx, gx):
    out = shape(SEG, DK, DK, dtype=BF)
    args = (*totals, nx, bx, gx)
    return call(
        enter_kernel,
        (out,),
        (1,),
        [whole(a) for a in args],
        (whole(out),),
        args,
        10**8,
        prefetch=place,
    )[0]


def norm_kernel(s_ref, car_ref, loc_ref, gn_ref, norm_ref, do_ref, dir_ref):
    for a in range(2):
        carried = car_ref[a]
        head = loc_ref[a] + mm_nt(carried, s_ref[a])
        scale = lax.rsqrt(lane_sum(head * head) * (1.0 / DK) + EPS)
        normed = head * scale
        norm_ref[:, a * DK : (a + 1) * DK] = normed.astype(BF)
        grad = gn_ref[:, a * DK : (a + 1) * DK]
        inner = lane_sum(grad * normed) * (1.0 / DK)
        back = (scale * (grad - normed * inner)).astype(BF)
        do_ref[a] = back
        dir_ref[a] = mm_tn(back, carried).astype(BF)


def norm_pass(state, carried, local, grad_normed):
    heads = 2 * KEYS
    return call(
        norm_kernel,
        (
            shape(TOK, heads * DK, dtype=BF),
            shape(heads, TOK, DK, dtype=BF),
            shape(heads, DK, DK, dtype=BF),
        ),
        (KEYS,),
        [heads_spec(DK, DK), heads_spec(TOK, DK), heads_spec(TOK, DK), wide_spec(2 * DK)],
        (wide_spec(2 * DK), heads_spec(TOK, DK), heads_spec(DK, DK)),
        (state, carried, local, grad_normed),
        10**8,
    )


def middle_kernel(
    q_ref, k_ref, v_ref, c_ref, cols_ref, s_ref, do_ref, p_ref, x_ref, wu_ref,
    dq_ref, u_ref, dk_ref, e_ref, y_ref, dcc_ref, dcr_ref,
):
    j = pl.program_id(0)
    unit, _ = unit_keys(k_ref[...])
    low = unit.astype(BF)
    query = q_ref[...]
    wide = query.astype(F32)
    cols = cols_ref[0]
    inclusive = iota((TOK, TOK), 0) >= iota((TOK, TOK), 1)
    lane = iota((TOK, DK), 1)
    sub = iota((8, TOK), 0)
    down = jnp.zeros((TOK, DK), F32)
    across = jnp.zeros((8, TOK), F32)
    pair_sum = jnp.zeros((TOK, TOK), F32)
    grad_query = jnp.zeros((TOK, DK), F32)
    for a in range(2):
        c_col = cols[:, a : a + 1]
        growth = jnp.exp(c_col)
        state, back, attend = s_ref[a], do_ref[a], p_ref[a]
        update = (wu_ref[a, :, DK:].astype(F32) - mm_nt(wu_ref[a, :, :DK], state)).astype(BF)
        u_ref[a] = update
        pairs = mm_nt(back, update)
        ratio = jnp.exp(jnp.minimum(c_col - c_ref[pl.ds(2 * j + a, 1), :], 0.0))
        pair_sum += jnp.where(inclusive, pairs * ratio, 0.0)
        shares = pairs * attend.astype(F32)
        reached = growth * mm(back, state)
        grad_query += reached
        down = jnp.where(lane == a, lane_sum(shares) + lane_sum(reached * wide), down)
        across = jnp.where(sub == a, -jnp.sum(shares, axis=0, keepdims=True), across)
        e_ref[a] = mm_tn(x_ref[a], mm_tn(attend, back))
        value = v_ref[:, a * DK : (a + 1) * DK].astype(F32)
        y_ref[a] = (value - growth * mm_nt(low, state)).astype(BF)
    pair_low = pair_sum.astype(BF)
    dq_ref[...] = grad_query + mm(pair_low, low)
    dk_ref[...] = mm_tn(pair_low, query)
    dcc_ref[0] = down
    dcr_ref[0] = across


def middle_pass(query, key, value, cums, cols, state, back, attend, inverse, wu, after):
    heads = 2 * KEYS
    return call(
        middle_kernel,
        (
            shape(TOK, KEYS * DK),
            shape(heads, TOK, DK, dtype=BF),
            shape(TOK, KEYS * DK),
            shape(heads, TOK, DK),
            shape(heads, TOK, DK, dtype=BF),
            shape(KEYS, TOK, DK),
            shape(KEYS, 8, TOK),
        ),
        (KEYS,),
        [
            wide_spec(DK),
            wide_spec(DK),
            wide_spec(2 * DK),
            whole(cums),
            lead_spec(TOK, DK),
            heads_spec(DK, DK),
            heads_spec(TOK, DK),
            heads_spec(TOK, TOK),
            heads_spec(TOK, TOK),
            heads_spec(TOK, 2 * DK),
        ],
        (
            wide_spec(DK),
            heads_spec(TOK, DK),
            wide_spec(DK),
            heads_spec(TOK, DK),
            heads_spec(TOK, DK),
            lead_spec(TOK, DK),
            lead_spec(8, TOK),
        ),
        (query, key, value, cums, cols, state, back, attend, inverse, wu),
        2 * 10**9,
        after=after,
    )


def later_kernel(pay_ref, dir_ref, d_ref, tot_ref):
    total = jnp.zeros((DK, DK), F32)
    for i in reversed(range(SEG)):
        d_ref[i] = total
        block = pay_ref[i]
        total = gate_of(block) * total - mm_nt(total, block[:DK]) + dir_ref[i].astype(F32)
    tot_ref[...] = total.astype(BF)


def later_pass(pay, direct, after):
    outs = (shape(SEG, DK, DK), shape(DK, DK, dtype=BF))
    args = (pay, direct)
    return call(
        later_kernel,
        outs,
        (1,),
        [whole(a) for a in args],
        tuple(whole(o) for o in outs),
        args,
        10**8,
        after=after,
    )


def leave_kernel(
    place_ref, one_ref, two_ref, three_ref, g1_ref, g2_ref, g3_ref, ns_ref, gs_ref, d_ref, g_ref
):
    here = place_ref[1]
    total = jnp.zeros((DK, DK), F32)
    for ahead, ref, grad in ((3, one_ref, g3_ref), (2, two_ref, g2_ref), (1, three_ref, g1_ref)):
        block = ref[...]
        moved = gate_of(block) * total - mm_nt(total, block[:DK]) + grad[...].astype(F32)
        total = jnp.where(here + ahead < NY, moved, total)
    for i in range(SEG):
        g_ref[i] = (gs_ref[i : i + 1, :] * total - mm_nt(total, ns_ref[i]) + d_ref[i]).astype(BF)


def leave_pass(place, totals, grads, ns, gs, directs, after):
    out = shape(SEG, DK, DK, dtype=BF)
    args = (*totals, *grads, ns, gs, directs)
    return call(
        leave_kernel,
        (out,),
        (1,),
        [whole(a) for a in args],
        (whole(out),),
        args,
        10**8,
        prefetch=place,
        after=after,
    )[0]


def last_kernel(
    k_ref, c_ref, cols_ref, s_ref, g_ref, e_ref, y_ref, u_ref, xz_ref, dk0_ref, dcc_ref, dcr_ref,
    dv_ref, dk_ref, db_ref, dd_ref,
):
    j = pl.program_id(0)
    unit, rate = unit_keys(k_ref[...])
    low = unit.astype(BF)
    gram = mm_nt(low, low)
    cols = cols_ref[0]
    strict = iota((TOK, TOK), 0) > iota((TOK, TOK), 1)
    last = iota((TOK, 1), 0) == TOK - 1
    lane = iota((TOK, DK), 1)
    down = jnp.zeros((TOK, DK), F32)
    pair_sum = jnp.zeros((TOK, TOK), F32)
    grad_key = dk0_ref[...]
    across = []
    for a in range(2):
        c_col, beta_col = cols[:, a : a + 1], cols[:, 2 + a : 3 + a]
        growth = jnp.exp(c_col)
        end = c_col[TOK - 1 : TOK, :]
        state, later, update = s_ref[a], g_ref[a], u_ref[a]
        error = e_ref[a] + mm_nt(xz_ref[a], later)
        ratio = jnp.exp(jnp.minimum(c_col - c_ref[pl.ds(2 * j + a, 1), :], 0.0))
        pairs = jnp.where(strict, -mm_nt(error, update) * ratio, 0.0)
        shares = pairs * gram
        row_share = lane_sum(shares)
        across.append(jnp.sum(beta_col * shares, axis=0, keepdims=True))
        pair_sum += beta_col * pairs
        grad_value = beta_col * error
        dv_ref[:, a * DK : (a + 1) * DK] = grad_value
        reached = growth * mm(grad_value, state)
        tail = jnp.exp(end - c_col) * mm(update, later)
        grad_key += tail - reached
        tail_share = lane_sum(tail * unit)
        gate_share = jnp.exp(end) * jnp.sum(
            lane_sum(state.astype(F32) * later.astype(F32)), axis=0, keepdims=True
        )
        total = jnp.sum(tail_share, axis=0, keepdims=True) + gate_share
        grad_cum = beta_col * row_share - lane_sum(reached * unit) - tail_share
        grad_cum += jnp.where(last, total, 0.0)
        grad_beta = row_share + lane_sum(error * y_ref[a].astype(F32))
        down = jnp.where(lane == a, grad_cum, jnp.where(lane == 2 + a, grad_beta, down))
    pair_low = pair_sum.astype(BF)
    grad_key += mm(pair_low, low) + mm_tn(pair_low, low)
    dk_ref[...] = rate * (grad_key - unit * lane_sum(unit * grad_key))
    turned = jnp.transpose(down + jnp.where(lane < 2, dcc_ref[0], 0.0))[:8]
    sub = iota((8, TOK), 0)
    cum = turned + dcr_ref[0]
    for a in range(2):
        cum = jnp.where(sub == a, cum - across[a], cum)
    decayed = suffix_lanes(cum)
    for a in range(2):
        mine = sub == 2 * j + a
        dd_ref[...] = jnp.where(mine, decayed[a : a + 1], dd_ref[...])
        db_ref[...] = jnp.where(mine, turned[2 + a : 3 + a], db_ref[...])


def last_pass(key, cums, cols, state, later, error, y, update, xz, dk0, dcc, dcr, after):
    heads = 2 * KEYS
    return call(
        last_kernel,
        (
            shape(TOK, heads * DK),
            shape(TOK, KEYS * DK),
            shape(heads, TOK),
            shape(heads, TOK),
        ),
        (KEYS,),
        [
            wide_spec(DK),
            whole(cums),
            lead_spec(TOK, DK),
            heads_spec(DK, DK),
            heads_spec(DK, DK),
            heads_spec(TOK, DK),
            heads_spec(TOK, DK),
            heads_spec(TOK, DK),
            heads_spec(TOK, DK),
            wide_spec(DK),
            lead_spec(TOK, DK),
            lead_spec(8, TOK),
        ],
        (wide_spec(2 * DK), wide_spec(DK), whole(cums), whole(cums)),
        (key, cums, cols, state, later, error, y, update, xz, dk0, dcc, dcr),
        2 * 10**9,
        after=after,
    )


def back_kernel(place_ref, cot_ref, w_ref, out_ref):
    part = mm(cot_ref[0], w_ref[...])

    @pl.when(pl.program_id(0) == 0)
    def _():
        out_ref[...] = part

    @pl.when(pl.program_id(0) > 0)
    def _():
        out_ref[...] += part


def back_pass(place, cot, weight):
    depth, wide = cot.shape[2], weight.shape[1]
    out = shape(TOK, wide)
    return call(
        back_kernel,
        (out,),
        (NH,),
        [
            pl.BlockSpec((1, TOK, depth), lambda k, place: (k, 0, 0)),
            pl.BlockSpec((depth, wide), lambda k, place: ((place[0] + k) % NH, 0)),
        ],
        (whole(out),),
        (cot, weight),
        2 * TOK * NH * depth * wide,
        prefetch=place,
    )[0]


def mix_kernel(place_ref, norm_ref, w_ref, out_ref):
    out_ref[0] = mm_nt(norm_ref[...], w_ref[...]).astype(BF)


def mix_pass(place, normed, weight, after):
    depth = weight.shape[0] // NH
    out = shape(NH, TOK, depth, dtype=BF)
    return call(
        mix_kernel,
        (out,),
        (NH,),
        [
            whole(normed),
            pl.BlockSpec((depth, weight.shape[1]), lambda k, place: ((place[0] + k) % NH, 0)),
        ],
        (pl.BlockSpec((1, TOK, depth), lambda k, place: (k, 0, 0)),),
        (normed, weight),
        2 * TOK * weight.size,
        prefetch=place,
        after=after,
    )[0]


def outer_kernel(place_ref, cot_ref, norm_ref, mine_ref, other_ref):
    here, core = place_ref[2], place_ref[3]
    rows = mine_ref.shape[2]
    for k in range(NZ):
        start = pl.multiple_of(((here + k) % NZ) * 2 * rows, 2 * rows)
        part = mm_tn(cot_ref[0, :, pl.ds(start, 2 * rows)], norm_ref[...]).astype(BF)
        first = core == 0
        mine_ref[0, k] = jnp.where(first, part[:rows], part[rows:])
        other_ref[0, k] = jnp.where(first, part[rows:], part[:rows])


def outer_pass(place, cot, normed):
    rows = cot.shape[2] // (NZ * NC)
    out = shape(NY, NZ, rows, normed.shape[1], dtype=BF)
    spec = pl.BlockSpec((1, NZ, rows, normed.shape[1]), lambda k, place: (k, 0, 0, 0))
    return call(
        outer_kernel,
        (out, out),
        (NY,),
        [
            pl.BlockSpec(
                (1, TOK, cot.shape[2]), lambda k, place: ((place[1] + k - place[0] + NH) % NH, 0, 0)
            ),
            whole(normed),
        ],
        (spec, spec),
        (cot, normed),
        2 * cot.size * normed.shape[1],
        prefetch=place,
    )


def shift(array, axis, count, step):
    return lax.ppermute(array, axis, [(i, (i + step) % count) for i in range(count)])


def scatter_stage(parts, axis, count):
    total = parts[0].astype(F32)
    for k in range(1, count):
        total = total + shift(parts[k], axis, count, k).astype(F32)
    return total


def body(query, key, value, beta, decay, wo_start, wo_end, curve_index, cotangent):
    place = jnp.stack([lax.axis_index(a) for a in ("head", "y", "z", "c")]).astype(jnp.int32)
    position = curve_index[0].astype(F32) / (CURVE_POINTS - 1)
    weight_local = (
        (1.0 - position) * wo_start.astype(F32) + position * wo_end.astype(F32)
    ).astype(BF)
    weight = lax.all_gather(weight_local, RING, axis=0, tiled=True)
    cot = jnp.stack([cotangent] + [shift(cotangent, "head", NH, -k) for k in range(1, NH)])

    pay, inverse, wu, cums, cols = pre_pass(key, value, beta, decay)
    pays = lax.all_to_all(pay, ("z", "c"), 0, 0, tiled=True)
    attend, carried, local, xz = attend_pass(query, key, cums, cols, inverse, wu)
    nx, bx, gx, total = prefix_pass(pays)
    totals = [shift(total, "y", NY, k) for k in range(1, NY)]
    ns, gs = suffix_pass(pays)
    states = enter_pass(place, totals, nx, bx, gx)
    state = lax.all_to_all(states, ("z", "c"), 0, 0, tiled=True)
    grad_normed = back_pass(place, cot, weight)
    normed, back, direct = norm_pass(state, carried, local, grad_normed)

    directs = lax.all_to_all(direct, ("z", "c"), 0, 0, tiled=True)
    mine, other = outer_pass(place, cot, normed)
    got = lax.ppermute(other, "c", [(0, 1), (1, 0)])
    pair = mine.astype(F32) + got.astype(F32)
    wide = pair.shape[-1] // 2
    left = [pair[:, k, :, :wide].astype(BF) for k in range(NZ)]
    right = [pair[k, :, :, wide:].astype(BF) for k in range(NY)]
    grad_query, update, dk0, error, y, dcc, dcr = middle_pass(
        query, key, value, cums, cols, state, back, attend, inverse, wu, (left[0],)
    )
    suffixes, grad_total = later_pass(pays, directs, (*left, *right))
    grads = [shift(grad_total, "y", NY, -k) for k in range(1, NY)]
    mixes = mix_pass(place, normed, weight, (grad_total,))
    mixed = scatter_stage([mixes[k] for k in range(NH)], "head", NH).astype(BF)
    laters = leave_pass(place, totals, grads, ns, gs, suffixes, (dk0,))
    later = lax.all_to_all(laters, ("z", "c"), 0, 0, tiled=True)
    left = scatter_stage(left, "z", NZ).astype(BF)
    right = scatter_stage(right, "y", NY).astype(BF)

    grad_value, grad_key, grad_beta, grad_decay = last_pass(
        key, cums, cols, state, later, error, y, update, xz, dk0, dcc, dcr, (left, right)
    )
    left = scatter_stage([left[k] for k in range(NY)], "y", NY)
    right = scatter_stage([right[k] for k in range(NZ)], "z", NZ)
    grad_weight = jnp.concatenate([left, right], axis=-1)
    return (
        mixed,
        grad_query,
        grad_key,
        grad_value,
        grad_beta,
        grad_decay,
        (1.0 - position) * grad_weight,
        position * grad_weight,
    )


def solution(mesh):
    fine = Mesh(mesh.devices.reshape(NY, NZ, NC, NH), ("y", "z", "c", "head"))
    rows, flipped = P(RING, "head"), P("head", RING)
    return jax.shard_map(
        body,
        mesh=fine,
        in_specs=(rows, rows, rows, flipped, flipped, rows, rows, P(), rows),
        out_specs=(rows, rows, rows, rows, flipped, flipped, rows, rows),
        check_vma=False,
    )
```

```python
import jax
import jax.numpy as jnp
from jax import lax
from jax.experimental import pallas as pl
from jax.experimental.pallas import tpu as pltpu
from jax.sharding import Mesh, PartitionSpec as P

DK = 128
DV = 128
CURVE_POINTS = 257
EPS = 1e-06
NY, NZ, NC, NH = 4, 4, 2, 4
TOK = 256
HALF = 128
KEYS = 4
ROWS = 272
GROUP = 4
VMEM = 14 * 2**20
SHORT = 10**6
LONG = 5 * 10**9
BF = jnp.bfloat16
F32 = jnp.float32
RING = ("y", "z", "c")
INTERPRET = False


def dot(left, right, dims):
    return lax.dot_general(
        left.astype(BF), right.astype(BF), (dims, ((), ())), preferred_element_type=F32
    )


def mm(left, right):
    return dot(left, right, ((1,), (0,)))


def mm_nt(left, right):
    return dot(left, right, ((1,), (1,)))


def mm_tn(left, right):
    return dot(left, right, ((0,), (0,)))


def iota(shape, dim):
    return lax.broadcasted_iota(jnp.int32, shape, dim)


def lane_sum(array):
    return jnp.sum(array, axis=1, keepdims=True)


def call(
    kernel, out_shape, grid, in_specs, out_specs, args, flops, prefetch=None, after=(), vmem=VMEM
):
    count = len(args) + (prefetch is not None)

    def run(*refs):
        kernel(*refs[:count], *refs[count + len(after) :])

    in_specs = [*in_specs, *(pl.BlockSpec(memory_space=pl.ANY) for _ in after)]
    args = (*args, *after)
    spec = dict(grid=grid, in_specs=in_specs, out_specs=out_specs)
    extra = {}
    if prefetch is None:
        extra = spec
    else:
        extra = dict(grid_spec=pltpu.PrefetchScalarGridSpec(num_scalar_prefetch=1, **spec))
        args = (prefetch, *args)
    return pl.pallas_call(
        run,
        out_shape=out_shape,
        compiler_params=pltpu.CompilerParams(vmem_limit_bytes=vmem),
        cost_estimate=pl.CostEstimate(flops=flops, bytes_accessed=1, transcendentals=0),
        interpret=INTERPRET,
        name=kernel.__name__,
        **extra,
    )(*args)


def shape(*dims, dtype=F32):
    return jax.ShapeDtypeStruct(dims, dtype)


def whole(array):
    return pl.BlockSpec(array.shape, lambda *_: (0,) * len(array.shape))


def heads_spec(rows, cols):
    return pl.BlockSpec((GROUP, rows, cols), lambda s, place: (s, 0, 0))


def lead_spec(rows, cols):
    return pl.BlockSpec((2, rows, cols), lambda s, place: (s, 0, 0))


def half_of(step, place):
    return (1 - place[3] + step) % 2


def key_head(i, place_ref):
    return 2 * half_of(pl.program_id(0), place_ref) + i


def wide_spec(cols):
    return pl.BlockSpec((TOK, 2 * cols), lambda s, place: (0, half_of(s, place)))


def gate_parts(gate):
    full = jnp.broadcast_to(gate, (16, DK))
    one = full.astype(BF)
    two = (full - one.astype(F32)).astype(BF)
    three = (full - one.astype(F32) - two.astype(F32)).astype(BF)
    place = iota((16, DK), 0)
    parts = jnp.where(place == 0, one.astype(F32), 0.0)
    parts = jnp.where(place == 1, two.astype(F32), parts)
    return jnp.where(place == 2, three.astype(F32), parts).astype(BF)


def gate_of(block):
    return jnp.sum(block[2 * DK :, :].astype(F32), axis=0, keepdims=True)


def unit_keys(key_block):
    raw = key_block.astype(F32)
    rate = lax.rsqrt(lane_sum(raw * raw) + EPS)
    return raw * rate, rate


def prefix_lanes(array):
    size = array.shape[1]
    lane = iota(array.shape, 1)
    step = 1
    while step < size:
        array = array + jnp.where(lane >= step, pltpu.roll(array, step, 1), 0.0)
        step *= 2
    return array


def suffix_lanes(array):
    size = array.shape[1]
    lane = iota(array.shape, 1)
    step = 1
    while step < size:
        array = array + jnp.where(lane < size - step, pltpu.roll(array, size - step, 1), 0.0)
        step *= 2
    return array


def invert_blocks(lowers):
    row, col = iota((HALF, HALF), 0), iota((HALF, HALF), 1)
    apart = row ^ col
    eye = jnp.where(row == col, 1.0, 0.0)
    found = [eye - jnp.where(apart < 2, low, 0.0) for low in lowers]
    size = 2
    while size < HALF:
        mask = (apart >= size) & (apart < 2 * size)
        offs = [jnp.where(mask, low, 0.0).astype(BF) for low in lowers]
        lows = [x.astype(BF) for x in found]
        halfway = [mm(x, off) for x, off in zip(lows, offs)]
        found = [f - mm(m, x) for f, m, x in zip(found, halfway, lows)]
        size *= 2
    return found


def pre_kernel(
    place_ref, k_ref, v_ref, beta_ref, decay_ref, sent_ref, kept_ref, x_ref, wu_ref, c_ref, cols_ref
):
    step = pl.program_id(0)

    @pl.when(step == 0)
    def _():
        c_ref[...] = prefix_lanes(decay_ref[...])

    strict = iota((TOK, TOK), 0) > iota((TOK, TOK), 1)
    sub = iota((8, TOK), 0)
    units, columns, lowers = [], [], []
    for i in range(2):
        j = key_head(i, place_ref)
        unit, _ = unit_keys(k_ref[:, i * DK : (i + 1) * DK])
        low = unit.astype(BF)
        gram = mm_nt(low, low)
        rows = [c_ref[pl.ds(2 * j + a, 1), :] for a in range(2)]
        rates = [beta_ref[pl.ds(2 * j + a, 1), :] for a in range(2)]
        packed = jnp.zeros((8, TOK), F32)
        for spot, line in enumerate((*rows, *rates)):
            packed = jnp.where(sub == spot, line, packed)
        cols = jnp.transpose(jnp.concatenate([packed, jnp.zeros((HALF - 8, TOK), F32)], axis=0))
        cols_ref[i] = cols
        units.append(unit)
        columns.append(cols)
        for a in range(2):
            ratio = jnp.exp(jnp.minimum(cols[:, a : a + 1] - rows[a], 0.0))
            lowers.append(jnp.where(strict, cols[:, 2 + a : 3 + a] * gram * ratio, 0.0))
    found = invert_blocks(
        [low[b * HALF : (b + 1) * HALF, b * HALF : (b + 1) * HALF] for low in lowers for b in (0, 1)]
    )
    for h in range(GROUP):
        i, a = h // 2, h % 2
        unit, cols = units[i], columns[i]
        first, second = found[2 * h].astype(BF), found[2 * h + 1].astype(BF)
        corner = -mm(mm(second, lowers[h][HALF:, :HALF]), first)
        inverse = jnp.concatenate(
            [
                jnp.concatenate([first, jnp.zeros((HALF, HALF), BF)], axis=1),
                jnp.concatenate([corner.astype(BF), second], axis=1),
            ],
            axis=0,
        )
        x_ref[h] = inverse
        c_col, beta_col = cols[:, a : a + 1], cols[:, 2 + a : 3 + a]
        value = v_ref[:, h * DK : (h + 1) * DK].astype(F32)
        right = jnp.concatenate(
            [(beta_col * jnp.exp(c_col) * unit).astype(BF), (beta_col * value).astype(BF)], axis=1
        )
        wu = mm(inverse, right).astype(BF)
        wu_ref[h] = wu
        end = c_col[TOK - 1 : TOK, :]
        moved = mm_tn(wu, jnp.exp(end - c_col) * unit).astype(BF)
        gate = gate_parts(jnp.exp(end))

        @pl.when(step == 0)
        def _():
            sent_ref[h, : 2 * DK, :] = moved
            sent_ref[h, 2 * DK :, :] = gate

        @pl.when(step == 1)
        def _():
            kept_ref[h, : 2 * DK, :] = moved
            kept_ref[h, 2 * DK :, :] = gate


def pre_pass(place, key, value, beta, decay):
    heads = 2 * KEYS
    pay = shape(GROUP, ROWS, DK, dtype=BF)

    return call(
        pre_kernel,
        (
            pay,
            pay,
            shape(heads, TOK, TOK, dtype=BF),
            shape(heads, TOK, 2 * DK, dtype=BF),
            shape(heads, TOK),
            shape(KEYS, TOK, DK),
        ),
        (2,),
        [wide_spec(DK), wide_spec(2 * DK), whole(beta), whole(decay)],
        (
            whole(pay),
            whole(pay),
            heads_spec(TOK, TOK),
            heads_spec(TOK, 2 * DK),
            whole(decay),
            lead_spec(TOK, DK),
        ),
        (key, value, beta, decay),
        SHORT,
        prefetch=place,
    )


def attend_kernel(
    place_ref, q_ref, k_ref, c_ref, cols_ref, x_ref, wu_ref, p_ref, car_ref, out_ref, xz_ref
):
    inclusive = iota((TOK, TOK), 0) >= iota((TOK, TOK), 1)
    for i in range(2):
        j = key_head(i, place_ref)
        unit, _ = unit_keys(k_ref[:, i * DK : (i + 1) * DK])
        query = q_ref[:, i * DK : (i + 1) * DK]
        gram = mm_nt(query, unit)
        cols = cols_ref[i]
        for a in range(2):
            h = 2 * i + a
            c_col = cols[:, a : a + 1]
            ratio = jnp.exp(jnp.minimum(c_col - c_ref[pl.ds(2 * j + a, 1), :], 0.0))
            attend = jnp.where(inclusive, gram * ratio, 0.0).astype(BF)
            p_ref[h] = attend
            both = mm(attend, wu_ref[h])
            car_ref[h] = (jnp.exp(c_col) * query.astype(F32) - both[:, :DK]).astype(BF)
            out_ref[h] = both[:, DK:]
            tail = jnp.exp(c_col[TOK - 1 : TOK, :] - c_col) * unit
            xz_ref[h] = mm_tn(x_ref[h], tail).astype(BF)


def attend_pass(place, query, key, cums, cols, inverse, wu):
    heads = 2 * KEYS
    return call(
        attend_kernel,
        (
            shape(heads, TOK, TOK, dtype=BF),
            shape(heads, TOK, DK, dtype=BF),
            shape(heads, TOK, DK),
            shape(heads, TOK, DK, dtype=BF),
        ),
        (2,),
        [
            wide_spec(DK),
            wide_spec(DK),
            whole(cums),
            lead_spec(TOK, DK),
            heads_spec(TOK, TOK),
            heads_spec(TOK, 2 * DK),
        ],
        (
            heads_spec(TOK, TOK),
            heads_spec(TOK, DK),
            heads_spec(TOK, DK),
            heads_spec(TOK, DK),
        ),
        (query, key, cums, cols, inverse, wu),
        LONG,
        prefetch=place,
    )


def single(kernel, outs, args, place, after=(), cost=SHORT):
    return call(
        kernel,
        outs,
        (1,),
        [whole(a) for a in args],
        tuple(whole(o) for o in outs),
        args,
        cost,
        prefetch=place,
        after=after,
    )


def pair_kernel(place_ref, kept_ref, got_ref, *out_refs):
    z, core = place_ref[2], place_ref[3]
    for k in range(NZ):
        head = (z + k) % NZ
        kept, got = kept_ref[head], got_ref[head]
        early, late = jnp.where(core == 0, kept, got), jnp.where(core == 0, got, kept)
        early_gate, late_gate = gate_of(early), gate_of(late)
        moved = late[:DK].astype(F32)
        out_refs[k][: 2 * DK, :] = (
            late_gate * early[: 2 * DK].astype(F32)
            - mm(early[: 2 * DK], late[:DK])
            + jnp.concatenate([early_gate * moved, late[DK : 2 * DK].astype(F32)], axis=0)
        ).astype(BF)
        out_refs[k][2 * DK :, :] = gate_parts(early_gate * late_gate)


def pair_pass(place, kept, got):
    return single(pair_kernel, (shape(ROWS, DK, dtype=BF),) * NZ, (kept, got), place)


def prefix_kernel(place_ref, *refs):
    parts, (row_ref, nx_ref, bx_ref, gx_ref, tot_ref) = refs[:NZ], refs[NZ:]
    z = place_ref[2]
    for k in range(NZ):
        row_ref[(z - k + NZ) % NZ] = parts[k][...]
    both = jnp.zeros((2 * DK, DK), F32)
    gate = jnp.ones((1, DK), F32)
    for i in range(NZ):
        nx_ref[i] = both[:DK].astype(BF)
        bx_ref[i] = both[DK:]
        gx_ref[i : i + 1, :] = gate
        block = row_ref[i]
        step_gate = gate_of(block)
        moved = block[:DK].astype(F32)
        both = (
            step_gate * both
            - mm(both, block[:DK])
            + jnp.concatenate([gate * moved, block[DK : 2 * DK].astype(F32)], axis=0)
        )
        gate = gate * step_gate
    tot_ref[: 2 * DK, :] = both.astype(BF)
    tot_ref[2 * DK :, :] = gate_parts(gate)


def prefix_pass(place, parts, after):
    outs = (
        shape(NZ, ROWS, DK, dtype=BF),
        shape(NZ, DK, DK, dtype=BF),
        shape(NZ, DK, DK),
        shape(8, DK),
        shape(ROWS, DK, dtype=BF),
    )
    return single(prefix_kernel, outs, parts, place, after)


def suffix_kernel(place_ref, row_ref, ns_ref, gs_ref):
    later = jnp.zeros((DK, DK), F32)
    gate = jnp.ones((1, DK), F32)
    for i in reversed(range(NZ)):
        ns_ref[i] = later.astype(BF)
        gs_ref[i : i + 1, :] = gate
        block = row_ref[i]
        step_gate = gate_of(block)
        moved = block[:DK]
        later = step_gate * later + gate * moved.astype(F32) - mm(moved, later)
        gate = gate * step_gate


def suffix_pass(place, row):
    return single(suffix_kernel, (shape(NZ, DK, DK, dtype=BF), shape(8, DK)), (row,), place, cost=LONG)


def enter_kernel(place_ref, one_ref, two_ref, three_ref, nx_ref, bx_ref, gx_ref, *out_refs):
    here, z = place_ref[1], place_ref[2]
    state = jnp.zeros((DK, DK), F32)
    for back, ref in ((3, three_ref), (2, two_ref), (1, one_ref)):
        block = ref[...]
        moved = gate_of(block) * state - mm(state, block[:DK]) + block[DK : 2 * DK].astype(F32)
        state = jnp.where(here >= back, moved, state)
    for k in range(NZ):
        i = (z + k) % NZ
        out_refs[k][...] = gx_ref[pl.ds(i, 1), :] * state - mm(state, nx_ref[i]) + bx_ref[i]


def enter_pass(place, totals, nx, bx, gx, after):
    outs = (shape(DK, DK),) * NZ
    return single(enter_kernel, outs, (*totals, nx, bx, gx), place, after)


def split_kernel(place_ref, *refs):
    states, (kept_ref, got_ref, own_ref, send_ref) = refs[:NZ], refs[NZ:]
    z, first = place_ref[2], place_ref[3] == 0
    for k in range(NZ):
        head = (z - k + NZ) % NZ
        early = jnp.where(first, kept_ref[head], got_ref[head])
        state = states[k][...]
        moved = (
            gate_of(early) * state - mm(state, early[:DK]) + early[DK : 2 * DK].astype(F32)
        )
        own_ref[head] = jnp.where(first, state, moved)
        send_ref[head] = jnp.where(first, moved, state)


def split_pass(place, states, kept, got, after):
    outs = (shape(GROUP, DK, DK),) * 2
    return single(split_kernel, outs, (*states, kept, got), place, after)


def two_parts(array):
    high = array.astype(BF)
    return high, (array - high.astype(F32)).astype(BF)


def select(theirs_ref, mine_ref, h):
    return jnp.where(pl.program_id(0) == 0, theirs_ref[h], mine_ref[h])


def norm_kernel(
    place_ref, got_ref, own_ref, car_ref, loc_ref, gn_ref,
    norm_ref, s_ref, do_ref, sent_ref, kept_ref,
):
    first = pl.program_id(0) == 0
    for h in range(GROUP):
        state, carried = select(got_ref, own_ref, h).astype(BF), car_ref[h]
        s_ref[h] = state
        head = loc_ref[h] + mm_nt(carried, state)
        scale = lax.rsqrt(lane_sum(head * head) * (1.0 / DK) + EPS)
        normed = head * scale
        norm_ref[:, h * DK : (h + 1) * DK] = normed.astype(BF)
        grad = gn_ref[:, h * DK : (h + 1) * DK]
        inner = lane_sum(grad * normed) * (1.0 / DK)
        back = scale * (grad - normed * inner)
        do_ref[h] = back
        both = mm_tn(jnp.concatenate(two_parts(back), axis=1), carried)
        direct = both[:DV] + both[DV:]

        @pl.when(first)
        def _():
            sent_ref[h] = direct

        @pl.when(jnp.logical_not(first))
        def _():
            kept_ref[h] = direct


def norm_pass(place, got, own, carried, local, grad_normed):
    heads = 2 * KEYS
    half = shape(GROUP, DK, DK)
    return call(
        norm_kernel,
        (
            shape(TOK, heads * DK, dtype=BF),
            shape(heads, DK, DK, dtype=BF),
            shape(heads, TOK, DK),
            half,
            half,
        ),
        (2,),
        [
            whole(got),
            whole(own),
            heads_spec(TOK, DK),
            heads_spec(TOK, DK),
            wide_spec(2 * DK),
        ],
        (wide_spec(2 * DK), heads_spec(DK, DK), heads_spec(TOK, DK), whole(half), whole(half)),
        (got, own, carried, local, grad_normed),
        SHORT,
        prefetch=place,
    )


def middle_kernel(
    place_ref, q_ref, k_ref, v_ref, c_ref, cols_ref, s_ref, do_ref, p_ref, x_ref, wu_ref,
    dq_ref, u_ref, dk_ref, e_ref, y_ref, dcc_ref, dcr_ref,
):
    inclusive = iota((TOK, TOK), 0) >= iota((TOK, TOK), 1)
    lane = iota((TOK, DK), 1)
    sub = iota((8, TOK), 0)
    for i in range(2):
        j = key_head(i, place_ref)
        unit, _ = unit_keys(k_ref[:, i * DK : (i + 1) * DK])
        low = unit.astype(BF)
        query = q_ref[:, i * DK : (i + 1) * DK]
        wide = query.astype(F32)
        cols = cols_ref[i]
        down = jnp.zeros((TOK, DK), F32)
        across = jnp.zeros((8, TOK), F32)
        pair_sum = jnp.zeros((TOK, TOK), F32)
        grad_query = jnp.zeros((TOK, DK), F32)
        for a in range(2):
            h = 2 * i + a
            c_col = cols[:, a : a + 1]
            growth = jnp.exp(c_col)
            state, attend = s_ref[h], p_ref[h]
            back, rest = two_parts(do_ref[h])
            update = (wu_ref[h, :, DK:].astype(F32) - mm_nt(wu_ref[h, :, :DK], state)).astype(BF)
            u_ref[h] = update
            pairs = mm_nt(back, update) + mm_nt(rest, update)
            ratio = jnp.exp(jnp.minimum(c_col - c_ref[pl.ds(2 * j + a, 1), :], 0.0))
            pair_sum += jnp.where(inclusive, pairs * ratio, 0.0)
            shares = pairs * attend.astype(F32)
            reached = growth * (mm(back, state) + mm(rest, state))
            grad_query += reached
            down = jnp.where(lane == a, lane_sum(shares) + lane_sum(reached * wide), down)
            across = jnp.where(sub == a, -jnp.sum(shares, axis=0, keepdims=True), across)
            e_ref[h] = mm_tn(x_ref[h], mm_tn(attend, back))
            value = v_ref[:, h * DK : (h + 1) * DK].astype(F32)
            y_ref[h] = (value - growth * mm_nt(low, state)).astype(BF)
        pair_low = pair_sum.astype(BF)
        dq_ref[:, i * DK : (i + 1) * DK] = grad_query + mm(pair_low, low)
        dk_ref[:, i * DK : (i + 1) * DK] = mm_tn(pair_low, query)
        dcc_ref[i] = down
        dcr_ref[i] = across


def middle_pass(place, query, key, value, cums, cols, state, back, attend, inverse, wu):
    heads = 2 * KEYS
    return call(
        middle_kernel,
        (
            shape(TOK, KEYS * DK),
            shape(heads, TOK, DK, dtype=BF),
            shape(TOK, KEYS * DK),
            shape(heads, TOK, DK),
            shape(heads, TOK, DK, dtype=BF),
            shape(KEYS, TOK, DK),
            shape(KEYS, 8, TOK),
        ),
        (2,),
        [
            wide_spec(DK),
            wide_spec(DK),
            wide_spec(2 * DK),
            whole(cums),
            lead_spec(TOK, DK),
            heads_spec(DK, DK),
            heads_spec(TOK, DK),
            heads_spec(TOK, TOK),
            heads_spec(TOK, TOK),
            heads_spec(TOK, 2 * DK),
        ],
        (
            wide_spec(DK),
            heads_spec(TOK, DK),
            wide_spec(DK),
            heads_spec(TOK, DK),
            heads_spec(TOK, DK),
            lead_spec(TOK, DK),
            lead_spec(8, TOK),
        ),
        (query, key, value, cums, cols, state, back, attend, inverse, wu),
        2 * LONG,
        prefetch=place,
    )


def join_kernel(place_ref, kept_ref, got_ref, dkept_ref, dgot_ref, *out_refs):
    z, first = place_ref[2], place_ref[3] == 0
    for k in range(NZ):
        head = (z + k) % NZ
        early = jnp.where(first, kept_ref[head], got_ref[head])
        before = jnp.where(first, dkept_ref[head], dgot_ref[head])
        after = jnp.where(first, dgot_ref[head], dkept_ref[head])
        out_refs[k][...] = gate_of(early) * after - mm_nt(after, early[:DK]) + before


def join_pass(place, kept, got, dkept, dgot, after):
    outs = (shape(DK, DK),) * NZ
    return single(join_kernel, outs, (kept, got, dkept, dgot), place, after)


def later_kernel(place_ref, *refs):
    parts, (row_ref, d_ref, tot_ref, line_ref) = refs[:NZ], refs[NZ:]
    z = place_ref[2]
    for k in range(NZ):
        line_ref[(z - k + NZ) % NZ] = parts[k][...]
    total = jnp.zeros((DK, DK), F32)
    for i in reversed(range(NZ)):
        d_ref[i] = total
        block = row_ref[i]
        total = gate_of(block) * total - mm_nt(total, block[:DK]) + line_ref[i]
    tot_ref[...] = total


def later_pass(place, parts, row, after):
    outs = (shape(NZ, DK, DK), shape(DK, DK), shape(NZ, DK, DK))
    return single(later_kernel, outs, (*parts, row), place, after)


def leave_kernel(
    place_ref, one_ref, two_ref, three_ref, g1_ref, g2_ref, g3_ref, ns_ref, gs_ref, d_ref, *out_refs
):
    here, z = place_ref[1], place_ref[2]
    total = jnp.zeros((DK, DK), F32)
    for ahead, ref, grad in ((3, one_ref, g3_ref), (2, two_ref, g2_ref), (1, three_ref, g1_ref)):
        block = ref[...]
        moved = gate_of(block) * total - mm_nt(total, block[:DK]) + grad[...]
        total = jnp.where(here + ahead < NY, moved, total)
    for k in range(NZ):
        i = (z + k) % NZ
        out_refs[k][...] = gs_ref[pl.ds(i, 1), :] * total - mm_nt(total, ns_ref[i]) + d_ref[i]


def leave_pass(place, totals, grads, ns, gs, directs, after):
    outs = (shape(DK, DK),) * NZ
    return single(leave_kernel, outs, (*totals, *grads, ns, gs, directs), place, after)


def part_kernel(place_ref, *refs):
    grads, (kept_ref, got_ref, dkept_ref, dgot_ref, own_ref, send_ref) = refs[:NZ], refs[NZ:]
    z, first = place_ref[2], place_ref[3] == 0
    for k in range(NZ):
        head = (z - k + NZ) % NZ
        late = jnp.where(first, got_ref[head], kept_ref[head])
        direct = jnp.where(first, dgot_ref[head], dkept_ref[head])
        grad = grads[k][...]
        moved = gate_of(late) * grad - mm_nt(grad, late[:DK]) + direct
        own_ref[head] = jnp.where(first, moved, grad)
        send_ref[head] = jnp.where(first, grad, moved)


def part_pass(place, grads, kept, got, dkept, dgot, after):
    outs = (shape(GROUP, DK, DK),) * 2
    return single(part_kernel, outs, (*grads, kept, got, dkept, dgot), place, after)


def last_kernel(
    place_ref, k_ref, c_ref, cols_ref, s_ref, ggot_ref, gown_ref, e_ref, y_ref, u_ref, xz_ref,
    dk0_ref, dcc_ref, dcr_ref, dv_ref, dk_ref, db_ref, dd_ref,
):
    strict = iota((TOK, TOK), 0) > iota((TOK, TOK), 1)
    last = iota((TOK, 1), 0) == TOK - 1
    lane = iota((TOK, DK), 1)
    sub = iota((8, TOK), 0)
    for i in range(2):
        j = key_head(i, place_ref)
        unit, rate = unit_keys(k_ref[:, i * DK : (i + 1) * DK])
        low = unit.astype(BF)
        gram = mm_nt(low, low)
        cols = cols_ref[i]
        down = jnp.zeros((TOK, DK), F32)
        pair_sum = jnp.zeros((TOK, TOK), F32)
        grad_key = dk0_ref[:, i * DK : (i + 1) * DK]
        across = []
        for a in range(2):
            h = 2 * i + a
            c_col, beta_col = cols[:, a : a + 1], cols[:, 2 + a : 3 + a]
            growth = jnp.exp(c_col)
            end = c_col[TOK - 1 : TOK, :]
            state, later, update = s_ref[h], select(ggot_ref, gown_ref, h), u_ref[h]
            error = e_ref[h] + mm_nt(xz_ref[h], later)
            ratio = jnp.exp(jnp.minimum(c_col - c_ref[pl.ds(2 * j + a, 1), :], 0.0))
            pairs = jnp.where(strict, -mm_nt(error, update) * ratio, 0.0)
            shares = pairs * gram
            row_share = lane_sum(shares)
            across.append(jnp.sum(beta_col * shares, axis=0, keepdims=True))
            pair_sum += beta_col * pairs
            grad_value = beta_col * error
            dv_ref[:, h * DK : (h + 1) * DK] = grad_value
            reached = growth * mm(grad_value, state)
            tail = jnp.exp(end - c_col) * mm(update, later)
            grad_key += tail - reached
            tail_share = lane_sum(tail * unit)
            gate_share = jnp.exp(end) * jnp.sum(
                lane_sum(state.astype(F32) * later.astype(F32)), axis=0, keepdims=True
            )
            total = jnp.sum(tail_share, axis=0, keepdims=True) + gate_share
            grad_cum = beta_col * row_share - lane_sum(reached * unit) - tail_share
            grad_cum += jnp.where(last, total, 0.0)
            grad_beta = row_share + lane_sum(error * y_ref[h].astype(F32))
            down = jnp.where(lane == a, grad_cum, jnp.where(lane == 2 + a, grad_beta, down))
        pair_low = pair_sum.astype(BF)
        grad_key += mm(pair_low, low) + mm_tn(pair_low, low)
        dk_ref[:, i * DK : (i + 1) * DK] = rate * (grad_key - unit * lane_sum(unit * grad_key))
        turned = jnp.transpose(down + jnp.where(lane < 2, dcc_ref[i], 0.0))[:8]
        cum = turned + dcr_ref[i]
        for a in range(2):
            cum = jnp.where(sub == a, cum - across[a], cum)
        decayed = suffix_lanes(cum)
        for a in range(2):
            dd_ref[pl.ds(2 * j + a, 1), :] = decayed[a : a + 1]
            db_ref[pl.ds(2 * j + a, 1), :] = turned[2 + a : 3 + a]


def last_pass(place, key, cums, cols, state, got, own, error, y, update, xz, dk0, dcc, dcr, after):
    heads = 2 * KEYS
    return call(
        last_kernel,
        (
            shape(TOK, heads * DK),
            shape(TOK, KEYS * DK),
            shape(heads, TOK),
            shape(heads, TOK),
        ),
        (2,),
        [
            wide_spec(DK),
            whole(cums),
            lead_spec(TOK, DK),
            heads_spec(DK, DK),
            whole(got),
            whole(own),
            heads_spec(TOK, DK),
            heads_spec(TOK, DK),
            heads_spec(TOK, DK),
            heads_spec(TOK, DK),
            wide_spec(DK),
            lead_spec(TOK, DK),
            lead_spec(8, TOK),
        ],
        (wide_spec(2 * DK), wide_spec(DK), whole(cums), whole(cums)),
        (key, cums, cols, state, got, own, error, y, update, xz, dk0, dcc, dcr),
        2 * LONG,
        prefetch=place,
        after=after,
    )


def back_kernel(place_ref, cot_ref, w_ref, out_ref):
    part = mm(cot_ref[0], w_ref[...])

    @pl.when(pl.program_id(0) == 0)
    def _():
        out_ref[...] = part

    @pl.when(pl.program_id(0) > 0)
    def _():
        out_ref[...] += part


def back_pass(place, cot, weight, after):
    depth, wide = cot.shape[2], weight.shape[1]
    out = shape(TOK, wide)
    return call(
        back_kernel,
        (out,),
        (NH,),
        [
            pl.BlockSpec((1, TOK, depth), lambda k, place: (k, 0, 0)),
            pl.BlockSpec((depth, wide), lambda k, place: ((place[0] + k) % NH, 0)),
        ],
        (whole(out),),
        (cot, weight),
        LONG,
        prefetch=place,
        after=after,
    )[0]


def mix_kernel(place_ref, norm_ref, w_ref, out_ref):
    out_ref[0] = mm_nt(norm_ref[...], w_ref[...]).astype(BF)


def mix_pass(place, normed, weight, after):
    depth = weight.shape[0] // NH
    out = shape(NH, TOK, depth, dtype=BF)
    return call(
        mix_kernel,
        (out,),
        (NH,),
        [
            whole(normed),
            pl.BlockSpec((depth, weight.shape[1]), lambda k, place: ((place[0] + k) % NH, 0)),
        ],
        (pl.BlockSpec((1, TOK, depth), lambda k, place: (k, 0, 0)),),
        (normed, weight),
        LONG,
        prefetch=place,
        after=after,
    )[0]


def outer_kernel(place_ref, cot_ref, norm_ref, mine_ref, other_ref):
    here, core = place_ref[2], place_ref[3]
    rows = mine_ref.shape[2]
    for k in range(NZ):
        start = pl.multiple_of(((here + k) % NZ) * 2 * rows, 2 * rows)
        part = mm_tn(cot_ref[0, :, pl.ds(start, 2 * rows)], norm_ref[...]).astype(BF)
        first = core == 0
        mine_ref[0, k] = jnp.where(first, part[:rows], part[rows:])
        other_ref[0, k] = jnp.where(first, part[rows:], part[:rows])


def outer_pass(place, cot, normed, after):
    rows = cot.shape[2] // (NZ * NC)
    out = shape(NY, NZ, rows, normed.shape[1], dtype=BF)
    spec = pl.BlockSpec((1, NZ, rows, normed.shape[1]), lambda k, place: (k, 0, 0, 0))
    return call(
        outer_kernel,
        (out, out),
        (NY,),
        [
            pl.BlockSpec(
                (1, TOK, cot.shape[2]), lambda k, place: ((place[1] + k - place[0] + NH) % NH, 0, 0)
            ),
            whole(normed),
        ],
        (spec, spec),
        (cot, normed),
        LONG,
        prefetch=place,
        after=after,
    )


def blend_kernel(place_ref, mine_ref, other_ref, *out_refs):
    for y in range(NY):
        for z in range(NZ):
            total = mine_ref[y, z].astype(F32) + other_ref[y, z].astype(F32)
            out_refs[z][y] = total.astype(BF)


def blend_pass(place, mine, other, after):
    outs = (shape(NY, *mine.shape[2:], dtype=BF),) * NZ
    return single(blend_kernel, outs, (mine, other), place, after, LONG)


def sum_kernel(place_ref, *refs):
    for y in range(NY):
        refs[NZ + y][...] = sum(refs[z][y].astype(F32) for z in range(NZ)).astype(BF)


def sum_pass(place, parts, after):
    outs = (shape(*parts[0].shape[1:], dtype=BF),) * NY
    return single(sum_kernel, outs, parts, place, after)


def shift(array, axis, count, step):
    return lax.ppermute(array, axis, [(i, (i + step) % count) for i in range(count)])


def spread(parts, axis, count, sign=1):
    return [parts[0]] + [shift(parts[k], axis, count, sign * k) for k in range(1, count)]


def scatter_stage(parts, axis, count):
    return sum(part.astype(F32) for part in spread(parts, axis, count))


def swap(array):
    return lax.ppermute(array, "c", [(0, 1), (1, 0)])


def body(query, key, value, beta, decay, wo_start, wo_end, curve_index, cotangent):
    place = jnp.stack([lax.axis_index(a) for a in ("head", "y", "z", "c")]).astype(jnp.int32)
    position = curve_index[0].astype(F32) / (CURVE_POINTS - 1)
    weight_local = (
        (1.0 - position) * wo_start.astype(F32) + position * wo_end.astype(F32)
    ).astype(BF)
    weight = lax.all_gather(weight_local, RING, axis=0, tiled=True)
    cot = jnp.stack([cotangent] + [shift(cotangent, "head", NH, -k) for k in range(1, NH)])

    sent, kept, inverse, wu, cums, cols = pre_pass(place, key, value, beta, decay)
    got = swap(sent)
    parts = spread(pair_pass(place, kept, got), "z", NZ)
    attend, carried, local, xz = attend_pass(place, query, key, cums, cols, inverse, wu)
    row, nx, bx, gx, total = prefix_pass(place, parts, (xz,))
    totals = [shift(total, "y", NY, k) for k in range(1, NY)]
    ns, gs = suffix_pass(place, row)
    states = spread(enter_pass(place, totals, nx, bx, gx, (ns,)), "z", NZ)
    grad_normed = back_pass(place, cot, weight, (ns,))
    own, send = split_pass(place, states, kept, got, (grad_normed,))
    normed, state, back, dsent, dkept = norm_pass(
        place, swap(send), own, carried, local, grad_normed
    )

    dgot = swap(dsent)
    grad_parts = spread(join_pass(place, kept, got, dkept, dgot, ()), "z", NZ)
    mine, other = outer_pass(place, cot, normed, (dgot,))
    theirs = swap(other)
    suffixes, grad_total, _ = later_pass(place, grad_parts, row, ())
    grads = [shift(grad_total, "y", NY, -k) for k in range(1, NY)]
    grad_query, update, dk0, error, y, dcc, dcr = middle_pass(
        place, query, key, value, cums, cols, state, back, attend, inverse, wu
    )
    laters = spread(leave_pass(place, totals, grads, ns, gs, suffixes, (dk0,)), "z", NZ)
    sums = spread(blend_pass(place, mine, theirs, (grad_total,)), "z", NZ)
    gown, gsend = part_pass(place, laters, kept, got, dkept, dgot, (sums[0],))
    ggot = swap(gsend)

    grad_value, grad_key, grad_beta, grad_decay = last_pass(
        place, key, cums, cols, state, ggot, gown, error, y, update, xz, dk0, dcc, dcr, ()
    )
    mixes = mix_pass(place, normed, weight, (grad_beta,))
    mixed = scatter_stage([mixes[k] for k in range(NH)], "head", NH).astype(BF)
    sums = sum_pass(place, sums, (grad_beta,))
    grad_weight = scatter_stage(sums, "y", NY)
    return (
        mixed,
        grad_query,
        grad_key,
        grad_value,
        grad_beta,
        grad_decay,
        (1.0 - position) * grad_weight,
        position * grad_weight,
    )


def solution(mesh):
    fine = Mesh(mesh.devices.reshape(NY, NZ, NC, NH), ("y", "z", "c", "head"))
    rows, flipped = P(RING, "head"), P("head", RING)
    return jax.shard_map(
        body,
        mesh=fine,
        in_specs=(rows, rows, rows, flipped, flipped, rows, rows, P(), rows),
        out_specs=(rows, rows, rows, rows, flipped, flipped, rows, rows),
        check_vma=False,
    )
```

```python
import jax
import jax.numpy as jnp
from jax import lax
from jax.experimental import pallas as pl
from jax.experimental.pallas import tpu as pltpu
from jax.sharding import Mesh, PartitionSpec as P

DK = 128
DV = 128
CURVE_POINTS = 257
EPS = 1e-06
NY, NZ, NC, NH = 4, 4, 2, 4
TOK = 256
HALF = 128
KEYS = 4
ROWS = 272
GROUP = 4
VMEM = 14 * 2**20
SHORT = 10**6
LONG = 5 * 10**9
BF = jnp.bfloat16
F32 = jnp.float32
RING = ("y", "z", "c")
INTERPRET = False


def dot(left, right, dims):
    return lax.dot_general(
        left.astype(BF), right.astype(BF), (dims, ((), ())), preferred_element_type=F32
    )


def mm(left, right):
    return dot(left, right, ((1,), (0,)))


def mm_nt(left, right):
    return dot(left, right, ((1,), (1,)))


def mm_tn(left, right):
    return dot(left, right, ((0,), (0,)))


def iota(shape, dim):
    return lax.broadcasted_iota(jnp.int32, shape, dim)


def lane_sum(array):
    return jnp.sum(array, axis=1, keepdims=True)


def call(
    kernel, out_shape, grid, in_specs, out_specs, args, flops, prefetch=None, after=(), vmem=VMEM
):
    count = len(args) + (prefetch is not None)

    def run(*refs):
        kernel(*refs[:count], *refs[count + len(after) :])

    in_specs = [*in_specs, *(pl.BlockSpec(memory_space=pl.ANY) for _ in after)]
    args = (*args, *after)
    spec = dict(grid=grid, in_specs=in_specs, out_specs=out_specs)
    extra = {}
    if prefetch is None:
        extra = spec
    else:
        extra = dict(grid_spec=pltpu.PrefetchScalarGridSpec(num_scalar_prefetch=1, **spec))
        args = (prefetch, *args)
    return pl.pallas_call(
        run,
        out_shape=out_shape,
        compiler_params=pltpu.CompilerParams(vmem_limit_bytes=vmem),
        cost_estimate=pl.CostEstimate(flops=flops, bytes_accessed=1, transcendentals=0),
        interpret=INTERPRET,
        name=kernel.__name__,
        **extra,
    )(*args)


def shape(*dims, dtype=F32):
    return jax.ShapeDtypeStruct(dims, dtype)


def whole(array):
    return pl.BlockSpec(array.shape, lambda *_: (0,) * len(array.shape))


def heads_spec(rows, cols):
    return pl.BlockSpec((GROUP, rows, cols), lambda s, place: (s, 0, 0))


def lead_spec(rows, cols):
    return pl.BlockSpec((2, rows, cols), lambda s, place: (s, 0, 0))


def half_of(step, place):
    return (1 - place[3] + step) % 2


def key_head(i, place_ref):
    return 2 * half_of(pl.program_id(0), place_ref) + i


def wide_spec(cols):
    return pl.BlockSpec((TOK, 2 * cols), lambda s, place: (0, half_of(s, place)))


def gate_parts(gate):
    full = jnp.broadcast_to(gate, (16, DK))
    one = full.astype(BF)
    two = (full - one.astype(F32)).astype(BF)
    three = (full - one.astype(F32) - two.astype(F32)).astype(BF)
    place = iota((16, DK), 0)
    parts = jnp.where(place == 0, one.astype(F32), 0.0)
    parts = jnp.where(place == 1, two.astype(F32), parts)
    return jnp.where(place == 2, three.astype(F32), parts).astype(BF)


def gate_of(block):
    return jnp.sum(block[2 * DK :, :].astype(F32), axis=0, keepdims=True)


def unit_keys(key_block):
    raw = key_block.astype(F32)
    rate = lax.rsqrt(lane_sum(raw * raw) + EPS)
    return raw * rate, rate


def prefix_lanes(array):
    size = array.shape[1]
    lane = iota(array.shape, 1)
    step = 1
    while step < size:
        array = array + jnp.where(lane >= step, pltpu.roll(array, step, 1), 0.0)
        step *= 2
    return array


def suffix_lanes(array):
    size = array.shape[1]
    lane = iota(array.shape, 1)
    step = 1
    while step < size:
        array = array + jnp.where(lane < size - step, pltpu.roll(array, size - step, 1), 0.0)
        step *= 2
    return array


def invert_blocks(lowers):
    row, col = iota((HALF, HALF), 0), iota((HALF, HALF), 1)
    apart = row ^ col
    eye = jnp.where(row == col, 1.0, 0.0)
    found = [eye - jnp.where(apart < 2, low, 0.0) for low in lowers]
    size = 2
    while size < HALF:
        mask = (apart >= size) & (apart < 2 * size)
        offs = [jnp.where(mask, low, 0.0).astype(BF) for low in lowers]
        lows = [x.astype(BF) for x in found]
        halfway = [mm(x, off) for x, off in zip(lows, offs)]
        found = [f - mm(m, x) for f, m, x in zip(found, halfway, lows)]
        size *= 2
    return found


def pre_kernel(
    place_ref, k_ref, v_ref, beta_ref, decay_ref, sent_ref, kept_ref, x_ref, wu_ref, c_ref, cols_ref
):
    step = pl.program_id(0)

    @pl.when(step == 0)
    def _():
        c_ref[...] = prefix_lanes(decay_ref[...])

    strict = iota((TOK, TOK), 0) > iota((TOK, TOK), 1)
    sub = iota((8, TOK), 0)
    units, columns, lowers = [], [], []
    for i in range(2):
        j = key_head(i, place_ref)
        unit, _ = unit_keys(k_ref[:, i * DK : (i + 1) * DK])
        low = unit.astype(BF)
        gram = mm_nt(low, low)
        rows = [c_ref[pl.ds(2 * j + a, 1), :] for a in range(2)]
        rates = [beta_ref[pl.ds(2 * j + a, 1), :] for a in range(2)]
        packed = jnp.zeros((8, TOK), F32)
        for spot, line in enumerate((*rows, *rates)):
            packed = jnp.where(sub == spot, line, packed)
        cols = jnp.transpose(jnp.concatenate([packed, jnp.zeros((HALF - 8, TOK), F32)], axis=0))
        cols_ref[i] = cols
        units.append(unit)
        columns.append(cols)
        for a in range(2):
            ratio = jnp.exp(jnp.minimum(cols[:, a : a + 1] - rows[a], 0.0))
            lowers.append(jnp.where(strict, cols[:, 2 + a : 3 + a] * gram * ratio, 0.0))
    found = invert_blocks(
        [low[b * HALF : (b + 1) * HALF, b * HALF : (b + 1) * HALF] for low in lowers for b in (0, 1)]
    )
    for h in range(GROUP):
        i, a = h // 2, h % 2
        unit, cols = units[i], columns[i]
        first, second = found[2 * h].astype(BF), found[2 * h + 1].astype(BF)
        corner = -mm(mm(second, lowers[h][HALF:, :HALF]), first)
        inverse = jnp.concatenate(
            [
                jnp.concatenate([first, jnp.zeros((HALF, HALF), BF)], axis=1),
                jnp.concatenate([corner.astype(BF), second], axis=1),
            ],
            axis=0,
        )
        x_ref[h] = inverse
        c_col, beta_col = cols[:, a : a + 1], cols[:, 2 + a : 3 + a]
        value = v_ref[:, h * DK : (h + 1) * DK].astype(F32)
        right = jnp.concatenate(
            [(beta_col * jnp.exp(c_col) * unit).astype(BF), (beta_col * value).astype(BF)], axis=1
        )
        wu = mm(inverse, right).astype(BF)
        wu_ref[h] = wu
        end = c_col[TOK - 1 : TOK, :]
        moved = mm_tn(wu, jnp.exp(end - c_col) * unit).astype(BF)
        gate = gate_parts(jnp.exp(end))

        @pl.when(step == 0)
        def _():
            sent_ref[h, : 2 * DK, :] = moved
            sent_ref[h, 2 * DK :, :] = gate

        @pl.when(step == 1)
        def _():
            kept_ref[h, : 2 * DK, :] = moved
            kept_ref[h, 2 * DK :, :] = gate


def pre_pass(place, key, value, beta, decay):
    heads = 2 * KEYS
    pay = shape(GROUP, ROWS, DK, dtype=BF)

    return call(
        pre_kernel,
        (
            pay,
            pay,
            shape(heads, TOK, TOK, dtype=BF),
            shape(heads, TOK, 2 * DK, dtype=BF),
            shape(heads, TOK),
            shape(KEYS, TOK, DK),
        ),
        (2,),
        [wide_spec(DK), wide_spec(2 * DK), whole(beta), whole(decay)],
        (
            whole(pay),
            whole(pay),
            heads_spec(TOK, TOK),
            heads_spec(TOK, 2 * DK),
            whole(decay),
            lead_spec(TOK, DK),
        ),
        (key, value, beta, decay),
        SHORT,
        prefetch=place,
    )


def attend_kernel(
    place_ref, q_ref, k_ref, c_ref, cols_ref, x_ref, wu_ref, p_ref, car_ref, out_ref, xz_ref
):
    inclusive = iota((TOK, TOK), 0) >= iota((TOK, TOK), 1)
    for i in range(2):
        j = key_head(i, place_ref)
        unit, _ = unit_keys(k_ref[:, i * DK : (i + 1) * DK])
        query = q_ref[:, i * DK : (i + 1) * DK]
        gram = mm_nt(query, unit)
        cols = cols_ref[i]
        for a in range(2):
            h = 2 * i + a
            c_col = cols[:, a : a + 1]
            ratio = jnp.exp(jnp.minimum(c_col - c_ref[pl.ds(2 * j + a, 1), :], 0.0))
            attend = jnp.where(inclusive, gram * ratio, 0.0).astype(BF)
            p_ref[h] = attend
            both = mm(attend, wu_ref[h])
            car_ref[h] = (jnp.exp(c_col) * query.astype(F32) - both[:, :DK]).astype(BF)
            out_ref[h] = both[:, DK:]
            tail = jnp.exp(c_col[TOK - 1 : TOK, :] - c_col) * unit
            xz_ref[h] = mm_tn(x_ref[h], tail).astype(BF)


def attend_pass(place, query, key, cums, cols, inverse, wu, after):
    heads = 2 * KEYS
    return call(
        attend_kernel,
        (
            shape(heads, TOK, TOK, dtype=BF),
            shape(heads, TOK, DK, dtype=BF),
            shape(heads, TOK, DK),
            shape(heads, TOK, DK, dtype=BF),
        ),
        (2,),
        [
            wide_spec(DK),
            wide_spec(DK),
            whole(cums),
            lead_spec(TOK, DK),
            heads_spec(TOK, TOK),
            heads_spec(TOK, 2 * DK),
        ],
        (
            heads_spec(TOK, TOK),
            heads_spec(TOK, DK),
            heads_spec(TOK, DK),
            heads_spec(TOK, DK),
        ),
        (query, key, cums, cols, inverse, wu),
        LONG,
        prefetch=place,
        after=after,
    )


def single(kernel, outs, args, place, after=(), cost=SHORT):
    return call(
        kernel,
        outs,
        (1,),
        [whole(a) for a in args],
        tuple(whole(o) for o in outs),
        args,
        cost,
        prefetch=place,
        after=after,
    )


def pair_kernel(place_ref, kept_ref, got_ref, *out_refs):
    z, core = place_ref[2], place_ref[3]
    for k in range(NZ):
        head = (z + k) % NZ
        kept, got = kept_ref[head], got_ref[head]
        early, late = jnp.where(core == 0, kept, got), jnp.where(core == 0, got, kept)
        early_gate, late_gate = gate_of(early), gate_of(late)
        moved = late[:DK].astype(F32)
        out_refs[k][: 2 * DK, :] = (
            late_gate * early[: 2 * DK].astype(F32)
            - mm(early[: 2 * DK], late[:DK])
            + jnp.concatenate([early_gate * moved, late[DK : 2 * DK].astype(F32)], axis=0)
        ).astype(BF)
        out_refs[k][2 * DK :, :] = gate_parts(early_gate * late_gate)


def pair_pass(place, kept, got):
    return single(pair_kernel, (shape(ROWS, DK, dtype=BF),) * NZ, (kept, got), place)


def prefix_kernel(place_ref, *refs):
    parts, (row_ref, nx_ref, bx_ref, gx_ref, tot_ref) = refs[:NZ], refs[NZ:]
    z = place_ref[2]
    for k in range(NZ):
        row_ref[(z - k + NZ) % NZ] = parts[k][...]
    both = jnp.zeros((2 * DK, DK), F32)
    gate = jnp.ones((1, DK), F32)
    for i in range(NZ):
        nx_ref[i] = both[:DK].astype(BF)
        bx_ref[i] = both[DK:]
        gx_ref[i : i + 1, :] = gate
        block = row_ref[i]
        step_gate = gate_of(block)
        moved = block[:DK].astype(F32)
        both = (
            step_gate * both
            - mm(both, block[:DK])
            + jnp.concatenate([gate * moved, block[DK : 2 * DK].astype(F32)], axis=0)
        )
        gate = gate * step_gate
    tot_ref[: 2 * DK, :] = both.astype(BF)
    tot_ref[2 * DK :, :] = gate_parts(gate)


def prefix_pass(place, parts, after):
    outs = (
        shape(NZ, ROWS, DK, dtype=BF),
        shape(NZ, DK, DK, dtype=BF),
        shape(NZ, DK, DK),
        shape(8, DK),
        shape(ROWS, DK, dtype=BF),
    )
    return single(prefix_kernel, outs, parts, place, after)


def suffix_kernel(place_ref, row_ref, ns_ref, gs_ref):
    later = jnp.zeros((DK, DK), F32)
    gate = jnp.ones((1, DK), F32)
    for i in reversed(range(NZ)):
        ns_ref[i] = later.astype(BF)
        gs_ref[i : i + 1, :] = gate
        block = row_ref[i]
        step_gate = gate_of(block)
        moved = block[:DK]
        later = step_gate * later + gate * moved.astype(F32) - mm(moved, later)
        gate = gate * step_gate


def suffix_pass(place, row):
    return single(suffix_kernel, (shape(NZ, DK, DK, dtype=BF), shape(8, DK)), (row,), place, cost=LONG)


def enter_kernel(place_ref, one_ref, two_ref, three_ref, nx_ref, bx_ref, gx_ref, *out_refs):
    here, z = place_ref[1], place_ref[2]
    state = jnp.zeros((DK, DK), F32)
    for back, ref in ((3, three_ref), (2, two_ref), (1, one_ref)):
        block = ref[...]
        moved = gate_of(block) * state - mm(state, block[:DK]) + block[DK : 2 * DK].astype(F32)
        state = jnp.where(here >= back, moved, state)
    for k in range(NZ):
        i = (z + k) % NZ
        out_refs[k][...] = gx_ref[pl.ds(i, 1), :] * state - mm(state, nx_ref[i]) + bx_ref[i]


def enter_pass(place, totals, nx, bx, gx, after):
    outs = (shape(DK, DK),) * NZ
    return single(enter_kernel, outs, (*totals, nx, bx, gx), place, after)


def split_kernel(place_ref, *refs):
    states, (kept_ref, got_ref, own_ref, send_ref) = refs[:NZ], refs[NZ:]
    z, first = place_ref[2], place_ref[3] == 0
    for k in range(NZ):
        head = (z - k + NZ) % NZ
        early = jnp.where(first, kept_ref[head], got_ref[head])
        state = states[k][...]
        moved = (
            gate_of(early) * state - mm(state, early[:DK]) + early[DK : 2 * DK].astype(F32)
        )
        own_ref[head] = jnp.where(first, state, moved)
        send_ref[head] = jnp.where(first, moved, state)


def split_pass(place, states, kept, got, after):
    outs = (shape(GROUP, DK, DK),) * 2
    return single(split_kernel, outs, (*states, kept, got), place, after)


def two_parts(array):
    high = array.astype(BF)
    return high, (array - high.astype(F32)).astype(BF)


def select(theirs_ref, mine_ref, h):
    return jnp.where(pl.program_id(0) == 0, theirs_ref[h], mine_ref[h])


def norm_kernel(
    place_ref, got_ref, own_ref, car_ref, loc_ref, gn_ref,
    norm_ref, s_ref, do_ref, sent_ref, kept_ref,
):
    first = pl.program_id(0) == 0
    for h in range(GROUP):
        state, carried = select(got_ref, own_ref, h).astype(BF), car_ref[h]
        s_ref[h] = state
        head = loc_ref[h] + mm_nt(carried, state)
        scale = lax.rsqrt(lane_sum(head * head) * (1.0 / DK) + EPS)
        normed = head * scale
        norm_ref[:, h * DK : (h + 1) * DK] = normed.astype(BF)
        grad = gn_ref[:, h * DK : (h + 1) * DK]
        inner = lane_sum(grad * normed) * (1.0 / DK)
        back = scale * (grad - normed * inner)
        do_ref[h] = back
        both = mm_tn(jnp.concatenate(two_parts(back), axis=1), carried)
        direct = both[:DV] + both[DV:]

        @pl.when(first)
        def _():
            sent_ref[h] = direct

        @pl.when(jnp.logical_not(first))
        def _():
            kept_ref[h] = direct


def norm_pass(place, got, own, carried, local, grad_normed):
    heads = 2 * KEYS
    half = shape(GROUP, DK, DK)
    return call(
        norm_kernel,
        (
            shape(TOK, heads * DK, dtype=BF),
            shape(heads, DK, DK, dtype=BF),
            shape(heads, TOK, DK),
            half,
            half,
        ),
        (2,),
        [
            whole(got),
            whole(own),
            heads_spec(TOK, DK),
            heads_spec(TOK, DK),
            wide_spec(2 * DK),
        ],
        (wide_spec(2 * DK), heads_spec(DK, DK), heads_spec(TOK, DK), whole(half), whole(half)),
        (got, own, carried, local, grad_normed),
        SHORT,
        prefetch=place,
    )


def middle_kernel(
    place_ref, q_ref, k_ref, v_ref, c_ref, cols_ref, s_ref, do_ref, p_ref, x_ref, wu_ref,
    dq_ref, u_ref, dk_ref, e_ref, y_ref, dcc_ref, dcr_ref,
):
    inclusive = iota((TOK, TOK), 0) >= iota((TOK, TOK), 1)
    lane = iota((TOK, DK), 1)
    sub = iota((8, TOK), 0)
    for i in range(2):
        j = key_head(i, place_ref)
        unit, _ = unit_keys(k_ref[:, i * DK : (i + 1) * DK])
        low = unit.astype(BF)
        query = q_ref[:, i * DK : (i + 1) * DK]
        wide = query.astype(F32)
        cols = cols_ref[i]
        down = jnp.zeros((TOK, DK), F32)
        across = jnp.zeros((8, TOK), F32)
        pair_sum = jnp.zeros((TOK, TOK), F32)
        grad_query = jnp.zeros((TOK, DK), F32)
        for a in range(2):
            h = 2 * i + a
            c_col = cols[:, a : a + 1]
            growth = jnp.exp(c_col)
            state, attend = s_ref[h], p_ref[h]
            back, rest = two_parts(do_ref[h])
            update = (wu_ref[h, :, DK:].astype(F32) - mm_nt(wu_ref[h, :, :DK], state)).astype(BF)
            u_ref[h] = update
            pairs = mm_nt(back, update) + mm_nt(rest, update)
            ratio = jnp.exp(jnp.minimum(c_col - c_ref[pl.ds(2 * j + a, 1), :], 0.0))
            pair_sum += jnp.where(inclusive, pairs * ratio, 0.0)
            shares = pairs * attend.astype(F32)
            reached = growth * (mm(back, state) + mm(rest, state))
            grad_query += reached
            down = jnp.where(lane == a, lane_sum(shares) + lane_sum(reached * wide), down)
            across = jnp.where(sub == a, -jnp.sum(shares, axis=0, keepdims=True), across)
            e_ref[h] = mm_tn(x_ref[h], mm_tn(attend, back))
            value = v_ref[:, h * DK : (h + 1) * DK].astype(F32)
            y_ref[h] = (value - growth * mm_nt(low, state)).astype(BF)
        pair_low = pair_sum.astype(BF)
        dq_ref[:, i * DK : (i + 1) * DK] = grad_query + mm(pair_low, low)
        dk_ref[:, i * DK : (i + 1) * DK] = mm_tn(pair_low, query)
        dcc_ref[i] = down
        dcr_ref[i] = across


def middle_pass(place, query, key, value, cums, cols, state, back, attend, inverse, wu):
    heads = 2 * KEYS
    return call(
        middle_kernel,
        (
            shape(TOK, KEYS * DK),
            shape(heads, TOK, DK, dtype=BF),
            shape(TOK, KEYS * DK),
            shape(heads, TOK, DK),
            shape(heads, TOK, DK, dtype=BF),
            shape(KEYS, TOK, DK),
            shape(KEYS, 8, TOK),
        ),
        (2,),
        [
            wide_spec(DK),
            wide_spec(DK),
            wide_spec(2 * DK),
            whole(cums),
            lead_spec(TOK, DK),
            heads_spec(DK, DK),
            heads_spec(TOK, DK),
            heads_spec(TOK, TOK),
            heads_spec(TOK, TOK),
            heads_spec(TOK, 2 * DK),
        ],
        (
            wide_spec(DK),
            heads_spec(TOK, DK),
            wide_spec(DK),
            heads_spec(TOK, DK),
            heads_spec(TOK, DK),
            lead_spec(TOK, DK),
            lead_spec(8, TOK),
        ),
        (query, key, value, cums, cols, state, back, attend, inverse, wu),
        2 * LONG,
        prefetch=place,
    )


def join_kernel(place_ref, kept_ref, got_ref, dkept_ref, dgot_ref, *out_refs):
    z, first = place_ref[2], place_ref[3] == 0
    for k in range(NZ):
        head = (z + k) % NZ
        early = jnp.where(first, kept_ref[head], got_ref[head])
        before = jnp.where(first, dkept_ref[head], dgot_ref[head])
        after = jnp.where(first, dgot_ref[head], dkept_ref[head])
        out_refs[k][...] = gate_of(early) * after - mm_nt(after, early[:DK]) + before


def join_pass(place, kept, got, dkept, dgot, after):
    outs = (shape(DK, DK),) * NZ
    return single(join_kernel, outs, (kept, got, dkept, dgot), place, after)


def later_kernel(place_ref, *refs):
    parts, (row_ref, d_ref, tot_ref, line_ref) = refs[:NZ], refs[NZ:]
    z = place_ref[2]
    for k in range(NZ):
        line_ref[(z - k + NZ) % NZ] = parts[k][...]
    total = jnp.zeros((DK, DK), F32)
    for i in reversed(range(NZ)):
        d_ref[i] = total
        block = row_ref[i]
        total = gate_of(block) * total - mm_nt(total, block[:DK]) + line_ref[i]
    tot_ref[...] = total


def later_pass(place, parts, row, after):
    outs = (shape(NZ, DK, DK), shape(DK, DK), shape(NZ, DK, DK))
    return single(later_kernel, outs, (*parts, row), place, after)


def leave_kernel(
    place_ref, one_ref, two_ref, three_ref, g1_ref, g2_ref, g3_ref, ns_ref, gs_ref, d_ref, *out_refs
):
    here, z = place_ref[1], place_ref[2]
    total = jnp.zeros((DK, DK), F32)
    for ahead, ref, grad in ((3, one_ref, g3_ref), (2, two_ref, g2_ref), (1, three_ref, g1_ref)):
        block = ref[...]
        moved = gate_of(block) * total - mm_nt(total, block[:DK]) + grad[...]
        total = jnp.where(here + ahead < NY, moved, total)
    for k in range(NZ):
        i = (z + k) % NZ
        out_refs[k][...] = gs_ref[pl.ds(i, 1), :] * total - mm_nt(total, ns_ref[i]) + d_ref[i]


def leave_pass(place, totals, grads, ns, gs, directs, after):
    outs = (shape(DK, DK),) * NZ
    return single(leave_kernel, outs, (*totals, *grads, ns, gs, directs), place, after)


def part_kernel(place_ref, *refs):
    grads, (kept_ref, got_ref, dkept_ref, dgot_ref, own_ref, send_ref) = refs[:NZ], refs[NZ:]
    z, first = place_ref[2], place_ref[3] == 0
    for k in range(NZ):
        head = (z - k + NZ) % NZ
        late = jnp.where(first, got_ref[head], kept_ref[head])
        direct = jnp.where(first, dgot_ref[head], dkept_ref[head])
        grad = grads[k][...]
        moved = gate_of(late) * grad - mm_nt(grad, late[:DK]) + direct
        own_ref[head] = jnp.where(first, moved, grad)
        send_ref[head] = jnp.where(first, grad, moved)


def part_pass(place, grads, kept, got, dkept, dgot, after):
    outs = (shape(GROUP, DK, DK),) * 2
    return single(part_kernel, outs, (*grads, kept, got, dkept, dgot), place, after)


def last_kernel(
    place_ref, k_ref, c_ref, cols_ref, s_ref, ggot_ref, gown_ref, e_ref, y_ref, u_ref, xz_ref,
    dk0_ref, dcc_ref, dcr_ref, dv_ref, dk_ref, db_ref, dd_ref,
):
    strict = iota((TOK, TOK), 0) > iota((TOK, TOK), 1)
    last = iota((TOK, 1), 0) == TOK - 1
    lane = iota((TOK, DK), 1)
    sub = iota((8, TOK), 0)
    for i in range(2):
        j = key_head(i, place_ref)
        unit, rate = unit_keys(k_ref[:, i * DK : (i + 1) * DK])
        low = unit.astype(BF)
        gram = mm_nt(low, low)
        cols = cols_ref[i]
        down = jnp.zeros((TOK, DK), F32)
        pair_sum = jnp.zeros((TOK, TOK), F32)
        grad_key = dk0_ref[:, i * DK : (i + 1) * DK]
        across = []
        for a in range(2):
            h = 2 * i + a
            c_col, beta_col = cols[:, a : a + 1], cols[:, 2 + a : 3 + a]
            growth = jnp.exp(c_col)
            end = c_col[TOK - 1 : TOK, :]
            state, later, update = s_ref[h], select(ggot_ref, gown_ref, h), u_ref[h]
            error = e_ref[h] + mm_nt(xz_ref[h], later)
            ratio = jnp.exp(jnp.minimum(c_col - c_ref[pl.ds(2 * j + a, 1), :], 0.0))
            pairs = jnp.where(strict, -mm_nt(error, update) * ratio, 0.0)
            shares = pairs * gram
            row_share = lane_sum(shares)
            across.append(jnp.sum(beta_col * shares, axis=0, keepdims=True))
            pair_sum += beta_col * pairs
            grad_value = beta_col * error
            dv_ref[:, h * DK : (h + 1) * DK] = grad_value
            reached = growth * mm(grad_value, state)
            tail = jnp.exp(end - c_col) * mm(update, later)
            grad_key += tail - reached
            tail_share = lane_sum(tail * unit)
            gate_share = jnp.exp(end) * jnp.sum(
                lane_sum(state.astype(F32) * later.astype(F32)), axis=0, keepdims=True
            )
            total = jnp.sum(tail_share, axis=0, keepdims=True) + gate_share
            grad_cum = beta_col * row_share - lane_sum(reached * unit) - tail_share
            grad_cum += jnp.where(last, total, 0.0)
            grad_beta = row_share + lane_sum(error * y_ref[h].astype(F32))
            down = jnp.where(lane == a, grad_cum, jnp.where(lane == 2 + a, grad_beta, down))
        pair_low = pair_sum.astype(BF)
        grad_key += mm(pair_low, low) + mm_tn(pair_low, low)
        dk_ref[:, i * DK : (i + 1) * DK] = rate * (grad_key - unit * lane_sum(unit * grad_key))
        turned = jnp.transpose(down + jnp.where(lane < 2, dcc_ref[i], 0.0))[:8]
        cum = turned + dcr_ref[i]
        for a in range(2):
            cum = jnp.where(sub == a, cum - across[a], cum)
        decayed = suffix_lanes(cum)
        for a in range(2):
            dd_ref[pl.ds(2 * j + a, 1), :] = decayed[a : a + 1]
            db_ref[pl.ds(2 * j + a, 1), :] = turned[2 + a : 3 + a]


def last_pass(place, key, cums, cols, state, got, own, error, y, update, xz, dk0, dcc, dcr, after):
    heads = 2 * KEYS
    return call(
        last_kernel,
        (
            shape(TOK, heads * DK),
            shape(TOK, KEYS * DK),
            shape(heads, TOK),
            shape(heads, TOK),
        ),
        (2,),
        [
            wide_spec(DK),
            whole(cums),
            lead_spec(TOK, DK),
            heads_spec(DK, DK),
            whole(got),
            whole(own),
            heads_spec(TOK, DK),
            heads_spec(TOK, DK),
            heads_spec(TOK, DK),
            heads_spec(TOK, DK),
            wide_spec(DK),
            lead_spec(TOK, DK),
            lead_spec(8, TOK),
        ],
        (wide_spec(2 * DK), wide_spec(DK), whole(cums), whole(cums)),
        (key, cums, cols, state, got, own, error, y, update, xz, dk0, dcc, dcr),
        SHORT,
        prefetch=place,
        after=after,
    )


def back_kernel(place_ref, cot_ref, w_ref, out_ref):
    part = mm(cot_ref[0], w_ref[...])

    @pl.when(pl.program_id(0) == 0)
    def _():
        out_ref[...] = part

    @pl.when(pl.program_id(0) > 0)
    def _():
        out_ref[...] += part


def back_pass(place, cot, weight, after):
    depth, wide = cot.shape[2], weight.shape[1]
    out = shape(TOK, wide)
    return call(
        back_kernel,
        (out,),
        (NH,),
        [
            pl.BlockSpec((1, TOK, depth), lambda k, place: (k, 0, 0)),
            pl.BlockSpec((depth, wide), lambda k, place: ((place[0] + k) % NH, 0)),
        ],
        (whole(out),),
        (cot, weight),
        LONG,
        prefetch=place,
        after=after,
    )[0]


def mix_kernel(place_ref, norm_ref, w_ref, out_ref):
    out_ref[0] = mm_nt(norm_ref[...], w_ref[...]).astype(BF)


def mix_pass(place, normed, weight, after):
    depth = weight.shape[0] // NH
    out = shape(NH, TOK, depth, dtype=BF)
    return call(
        mix_kernel,
        (out,),
        (NH,),
        [
            whole(normed),
            pl.BlockSpec((depth, weight.shape[1]), lambda k, place: ((place[0] + k) % NH, 0)),
        ],
        (pl.BlockSpec((1, TOK, depth), lambda k, place: (k, 0, 0)),),
        (normed, weight),
        SHORT,
        prefetch=place,
        after=after,
    )[0]


def outer_kernel(place_ref, cot_ref, norm_ref, mine_ref, other_ref):
    here, core = place_ref[2], place_ref[3]
    rows = mine_ref.shape[2]
    for k in range(NZ):
        start = pl.multiple_of(((here + k) % NZ) * 2 * rows, 2 * rows)
        part = mm_tn(cot_ref[0, :, pl.ds(start, 2 * rows)], norm_ref[...]).astype(BF)
        first = core == 0
        mine_ref[0, k] = jnp.where(first, part[:rows], part[rows:])
        other_ref[0, k] = jnp.where(first, part[rows:], part[:rows])


def outer_pass(place, cot, normed, after):
    rows = cot.shape[2] // (NZ * NC)
    out = shape(NY, NZ, rows, normed.shape[1], dtype=BF)
    spec = pl.BlockSpec((1, NZ, rows, normed.shape[1]), lambda k, place: (k, 0, 0, 0))
    return call(
        outer_kernel,
        (out, out),
        (NY,),
        [
            pl.BlockSpec(
                (1, TOK, cot.shape[2]), lambda k, place: ((place[1] + k - place[0] + NH) % NH, 0, 0)
            ),
            whole(normed),
        ],
        (spec, spec),
        (cot, normed),
        LONG,
        prefetch=place,
        after=after,
    )


def blend_kernel(place_ref, mine_ref, other_ref, *out_refs):
    for y in range(NY):
        for z in range(NZ):
            total = mine_ref[y, z].astype(F32) + other_ref[y, z].astype(F32)
            out_refs[y][z] = total.astype(BF)


def blend_pass(place, mine, other, after):
    outs = (shape(NZ, *mine.shape[2:], dtype=BF),) * NY
    return single(blend_kernel, outs, (mine, other), place, after, LONG)


def sum_kernel(place_ref, *refs):
    for z in range(NZ):
        refs[NY + z][...] = sum(refs[y][z].astype(F32) for y in range(NY)).astype(BF)


def sum_pass(place, parts, after):
    outs = (shape(*parts[0].shape[1:], dtype=BF),) * NZ
    return single(sum_kernel, outs, parts, place, after)


def shift(array, axis, count, step):
    return lax.ppermute(array, axis, [(i, (i + step) % count) for i in range(count)])


def spread(parts, axis, count, sign=1):
    return [parts[0]] + [shift(parts[k], axis, count, sign * k) for k in range(1, count)]


def scatter_stage(parts, axis, count):
    return sum(part.astype(F32) for part in spread(parts, axis, count))


def swap(array):
    return lax.ppermute(array, "c", [(0, 1), (1, 0)])


def body(query, key, value, beta, decay, wo_start, wo_end, curve_index, cotangent):
    place = jnp.stack([lax.axis_index(a) for a in ("head", "y", "z", "c")]).astype(jnp.int32)
    position = curve_index[0].astype(F32) / (CURVE_POINTS - 1)
    weight_local = (
        (1.0 - position) * wo_start.astype(F32) + position * wo_end.astype(F32)
    ).astype(BF)
    weight = lax.all_gather(weight_local, RING, axis=0, tiled=True)
    cot = jnp.stack([cotangent] + [shift(cotangent, "head", NH, -k) for k in range(1, NH)])

    sent, kept, inverse, wu, cums, cols = pre_pass(place, key, value, beta, decay)
    got = swap(sent)
    parts = spread(pair_pass(place, kept, got), "z", NZ)
    attend, carried, local, xz = attend_pass(
        place, query, key, cums, cols, inverse, wu, (parts[0],)
    )
    row, nx, bx, gx, total = prefix_pass(place, parts, (xz,))
    totals = [shift(total, "y", NY, k) for k in range(1, NY)]
    ns, gs = suffix_pass(place, row)
    states = spread(enter_pass(place, totals, nx, bx, gx, (ns,)), "z", NZ)
    grad_normed = back_pass(place, cot, weight, (ns,))
    own, send = split_pass(place, states, kept, got, (grad_normed,))
    normed, state, back, dsent, dkept = norm_pass(
        place, swap(send), own, carried, local, grad_normed
    )

    dgot = swap(dsent)
    grad_parts = spread(join_pass(place, kept, got, dkept, dgot, ()), "z", NZ)
    mine, other = outer_pass(place, cot, normed, (dgot,))
    theirs = swap(other)
    suffixes, grad_total, _ = later_pass(place, grad_parts, row, ())
    grads = [shift(grad_total, "y", NY, -k) for k in range(1, NY)]
    grad_query, update, dk0, error, y, dcc, dcr = middle_pass(
        place, query, key, value, cums, cols, state, back, attend, inverse, wu
    )
    laters = spread(leave_pass(place, totals, grads, ns, gs, suffixes, (dk0,)), "z", NZ)
    sums = spread(blend_pass(place, mine, theirs, (laters[0],)), "y", NY)
    gown, gsend = part_pass(place, laters, kept, got, dkept, dgot, (sums[0],))
    ggot = swap(gsend)

    grad_value, grad_key, grad_beta, grad_decay = last_pass(
        place, key, cums, cols, state, ggot, gown, error, y, update, xz, dk0, dcc, dcr, ()
    )
    mixes = mix_pass(place, normed, weight, (grad_beta,))
    mixed = scatter_stage([mixes[k] for k in range(NH)], "head", NH).astype(BF)
    sums = sum_pass(place, sums, (grad_beta,))
    grad_weight = scatter_stage(sums, "z", NZ)
    return (
        mixed,
        grad_query,
        grad_key,
        grad_value,
        grad_beta,
        grad_decay,
        (1.0 - position) * grad_weight,
        position * grad_weight,
    )


def solution(mesh):
    fine = Mesh(mesh.devices.reshape(NY, NZ, NC, NH), ("y", "z", "c", "head"))
    rows, flipped = P(RING, "head"), P("head", RING)
    return jax.shard_map(
        body,
        mesh=fine,
        in_specs=(rows, rows, rows, flipped, flipped, rows, rows, P(), rows),
        out_specs=(rows, rows, rows, rows, flipped, flipped, rows, rows),
        check_vma=False,
    )
```

```python
import jax
import jax.numpy as jnp
from jax import lax
from jax.experimental import pallas as pl
from jax.experimental.pallas import tpu as pltpu
from jax.sharding import Mesh, PartitionSpec as P

DK = 128
DV = 128
CURVE_POINTS = 257
EPS = 1e-06
NY, NZ, NC, NH = 4, 4, 2, 4
TOK = 256
HALF = 128
KEYS = 4
ROWS = 272
GROUP = 4
VMEM = 14 * 2**20
SHORT = 10**6
LONG = 5 * 10**9
BF = jnp.bfloat16
F32 = jnp.float32
RING = ("y", "z", "c")
INTERPRET = False


def dot(left, right, dims):
    return lax.dot_general(
        left.astype(BF), right.astype(BF), (dims, ((), ())), preferred_element_type=F32
    )


def mm(left, right):
    return dot(left, right, ((1,), (0,)))


def mm_nt(left, right):
    return dot(left, right, ((1,), (1,)))


def mm_tn(left, right):
    return dot(left, right, ((0,), (0,)))


def iota(shape, dim):
    return lax.broadcasted_iota(jnp.int32, shape, dim)


def lane_sum(array):
    return jnp.sum(array, axis=1, keepdims=True)


def call(
    kernel, out_shape, grid, in_specs, out_specs, args, flops, prefetch=None, after=(), vmem=VMEM
):
    count = len(args) + (prefetch is not None)

    def run(*refs):
        kernel(*refs[:count], *refs[count + len(after) :])

    in_specs = [*in_specs, *(pl.BlockSpec(memory_space=pl.ANY) for _ in after)]
    args = (*args, *after)
    spec = dict(grid=grid, in_specs=in_specs, out_specs=out_specs)
    extra = {}
    if prefetch is None:
        extra = spec
    else:
        extra = dict(grid_spec=pltpu.PrefetchScalarGridSpec(num_scalar_prefetch=1, **spec))
        args = (prefetch, *args)
    return pl.pallas_call(
        run,
        out_shape=out_shape,
        compiler_params=pltpu.CompilerParams(vmem_limit_bytes=vmem),
        cost_estimate=pl.CostEstimate(flops=flops, bytes_accessed=1, transcendentals=0),
        interpret=INTERPRET,
        name=kernel.__name__,
        **extra,
    )(*args)


def shape(*dims, dtype=F32):
    return jax.ShapeDtypeStruct(dims, dtype)


def whole(array):
    return pl.BlockSpec(array.shape, lambda *_: (0,) * len(array.shape))


def heads_spec(rows, cols):
    return pl.BlockSpec((GROUP, rows, cols), lambda s, place: (s, 0, 0))


def lead_spec(rows, cols):
    return pl.BlockSpec((2, rows, cols), lambda s, place: (s, 0, 0))


def half_of(step, place):
    return (1 - place[3] + step) % 2


def key_head(i, place_ref):
    return 2 * half_of(pl.program_id(0), place_ref) + i


def wide_spec(cols):
    return pl.BlockSpec((TOK, 2 * cols), lambda s, place: (0, half_of(s, place)))


def gate_parts(gate):
    full = jnp.broadcast_to(gate, (16, DK))
    one = full.astype(BF)
    two = (full - one.astype(F32)).astype(BF)
    three = (full - one.astype(F32) - two.astype(F32)).astype(BF)
    place = iota((16, DK), 0)
    parts = jnp.where(place == 0, one.astype(F32), 0.0)
    parts = jnp.where(place == 1, two.astype(F32), parts)
    return jnp.where(place == 2, three.astype(F32), parts).astype(BF)


def gate_of(block):
    return jnp.sum(block[2 * DK :, :].astype(F32), axis=0, keepdims=True)


def unit_keys(key_block):
    raw = key_block.astype(F32)
    rate = lax.rsqrt(lane_sum(raw * raw) + EPS)
    return raw * rate, rate


def prefix_lanes(array):
    size = array.shape[1]
    lane = iota(array.shape, 1)
    step = 1
    while step < size:
        array = array + jnp.where(lane >= step, pltpu.roll(array, step, 1), 0.0)
        step *= 2
    return array


def suffix_lanes(array):
    size = array.shape[1]
    lane = iota(array.shape, 1)
    step = 1
    while step < size:
        array = array + jnp.where(lane < size - step, pltpu.roll(array, size - step, 1), 0.0)
        step *= 2
    return array


def invert_blocks(lowers):
    row, col = iota((HALF, HALF), 0), iota((HALF, HALF), 1)
    apart = row ^ col
    eye = jnp.where(row == col, 1.0, 0.0)
    found = [eye - jnp.where(apart < 2, low, 0.0) for low in lowers]
    size = 2
    while size < HALF:
        mask = (apart >= size) & (apart < 2 * size)
        offs = [jnp.where(mask, low, 0.0).astype(BF) for low in lowers]
        lows = [x.astype(BF) for x in found]
        halfway = [mm(x, off) for x, off in zip(lows, offs)]
        found = [f - mm(m, x) for f, m, x in zip(found, halfway, lows)]
        size *= 2
    return found


def pre_kernel(
    place_ref, k_ref, v_ref, beta_ref, decay_ref, sent_ref, kept_ref, x_ref, wu_ref, c_ref, cols_ref
):
    step = pl.program_id(0)

    @pl.when(step == 0)
    def _():
        c_ref[...] = prefix_lanes(decay_ref[...])

    strict = iota((TOK, TOK), 0) > iota((TOK, TOK), 1)
    sub = iota((8, TOK), 0)
    units, columns, lowers = [], [], []
    for i in range(2):
        j = key_head(i, place_ref)
        unit, _ = unit_keys(k_ref[:, i * DK : (i + 1) * DK])
        low = unit.astype(BF)
        gram = mm_nt(low, low)
        rows = [c_ref[pl.ds(2 * j + a, 1), :] for a in range(2)]
        rates = [beta_ref[pl.ds(2 * j + a, 1), :] for a in range(2)]
        packed = jnp.zeros((8, TOK), F32)
        for spot, line in enumerate((*rows, *rates)):
            packed = jnp.where(sub == spot, line, packed)
        cols = jnp.transpose(jnp.concatenate([packed, jnp.zeros((HALF - 8, TOK), F32)], axis=0))
        cols_ref[i] = cols
        units.append(unit)
        columns.append(cols)
        for a in range(2):
            ratio = jnp.exp(jnp.minimum(cols[:, a : a + 1] - rows[a], 0.0))
            lowers.append(jnp.where(strict, cols[:, 2 + a : 3 + a] * gram * ratio, 0.0))
    found = invert_blocks(
        [low[b * HALF : (b + 1) * HALF, b * HALF : (b + 1) * HALF] for low in lowers for b in (0, 1)]
    )
    for h in range(GROUP):
        i, a = h // 2, h % 2
        unit, cols = units[i], columns[i]
        first, second = found[2 * h].astype(BF), found[2 * h + 1].astype(BF)
        corner = -mm(mm(second, lowers[h][HALF:, :HALF]), first)
        inverse = jnp.concatenate(
            [
                jnp.concatenate([first, jnp.zeros((HALF, HALF), BF)], axis=1),
                jnp.concatenate([corner.astype(BF), second], axis=1),
            ],
            axis=0,
        )
        x_ref[h] = inverse
        c_col, beta_col = cols[:, a : a + 1], cols[:, 2 + a : 3 + a]
        value = v_ref[:, h * DK : (h + 1) * DK].astype(F32)
        right = jnp.concatenate(
            [(beta_col * jnp.exp(c_col) * unit).astype(BF), (beta_col * value).astype(BF)], axis=1
        )
        wu = mm(inverse, right).astype(BF)
        wu_ref[h] = wu
        end = c_col[TOK - 1 : TOK, :]
        moved = mm_tn(wu, jnp.exp(end - c_col) * unit).astype(BF)
        gate = gate_parts(jnp.exp(end))

        @pl.when(step == 0)
        def _():
            sent_ref[h, : 2 * DK, :] = moved
            sent_ref[h, 2 * DK :, :] = gate

        @pl.when(step == 1)
        def _():
            kept_ref[h, : 2 * DK, :] = moved
            kept_ref[h, 2 * DK :, :] = gate


def pre_pass(place, key, value, beta, decay):
    heads = 2 * KEYS
    pay = shape(GROUP, ROWS, DK, dtype=BF)

    return call(
        pre_kernel,
        (
            pay,
            pay,
            shape(heads, TOK, TOK, dtype=BF),
            shape(heads, TOK, 2 * DK, dtype=BF),
            shape(heads, TOK),
            shape(KEYS, TOK, DK),
        ),
        (2,),
        [wide_spec(DK), wide_spec(2 * DK), whole(beta), whole(decay)],
        (
            whole(pay),
            whole(pay),
            heads_spec(TOK, TOK),
            heads_spec(TOK, 2 * DK),
            whole(decay),
            lead_spec(TOK, DK),
        ),
        (key, value, beta, decay),
        SHORT,
        prefetch=place,
    )


def attend_kernel(
    place_ref, q_ref, k_ref, c_ref, cols_ref, x_ref, wu_ref, p_ref, car_ref, out_ref, xz_ref
):
    inclusive = iota((TOK, TOK), 0) >= iota((TOK, TOK), 1)
    for i in range(2):
        j = key_head(i, place_ref)
        unit, _ = unit_keys(k_ref[:, i * DK : (i + 1) * DK])
        query = q_ref[:, i * DK : (i + 1) * DK]
        gram = mm_nt(query, unit)
        cols = cols_ref[i]
        for a in range(2):
            h = 2 * i + a
            c_col = cols[:, a : a + 1]
            ratio = jnp.exp(jnp.minimum(c_col - c_ref[pl.ds(2 * j + a, 1), :], 0.0))
            attend = jnp.where(inclusive, gram * ratio, 0.0).astype(BF)
            p_ref[h] = attend
            both = mm(attend, wu_ref[h])
            car_ref[h] = (jnp.exp(c_col) * query.astype(F32) - both[:, :DK]).astype(BF)
            out_ref[h] = both[:, DK:]
            tail = jnp.exp(c_col[TOK - 1 : TOK, :] - c_col) * unit
            xz_ref[h] = mm_tn(x_ref[h], tail).astype(BF)


def attend_pass(place, query, key, cums, cols, inverse, wu, after):
    heads = 2 * KEYS
    return call(
        attend_kernel,
        (
            shape(heads, TOK, TOK, dtype=BF),
            shape(heads, TOK, DK, dtype=BF),
            shape(heads, TOK, DK),
            shape(heads, TOK, DK, dtype=BF),
        ),
        (2,),
        [
            wide_spec(DK),
            wide_spec(DK),
            whole(cums),
            lead_spec(TOK, DK),
            heads_spec(TOK, TOK),
            heads_spec(TOK, 2 * DK),
        ],
        (
            heads_spec(TOK, TOK),
            heads_spec(TOK, DK),
            heads_spec(TOK, DK),
            heads_spec(TOK, DK),
        ),
        (query, key, cums, cols, inverse, wu),
        LONG,
        prefetch=place,
        after=after,
    )


def single(kernel, outs, args, place, after=(), cost=SHORT):
    return call(
        kernel,
        outs,
        (1,),
        [whole(a) for a in args],
        tuple(whole(o) for o in outs),
        args,
        cost,
        prefetch=place,
        after=after,
    )


def pair_kernel(place_ref, kept_ref, got_ref, *out_refs):
    z, core = place_ref[2], place_ref[3]
    for k in range(NZ):
        head = (z + k) % NZ
        kept, got = kept_ref[head], got_ref[head]
        early, late = jnp.where(core == 0, kept, got), jnp.where(core == 0, got, kept)
        early_gate, late_gate = gate_of(early), gate_of(late)
        moved = late[:DK].astype(F32)
        out_refs[k][: 2 * DK, :] = (
            late_gate * early[: 2 * DK].astype(F32)
            - mm(early[: 2 * DK], late[:DK])
            + jnp.concatenate([early_gate * moved, late[DK : 2 * DK].astype(F32)], axis=0)
        ).astype(BF)
        out_refs[k][2 * DK :, :] = gate_parts(early_gate * late_gate)


def pair_pass(place, kept, got):
    return single(pair_kernel, (shape(ROWS, DK, dtype=BF),) * NZ, (kept, got), place)


def prefix_kernel(place_ref, *refs):
    parts, (row_ref, nx_ref, bx_ref, gx_ref, tot_ref) = refs[:NZ], refs[NZ:]
    z = place_ref[2]
    for k in range(NZ):
        row_ref[(z - k + NZ) % NZ] = parts[k][...]
    both = jnp.zeros((2 * DK, DK), F32)
    gate = jnp.ones((1, DK), F32)
    for i in range(NZ):
        nx_ref[i] = both[:DK].astype(BF)
        bx_ref[i] = both[DK:]
        gx_ref[i : i + 1, :] = gate
        block = row_ref[i]
        step_gate = gate_of(block)
        moved = block[:DK].astype(F32)
        both = (
            step_gate * both
            - mm(both, block[:DK])
            + jnp.concatenate([gate * moved, block[DK : 2 * DK].astype(F32)], axis=0)
        )
        gate = gate * step_gate
    tot_ref[: 2 * DK, :] = both.astype(BF)
    tot_ref[2 * DK :, :] = gate_parts(gate)


def prefix_pass(place, parts, after):
    outs = (
        shape(NZ, ROWS, DK, dtype=BF),
        shape(NZ, DK, DK, dtype=BF),
        shape(NZ, DK, DK),
        shape(8, DK),
        shape(ROWS, DK, dtype=BF),
    )
    return single(prefix_kernel, outs, parts, place, after)


def suffix_kernel(place_ref, row_ref, ns_ref, gs_ref):
    later = jnp.zeros((DK, DK), F32)
    gate = jnp.ones((1, DK), F32)
    for i in reversed(range(NZ)):
        ns_ref[i] = later.astype(BF)
        gs_ref[i : i + 1, :] = gate
        block = row_ref[i]
        step_gate = gate_of(block)
        moved = block[:DK]
        later = step_gate * later + gate * moved.astype(F32) - mm(moved, later)
        gate = gate * step_gate


def suffix_pass(place, row):
    return single(suffix_kernel, (shape(NZ, DK, DK, dtype=BF), shape(8, DK)), (row,), place, cost=LONG)


def enter_kernel(place_ref, one_ref, two_ref, three_ref, nx_ref, bx_ref, gx_ref, *out_refs):
    here, z = place_ref[1], place_ref[2]
    state = jnp.zeros((DK, DK), F32)
    for back, ref in ((3, three_ref), (2, two_ref), (1, one_ref)):
        block = ref[...]
        moved = gate_of(block) * state - mm(state, block[:DK]) + block[DK : 2 * DK].astype(F32)
        state = jnp.where(here >= back, moved, state)
    for k in range(NZ):
        i = (z + k) % NZ
        out_refs[k][...] = gx_ref[pl.ds(i, 1), :] * state - mm(state, nx_ref[i]) + bx_ref[i]


def enter_pass(place, totals, nx, bx, gx, after):
    outs = (shape(DK, DK),) * NZ
    return single(enter_kernel, outs, (*totals, nx, bx, gx), place, after)


def split_kernel(place_ref, *refs):
    states, (kept_ref, got_ref, own_ref, send_ref) = refs[:NZ], refs[NZ:]
    z, first = place_ref[2], place_ref[3] == 0
    for k in range(NZ):
        head = (z - k + NZ) % NZ
        early = jnp.where(first, kept_ref[head], got_ref[head])
        state = states[k][...]
        moved = (
            gate_of(early) * state - mm(state, early[:DK]) + early[DK : 2 * DK].astype(F32)
        )
        own_ref[head] = jnp.where(first, state, moved)
        send_ref[head] = jnp.where(first, moved, state)


def split_pass(place, states, kept, got, after):
    outs = (shape(GROUP, DK, DK),) * 2
    return single(split_kernel, outs, (*states, kept, got), place, after)


def two_parts(array):
    high = array.astype(BF)
    return high, (array - high.astype(F32)).astype(BF)


def select(theirs_ref, mine_ref, h):
    return jnp.where(pl.program_id(0) == 0, theirs_ref[h], mine_ref[h])


def norm_kernel(
    place_ref, got_ref, own_ref, car_ref, loc_ref, gn_ref,
    norm_ref, s_ref, do_ref, sent_ref, kept_ref,
):
    first = pl.program_id(0) == 0
    for h in range(GROUP):
        state, carried = select(got_ref, own_ref, h).astype(BF), car_ref[h]
        s_ref[h] = state
        head = loc_ref[h] + mm_nt(carried, state)
        scale = lax.rsqrt(lane_sum(head * head) * (1.0 / DK) + EPS)
        normed = head * scale
        norm_ref[:, h * DK : (h + 1) * DK] = normed.astype(BF)
        grad = gn_ref[:, h * DK : (h + 1) * DK]
        inner = lane_sum(grad * normed) * (1.0 / DK)
        back = scale * (grad - normed * inner)
        do_ref[h] = back
        both = mm_tn(jnp.concatenate(two_parts(back), axis=1), carried)
        direct = both[:DV] + both[DV:]

        @pl.when(first)
        def _():
            sent_ref[h] = direct

        @pl.when(jnp.logical_not(first))
        def _():
            kept_ref[h] = direct


def norm_pass(place, got, own, carried, local, grad_normed):
    heads = 2 * KEYS
    half = shape(GROUP, DK, DK)
    return call(
        norm_kernel,
        (
            shape(TOK, heads * DK, dtype=BF),
            shape(heads, DK, DK, dtype=BF),
            shape(heads, TOK, DK),
            half,
            half,
        ),
        (2,),
        [
            whole(got),
            whole(own),
            heads_spec(TOK, DK),
            heads_spec(TOK, DK),
            wide_spec(2 * DK),
        ],
        (wide_spec(2 * DK), heads_spec(DK, DK), heads_spec(TOK, DK), whole(half), whole(half)),
        (got, own, carried, local, grad_normed),
        SHORT,
        prefetch=place,
    )


def middle_kernel(
    place_ref, q_ref, k_ref, v_ref, c_ref, cols_ref, s_ref, do_ref, p_ref, x_ref, wu_ref,
    dq_ref, u_ref, dk_ref, e_ref, y_ref, dcc_ref, dcr_ref,
):
    inclusive = iota((TOK, TOK), 0) >= iota((TOK, TOK), 1)
    lane = iota((TOK, DK), 1)
    sub = iota((8, TOK), 0)
    for i in range(2):
        j = key_head(i, place_ref)
        unit, _ = unit_keys(k_ref[:, i * DK : (i + 1) * DK])
        low = unit.astype(BF)
        query = q_ref[:, i * DK : (i + 1) * DK]
        wide = query.astype(F32)
        cols = cols_ref[i]
        down = jnp.zeros((TOK, DK), F32)
        across = jnp.zeros((8, TOK), F32)
        pair_sum = jnp.zeros((TOK, TOK), F32)
        grad_query = jnp.zeros((TOK, DK), F32)
        for a in range(2):
            h = 2 * i + a
            c_col = cols[:, a : a + 1]
            growth = jnp.exp(c_col)
            state, attend = s_ref[h], p_ref[h]
            back, rest = two_parts(do_ref[h])
            update = (wu_ref[h, :, DK:].astype(F32) - mm_nt(wu_ref[h, :, :DK], state)).astype(BF)
            u_ref[h] = update
            pairs = mm_nt(back, update) + mm_nt(rest, update)
            ratio = jnp.exp(jnp.minimum(c_col - c_ref[pl.ds(2 * j + a, 1), :], 0.0))
            pair_sum += jnp.where(inclusive, pairs * ratio, 0.0)
            shares = pairs * attend.astype(F32)
            reached = growth * (mm(back, state) + mm(rest, state))
            grad_query += reached
            down = jnp.where(lane == a, lane_sum(shares) + lane_sum(reached * wide), down)
            across = jnp.where(sub == a, -jnp.sum(shares, axis=0, keepdims=True), across)
            e_ref[h] = mm_tn(x_ref[h], mm_tn(attend, back))
            value = v_ref[:, h * DK : (h + 1) * DK].astype(F32)
            y_ref[h] = (value - growth * mm_nt(low, state)).astype(BF)
        pair_low = pair_sum.astype(BF)
        dq_ref[:, i * DK : (i + 1) * DK] = grad_query + mm(pair_low, low)
        dk_ref[:, i * DK : (i + 1) * DK] = mm_tn(pair_low, query)
        dcc_ref[i] = down
        dcr_ref[i] = across


def middle_pass(place, query, key, value, cums, cols, state, back, attend, inverse, wu):
    heads = 2 * KEYS
    return call(
        middle_kernel,
        (
            shape(TOK, KEYS * DK),
            shape(heads, TOK, DK, dtype=BF),
            shape(TOK, KEYS * DK),
            shape(heads, TOK, DK),
            shape(heads, TOK, DK, dtype=BF),
            shape(KEYS, TOK, DK),
            shape(KEYS, 8, TOK),
        ),
        (2,),
        [
            wide_spec(DK),
            wide_spec(DK),
            wide_spec(2 * DK),
            whole(cums),
            lead_spec(TOK, DK),
            heads_spec(DK, DK),
            heads_spec(TOK, DK),
            heads_spec(TOK, TOK),
            heads_spec(TOK, TOK),
            heads_spec(TOK, 2 * DK),
        ],
        (
            wide_spec(DK),
            heads_spec(TOK, DK),
            wide_spec(DK),
            heads_spec(TOK, DK),
            heads_spec(TOK, DK),
            lead_spec(TOK, DK),
            lead_spec(8, TOK),
        ),
        (query, key, value, cums, cols, state, back, attend, inverse, wu),
        2 * LONG,
        prefetch=place,
    )


def join_kernel(place_ref, kept_ref, got_ref, dkept_ref, dgot_ref, *out_refs):
    z, first = place_ref[2], place_ref[3] == 0
    for k in range(NZ):
        head = (z + k) % NZ
        early = jnp.where(first, kept_ref[head], got_ref[head])
        before = jnp.where(first, dkept_ref[head], dgot_ref[head])
        after = jnp.where(first, dgot_ref[head], dkept_ref[head])
        out_refs[k][...] = gate_of(early) * after - mm_nt(after, early[:DK]) + before


def join_pass(place, kept, got, dkept, dgot, after):
    outs = (shape(DK, DK),) * NZ
    return single(join_kernel, outs, (kept, got, dkept, dgot), place, after)


def later_kernel(place_ref, *refs):
    parts, (row_ref, d_ref, tot_ref, line_ref) = refs[:NZ], refs[NZ:]
    z = place_ref[2]
    for k in range(NZ):
        line_ref[(z - k + NZ) % NZ] = parts[k][...]
    total = jnp.zeros((DK, DK), F32)
    for i in reversed(range(NZ)):
        d_ref[i] = total
        block = row_ref[i]
        total = gate_of(block) * total - mm_nt(total, block[:DK]) + line_ref[i]
    tot_ref[...] = total


def later_pass(place, parts, row, after):
    outs = (shape(NZ, DK, DK), shape(DK, DK), shape(NZ, DK, DK))
    return single(later_kernel, outs, (*parts, row), place, after)


def leave_kernel(
    place_ref, one_ref, two_ref, three_ref, g1_ref, g2_ref, g3_ref, ns_ref, gs_ref, d_ref, *out_refs
):
    here, z = place_ref[1], place_ref[2]
    total = jnp.zeros((DK, DK), F32)
    for ahead, ref, grad in ((3, one_ref, g3_ref), (2, two_ref, g2_ref), (1, three_ref, g1_ref)):
        block = ref[...]
        moved = gate_of(block) * total - mm_nt(total, block[:DK]) + grad[...]
        total = jnp.where(here + ahead < NY, moved, total)
    for k in range(NZ):
        i = (z + k) % NZ
        out_refs[k][...] = gs_ref[pl.ds(i, 1), :] * total - mm_nt(total, ns_ref[i]) + d_ref[i]


def leave_pass(place, totals, grads, ns, gs, directs, after):
    outs = (shape(DK, DK),) * NZ
    return single(leave_kernel, outs, (*totals, *grads, ns, gs, directs), place, after)


def part_kernel(place_ref, *refs):
    grads, (kept_ref, got_ref, dkept_ref, dgot_ref, own_ref, send_ref) = refs[:NZ], refs[NZ:]
    z, first = place_ref[2], place_ref[3] == 0
    for k in range(NZ):
        head = (z - k + NZ) % NZ
        late = jnp.where(first, got_ref[head], kept_ref[head])
        direct = jnp.where(first, dgot_ref[head], dkept_ref[head])
        grad = grads[k][...]
        moved = gate_of(late) * grad - mm_nt(grad, late[:DK]) + direct
        own_ref[head] = jnp.where(first, moved, grad)
        send_ref[head] = jnp.where(first, grad, moved)


def part_pass(place, grads, kept, got, dkept, dgot, after):
    outs = (shape(GROUP, DK, DK),) * 2
    return single(part_kernel, outs, (*grads, kept, got, dkept, dgot), place, after)


def last_kernel(
    place_ref, k_ref, c_ref, cols_ref, s_ref, ggot_ref, gown_ref, e_ref, y_ref, u_ref, xz_ref,
    dk0_ref, dcc_ref, dcr_ref, dv_ref, dk_ref, db_ref, dd_ref,
):
    strict = iota((TOK, TOK), 0) > iota((TOK, TOK), 1)
    last = iota((TOK, 1), 0) == TOK - 1
    lane = iota((TOK, DK), 1)
    sub = iota((8, TOK), 0)
    for i in range(2):
        j = key_head(i, place_ref)
        unit, rate = unit_keys(k_ref[:, i * DK : (i + 1) * DK])
        low = unit.astype(BF)
        gram = mm_nt(low, low)
        cols = cols_ref[i]
        down = jnp.zeros((TOK, DK), F32)
        pair_sum = jnp.zeros((TOK, TOK), F32)
        grad_key = dk0_ref[:, i * DK : (i + 1) * DK]
        across = []
        for a in range(2):
            h = 2 * i + a
            c_col, beta_col = cols[:, a : a + 1], cols[:, 2 + a : 3 + a]
            growth = jnp.exp(c_col)
            end = c_col[TOK - 1 : TOK, :]
            state, later, update = s_ref[h], select(ggot_ref, gown_ref, h), u_ref[h]
            error = e_ref[h] + mm_nt(xz_ref[h], later)
            ratio = jnp.exp(jnp.minimum(c_col - c_ref[pl.ds(2 * j + a, 1), :], 0.0))
            pairs = jnp.where(strict, -mm_nt(error, update) * ratio, 0.0)
            shares = pairs * gram
            row_share = lane_sum(shares)
            across.append(jnp.sum(beta_col * shares, axis=0, keepdims=True))
            pair_sum += beta_col * pairs
            grad_value = beta_col * error
            dv_ref[:, h * DK : (h + 1) * DK] = grad_value
            reached = growth * mm(grad_value, state)
            tail = jnp.exp(end - c_col) * mm(update, later)
            grad_key += tail - reached
            tail_share = lane_sum(tail * unit)
            gate_share = jnp.exp(end) * jnp.sum(
                lane_sum(state.astype(F32) * later.astype(F32)), axis=0, keepdims=True
            )
            total = jnp.sum(tail_share, axis=0, keepdims=True) + gate_share
            grad_cum = beta_col * row_share - lane_sum(reached * unit) - tail_share
            grad_cum += jnp.where(last, total, 0.0)
            grad_beta = row_share + lane_sum(error * y_ref[h].astype(F32))
            down = jnp.where(lane == a, grad_cum, jnp.where(lane == 2 + a, grad_beta, down))
        pair_low = pair_sum.astype(BF)
        grad_key += mm(pair_low, low) + mm_tn(pair_low, low)
        dk_ref[:, i * DK : (i + 1) * DK] = rate * (grad_key - unit * lane_sum(unit * grad_key))
        turned = jnp.transpose(down + jnp.where(lane < 2, dcc_ref[i], 0.0))[:8]
        cum = turned + dcr_ref[i]
        for a in range(2):
            cum = jnp.where(sub == a, cum - across[a], cum)
        decayed = suffix_lanes(cum)
        for a in range(2):
            dd_ref[pl.ds(2 * j + a, 1), :] = decayed[a : a + 1]
            db_ref[pl.ds(2 * j + a, 1), :] = turned[2 + a : 3 + a]


def last_pass(place, key, cums, cols, state, got, own, error, y, update, xz, dk0, dcc, dcr, after):
    heads = 2 * KEYS
    return call(
        last_kernel,
        (
            shape(TOK, heads * DK),
            shape(TOK, KEYS * DK),
            shape(heads, TOK),
            shape(heads, TOK),
        ),
        (2,),
        [
            wide_spec(DK),
            whole(cums),
            lead_spec(TOK, DK),
            heads_spec(DK, DK),
            whole(got),
            whole(own),
            heads_spec(TOK, DK),
            heads_spec(TOK, DK),
            heads_spec(TOK, DK),
            heads_spec(TOK, DK),
            wide_spec(DK),
            lead_spec(TOK, DK),
            lead_spec(8, TOK),
        ],
        (wide_spec(2 * DK), wide_spec(DK), whole(cums), whole(cums)),
        (key, cums, cols, state, got, own, error, y, update, xz, dk0, dcc, dcr),
        SHORT,
        prefetch=place,
        after=after,
    )


def back_kernel(place_ref, cot_ref, w_ref, out_ref):
    part = mm(cot_ref[0], w_ref[...])

    @pl.when(pl.program_id(0) == 0)
    def _():
        out_ref[...] = part

    @pl.when(pl.program_id(0) > 0)
    def _():
        out_ref[...] += part


def back_pass(place, cot, weight, after):
    depth, wide = cot.shape[2], weight.shape[1]
    out = shape(TOK, wide)
    return call(
        back_kernel,
        (out,),
        (NH,),
        [
            pl.BlockSpec((1, TOK, depth), lambda k, place: (k, 0, 0)),
            pl.BlockSpec((depth, wide), lambda k, place: ((place[0] + k) % NH, 0)),
        ],
        (whole(out),),
        (cot, weight),
        LONG,
        prefetch=place,
        after=after,
    )[0]


def mix_kernel(place_ref, norm_ref, w_ref, out_ref):
    out_ref[0] = mm_nt(norm_ref[...], w_ref[...]).astype(BF)


def mix_pass(place, normed, weight, after):
    depth = weight.shape[0] // NH
    out = shape(NH, TOK, depth, dtype=BF)
    return call(
        mix_kernel,
        (out,),
        (NH,),
        [
            whole(normed),
            pl.BlockSpec((depth, weight.shape[1]), lambda k, place: ((place[0] + k) % NH, 0)),
        ],
        (pl.BlockSpec((1, TOK, depth), lambda k, place: (k, 0, 0)),),
        (normed, weight),
        LONG,
        prefetch=place,
        after=after,
    )[0]


def outer_kernel(place_ref, cot_ref, norm_ref, mine_ref, other_ref):
    here, core = place_ref[2], place_ref[3]
    rows = mine_ref.shape[2]
    for k in range(NZ):
        start = pl.multiple_of(((here + k) % NZ) * 2 * rows, 2 * rows)
        part = mm_tn(cot_ref[0, :, pl.ds(start, 2 * rows)], norm_ref[...]).astype(BF)
        first = core == 0
        mine_ref[0, k] = jnp.where(first, part[:rows], part[rows:])
        other_ref[0, k] = jnp.where(first, part[rows:], part[:rows])


def outer_pass(place, cot, normed, after):
    rows = cot.shape[2] // (NZ * NC)
    out = shape(NY, NZ, rows, normed.shape[1], dtype=BF)
    spec = pl.BlockSpec((1, NZ, rows, normed.shape[1]), lambda k, place: (k, 0, 0, 0))
    return call(
        outer_kernel,
        (out, out),
        (NY,),
        [
            pl.BlockSpec(
                (1, TOK, cot.shape[2]), lambda k, place: ((place[1] + k - place[0] + NH) % NH, 0, 0)
            ),
            whole(normed),
        ],
        (spec, spec),
        (cot, normed),
        LONG,
        prefetch=place,
        after=after,
    )


def blend_kernel(place_ref, mine_ref, other_ref, *out_refs):
    for y in range(NY):
        for z in range(NZ):
            total = mine_ref[y, z].astype(F32) + other_ref[y, z].astype(F32)
            out_refs[y][z] = total.astype(BF)


def blend_pass(place, mine, other, after):
    outs = (shape(NZ, *mine.shape[2:], dtype=BF),) * NY
    return single(blend_kernel, outs, (mine, other), place, after, LONG)


def sum_kernel(place_ref, *refs):
    for z in range(NZ):
        refs[NY + z][...] = sum(refs[y][z].astype(F32) for y in range(NY)).astype(BF)


def sum_pass(place, parts, after):
    outs = (shape(*parts[0].shape[1:], dtype=BF),) * NZ
    return single(sum_kernel, outs, parts, place, after)


def shift(array, axis, count, step):
    return lax.ppermute(array, axis, [(i, (i + step) % count) for i in range(count)])


def spread(parts, axis, count, sign=1):
    return [parts[0]] + [shift(parts[k], axis, count, sign * k) for k in range(1, count)]


def scatter_stage(parts, axis, count):
    return sum(part.astype(F32) for part in spread(parts, axis, count))


def swap(array):
    return lax.ppermute(array, "c", [(0, 1), (1, 0)])


def body(query, key, value, beta, decay, wo_start, wo_end, curve_index, cotangent):
    place = jnp.stack([lax.axis_index(a) for a in ("head", "y", "z", "c")]).astype(jnp.int32)
    position = curve_index[0].astype(F32) / (CURVE_POINTS - 1)
    weight_local = (
        (1.0 - position) * wo_start.astype(F32) + position * wo_end.astype(F32)
    ).astype(BF)
    weight = lax.all_gather(weight_local, RING, axis=0, tiled=True)
    cot = jnp.stack([cotangent] + [shift(cotangent, "head", NH, -k) for k in range(1, NH)])

    sent, kept, inverse, wu, cums, cols = pre_pass(place, key, value, beta, decay)
    got = swap(sent)
    parts = spread(pair_pass(place, kept, got), "z", NZ)
    attend, carried, local, xz = attend_pass(
        place, query, key, cums, cols, inverse, wu, (parts[0],)
    )
    row, nx, bx, gx, total = prefix_pass(place, parts, (xz,))
    totals = [shift(total, "y", NY, k) for k in range(1, NY)]
    ns, gs = suffix_pass(place, row)
    states = spread(enter_pass(place, totals, nx, bx, gx, (ns,)), "z", NZ)
    grad_normed = back_pass(place, cot, weight, (ns,))
    own, send = split_pass(place, states, kept, got, (grad_normed,))
    normed, state, back, dsent, dkept = norm_pass(
        place, swap(send), own, carried, local, grad_normed
    )

    dgot = swap(dsent)
    grad_parts = spread(join_pass(place, kept, got, dkept, dgot, ()), "z", NZ)
    mine, other = outer_pass(place, cot, normed, (dgot,))
    theirs = swap(other)
    mixes = mix_pass(place, normed, weight, (grad_parts[0],))
    suffixes, grad_total, _ = later_pass(place, grad_parts, row, (mixes,))
    grads = [shift(grad_total, "y", NY, -k) for k in range(1, NY)]
    grad_query, update, dk0, error, y, dcc, dcr = middle_pass(
        place, query, key, value, cums, cols, state, back, attend, inverse, wu
    )
    laters = spread(leave_pass(place, totals, grads, ns, gs, suffixes, (dk0,)), "z", NZ)
    sums = spread(blend_pass(place, mine, theirs, (laters[0],)), "y", NY)
    gown, gsend = part_pass(place, laters, kept, got, dkept, dgot, (sums[0],))
    ggot = swap(gsend)

    grad_value, grad_key, grad_beta, grad_decay = last_pass(
        place, key, cums, cols, state, ggot, gown, error, y, update, xz, dk0, dcc, dcr, ()
    )
    mixes, grad_beta = lax.optimization_barrier((mixes, grad_beta))
    mixed = scatter_stage([mixes[k] for k in range(NH)], "head", NH).astype(BF)
    sums = sum_pass(place, sums, (grad_beta,))
    grad_weight = scatter_stage(sums, "z", NZ)
    return (
        mixed,
        grad_query,
        grad_key,
        grad_value,
        grad_beta,
        grad_decay,
        (1.0 - position) * grad_weight,
        position * grad_weight,
    )


def solution(mesh):
    fine = Mesh(mesh.devices.reshape(NY, NZ, NC, NH), ("y", "z", "c", "head"))
    rows, flipped = P(RING, "head"), P("head", RING)
    return jax.shard_map(
        body,
        mesh=fine,
        in_specs=(rows, rows, rows, flipped, flipped, rows, rows, P(), rows),
        out_specs=(rows, rows, rows, rows, flipped, flipped, rows, rows),
        check_vma=False,
    )
```

```python
import jax
import jax.numpy as jnp
from jax import lax
from jax.experimental import pallas as pl
from jax.experimental.pallas import tpu as pltpu
from jax.sharding import Mesh, PartitionSpec as P

DK = 128
DV = 128
CURVE_POINTS = 257
EPS = 1e-06
NY, NZ, NC, NH = 4, 4, 2, 4
TOK = 256
HALF = 128
KEYS = 4
ROWS = 272
GROUP = 4
VMEM = 14 * 2**20
SHORT = 10**6
LONG = 5 * 10**9
BF = jnp.bfloat16
F32 = jnp.float32
RING = ("y", "z", "c")
INTERPRET = False


def dot(left, right, dims):
    return lax.dot_general(
        left.astype(BF), right.astype(BF), (dims, ((), ())), preferred_element_type=F32
    )


def mm(left, right):
    return dot(left, right, ((1,), (0,)))


def mm_nt(left, right):
    return dot(left, right, ((1,), (1,)))


def mm_tn(left, right):
    return dot(left, right, ((0,), (0,)))


def iota(shape, dim):
    return lax.broadcasted_iota(jnp.int32, shape, dim)


def lane_sum(array):
    return jnp.sum(array, axis=1, keepdims=True)


def call(
    kernel, out_shape, grid, in_specs, out_specs, args, flops, prefetch=None, after=(), vmem=VMEM
):
    count = len(args) + (prefetch is not None)

    def run(*refs):
        kernel(*refs[:count], *refs[count + len(after) :])

    in_specs = [*in_specs, *(pl.BlockSpec(memory_space=pl.ANY) for _ in after)]
    args = (*args, *after)
    spec = dict(grid=grid, in_specs=in_specs, out_specs=out_specs)
    extra = {}
    if prefetch is None:
        extra = spec
    else:
        extra = dict(grid_spec=pltpu.PrefetchScalarGridSpec(num_scalar_prefetch=1, **spec))
        args = (prefetch, *args)
    return pl.pallas_call(
        run,
        out_shape=out_shape,
        compiler_params=pltpu.CompilerParams(vmem_limit_bytes=vmem),
        cost_estimate=pl.CostEstimate(flops=flops, bytes_accessed=1, transcendentals=0),
        interpret=INTERPRET,
        name=kernel.__name__,
        **extra,
    )(*args)


def shape(*dims, dtype=F32):
    return jax.ShapeDtypeStruct(dims, dtype)


def whole(array):
    return pl.BlockSpec(array.shape, lambda *_: (0,) * len(array.shape))


def heads_spec(rows, cols):
    return pl.BlockSpec((GROUP, rows, cols), lambda s, place: (s, 0, 0))


def lead_spec(rows, cols):
    return pl.BlockSpec((2, rows, cols), lambda s, place: (s, 0, 0))


def half_of(step, place):
    return (1 - place[3] + step) % 2


def key_head(i, place_ref):
    return 2 * half_of(pl.program_id(0), place_ref) + i


def wide_spec(cols):
    return pl.BlockSpec((TOK, 2 * cols), lambda s, place: (0, half_of(s, place)))


def gate_parts(gate):
    full = jnp.broadcast_to(gate, (16, DK))
    one = full.astype(BF)
    two = (full - one.astype(F32)).astype(BF)
    three = (full - one.astype(F32) - two.astype(F32)).astype(BF)
    place = iota((16, DK), 0)
    parts = jnp.where(place == 0, one.astype(F32), 0.0)
    parts = jnp.where(place == 1, two.astype(F32), parts)
    return jnp.where(place == 2, three.astype(F32), parts).astype(BF)


def gate_of(block):
    return jnp.sum(block[2 * DK :, :].astype(F32), axis=0, keepdims=True)


def unit_keys(key_block):
    raw = key_block.astype(F32)
    rate = lax.rsqrt(lane_sum(raw * raw) + EPS)
    return raw * rate, rate


def prefix_lanes(array):
    size = array.shape[1]
    lane = iota(array.shape, 1)
    step = 1
    while step < size:
        array = array + jnp.where(lane >= step, pltpu.roll(array, step, 1), 0.0)
        step *= 2
    return array


def suffix_lanes(array):
    size = array.shape[1]
    lane = iota(array.shape, 1)
    step = 1
    while step < size:
        array = array + jnp.where(lane < size - step, pltpu.roll(array, size - step, 1), 0.0)
        step *= 2
    return array


def invert_blocks(lowers):
    row, col = iota((HALF, HALF), 0), iota((HALF, HALF), 1)
    apart = row ^ col
    eye = jnp.where(row == col, 1.0, 0.0)
    found = [eye - jnp.where(apart < 2, low, 0.0) for low in lowers]
    size = 2
    while size < HALF:
        mask = (apart >= size) & (apart < 2 * size)
        offs = [jnp.where(mask, low, 0.0).astype(BF) for low in lowers]
        lows = [x.astype(BF) for x in found]
        halfway = [mm(x, off) for x, off in zip(lows, offs)]
        found = [f - mm(m, x) for f, m, x in zip(found, halfway, lows)]
        size *= 2
    return found


def pre_kernel(
    place_ref, k_ref, v_ref, beta_ref, decay_ref, sent_ref, kept_ref, x_ref, wu_ref, c_ref, cols_ref
):
    step = pl.program_id(0)

    @pl.when(step == 0)
    def _():
        c_ref[...] = prefix_lanes(decay_ref[...])

    strict = iota((TOK, TOK), 0) > iota((TOK, TOK), 1)
    sub = iota((8, TOK), 0)
    units, columns, lowers = [], [], []
    for i in range(2):
        j = key_head(i, place_ref)
        unit, _ = unit_keys(k_ref[:, i * DK : (i + 1) * DK])
        low = unit.astype(BF)
        gram = mm_nt(low, low)
        rows = [c_ref[pl.ds(2 * j + a, 1), :] for a in range(2)]
        rates = [beta_ref[pl.ds(2 * j + a, 1), :] for a in range(2)]
        packed = jnp.zeros((8, TOK), F32)
        for spot, line in enumerate((*rows, *rates)):
            packed = jnp.where(sub == spot, line, packed)
        cols = jnp.transpose(jnp.concatenate([packed, jnp.zeros((HALF - 8, TOK), F32)], axis=0))
        cols_ref[i] = cols
        units.append(unit)
        columns.append(cols)
        for a in range(2):
            ratio = jnp.exp(jnp.minimum(cols[:, a : a + 1] - rows[a], 0.0))
            lowers.append(jnp.where(strict, cols[:, 2 + a : 3 + a] * gram * ratio, 0.0))
    found = invert_blocks(
        [low[b * HALF : (b + 1) * HALF, b * HALF : (b + 1) * HALF] for low in lowers for b in (0, 1)]
    )
    for h in range(GROUP):
        i, a = h // 2, h % 2
        unit, cols = units[i], columns[i]
        first, second = found[2 * h].astype(BF), found[2 * h + 1].astype(BF)
        corner = -mm(mm(second, lowers[h][HALF:, :HALF]), first)
        inverse = jnp.concatenate(
            [
                jnp.concatenate([first, jnp.zeros((HALF, HALF), BF)], axis=1),
                jnp.concatenate([corner.astype(BF), second], axis=1),
            ],
            axis=0,
        )
        x_ref[h] = inverse
        c_col, beta_col = cols[:, a : a + 1], cols[:, 2 + a : 3 + a]
        value = v_ref[:, h * DK : (h + 1) * DK].astype(F32)
        right = jnp.concatenate(
            [(beta_col * jnp.exp(c_col) * unit).astype(BF), (beta_col * value).astype(BF)], axis=1
        )
        wu = mm(inverse, right).astype(BF)
        wu_ref[h] = wu
        end = c_col[TOK - 1 : TOK, :]
        moved = mm_tn(wu, jnp.exp(end - c_col) * unit).astype(BF)
        gate = gate_parts(jnp.exp(end))

        @pl.when(step == 0)
        def _():
            sent_ref[h, : 2 * DK, :] = moved
            sent_ref[h, 2 * DK :, :] = gate

        @pl.when(step == 1)
        def _():
            kept_ref[h, : 2 * DK, :] = moved
            kept_ref[h, 2 * DK :, :] = gate


def pre_pass(place, key, value, beta, decay):
    heads = 2 * KEYS
    pay = shape(GROUP, ROWS, DK, dtype=BF)

    return call(
        pre_kernel,
        (
            pay,
            pay,
            shape(heads, TOK, TOK, dtype=BF),
            shape(heads, TOK, 2 * DK, dtype=BF),
            shape(heads, TOK),
            shape(KEYS, TOK, DK),
        ),
        (2,),
        [wide_spec(DK), wide_spec(2 * DK), whole(beta), whole(decay)],
        (
            whole(pay),
            whole(pay),
            heads_spec(TOK, TOK),
            heads_spec(TOK, 2 * DK),
            whole(decay),
            lead_spec(TOK, DK),
        ),
        (key, value, beta, decay),
        SHORT,
        prefetch=place,
    )


def attend_kernel(
    place_ref, q_ref, k_ref, c_ref, cols_ref, x_ref, wu_ref, p_ref, car_ref, out_ref, xz_ref
):
    inclusive = iota((TOK, TOK), 0) >= iota((TOK, TOK), 1)
    for i in range(2):
        j = key_head(i, place_ref)
        unit, _ = unit_keys(k_ref[:, i * DK : (i + 1) * DK])
        query = q_ref[:, i * DK : (i + 1) * DK]
        gram = mm_nt(query, unit)
        cols = cols_ref[i]
        for a in range(2):
            h = 2 * i + a
            c_col = cols[:, a : a + 1]
            ratio = jnp.exp(jnp.minimum(c_col - c_ref[pl.ds(2 * j + a, 1), :], 0.0))
            attend = jnp.where(inclusive, gram * ratio, 0.0).astype(BF)
            p_ref[h] = attend
            both = mm(attend, wu_ref[h])
            car_ref[h] = (jnp.exp(c_col) * query.astype(F32) - both[:, :DK]).astype(BF)
            out_ref[h] = both[:, DK:]
            tail = jnp.exp(c_col[TOK - 1 : TOK, :] - c_col) * unit
            xz_ref[h] = mm_tn(x_ref[h], tail).astype(BF)


def attend_pass(place, query, key, cums, cols, inverse, wu, after):
    heads = 2 * KEYS
    return call(
        attend_kernel,
        (
            shape(heads, TOK, TOK, dtype=BF),
            shape(heads, TOK, DK, dtype=BF),
            shape(heads, TOK, DK),
            shape(heads, TOK, DK, dtype=BF),
        ),
        (2,),
        [
            wide_spec(DK),
            wide_spec(DK),
            whole(cums),
            lead_spec(TOK, DK),
            heads_spec(TOK, TOK),
            heads_spec(TOK, 2 * DK),
        ],
        (
            heads_spec(TOK, TOK),
            heads_spec(TOK, DK),
            heads_spec(TOK, DK),
            heads_spec(TOK, DK),
        ),
        (query, key, cums, cols, inverse, wu),
        LONG,
        prefetch=place,
        after=after,
    )


def single(kernel, outs, args, place, after=(), cost=SHORT):
    return call(
        kernel,
        outs,
        (1,),
        [whole(a) for a in args],
        tuple(whole(o) for o in outs),
        args,
        cost,
        prefetch=place,
        after=after,
    )


def pair_kernel(place_ref, kept_ref, got_ref, *out_refs):
    z, core = place_ref[2], place_ref[3]
    for k in range(NZ):
        head = (z + k) % NZ
        kept, got = kept_ref[head], got_ref[head]
        early, late = jnp.where(core == 0, kept, got), jnp.where(core == 0, got, kept)
        early_gate, late_gate = gate_of(early), gate_of(late)
        moved = late[:DK].astype(F32)
        out_refs[k][: 2 * DK, :] = (
            late_gate * early[: 2 * DK].astype(F32)
            - mm(early[: 2 * DK], late[:DK])
            + jnp.concatenate([early_gate * moved, late[DK : 2 * DK].astype(F32)], axis=0)
        ).astype(BF)
        out_refs[k][2 * DK :, :] = gate_parts(early_gate * late_gate)


def pair_pass(place, kept, got):
    return single(pair_kernel, (shape(ROWS, DK, dtype=BF),) * NZ, (kept, got), place)


def prefix_kernel(place_ref, *refs):
    parts, (row_ref, nx_ref, bx_ref, gx_ref, tot_ref) = refs[:NZ], refs[NZ:]
    z = place_ref[2]
    for k in range(NZ):
        row_ref[(z - k + NZ) % NZ] = parts[k][...]
    both = jnp.zeros((2 * DK, DK), F32)
    gate = jnp.ones((1, DK), F32)
    for i in range(NZ):
        nx_ref[i] = both[:DK].astype(BF)
        bx_ref[i] = both[DK:]
        gx_ref[i : i + 1, :] = gate
        block = row_ref[i]
        step_gate = gate_of(block)
        moved = block[:DK].astype(F32)
        both = (
            step_gate * both
            - mm(both, block[:DK])
            + jnp.concatenate([gate * moved, block[DK : 2 * DK].astype(F32)], axis=0)
        )
        gate = gate * step_gate
    tot_ref[: 2 * DK, :] = both.astype(BF)
    tot_ref[2 * DK :, :] = gate_parts(gate)


def prefix_pass(place, parts, after):
    outs = (
        shape(NZ, ROWS, DK, dtype=BF),
        shape(NZ, DK, DK, dtype=BF),
        shape(NZ, DK, DK),
        shape(8, DK),
        shape(ROWS, DK, dtype=BF),
    )
    return single(prefix_kernel, outs, parts, place, after)


def suffix_kernel(place_ref, row_ref, ns_ref, gs_ref):
    later = jnp.zeros((DK, DK), F32)
    gate = jnp.ones((1, DK), F32)
    for i in reversed(range(NZ)):
        ns_ref[i] = later.astype(BF)
        gs_ref[i : i + 1, :] = gate
        block = row_ref[i]
        step_gate = gate_of(block)
        moved = block[:DK]
        later = step_gate * later + gate * moved.astype(F32) - mm(moved, later)
        gate = gate * step_gate


def suffix_pass(place, row):
    return single(suffix_kernel, (shape(NZ, DK, DK, dtype=BF), shape(8, DK)), (row,), place, cost=LONG)


def enter_kernel(place_ref, one_ref, two_ref, three_ref, nx_ref, bx_ref, gx_ref, *out_refs):
    here, z = place_ref[1], place_ref[2]
    state = jnp.zeros((DK, DK), F32)
    for back, ref in ((3, three_ref), (2, two_ref), (1, one_ref)):
        block = ref[...]
        moved = gate_of(block) * state - mm(state, block[:DK]) + block[DK : 2 * DK].astype(F32)
        state = jnp.where(here >= back, moved, state)
    for k in range(NZ):
        i = (z + k) % NZ
        out_refs[k][...] = gx_ref[pl.ds(i, 1), :] * state - mm(state, nx_ref[i]) + bx_ref[i]


def enter_pass(place, totals, nx, bx, gx, after):
    outs = (shape(DK, DK),) * NZ
    return single(enter_kernel, outs, (*totals, nx, bx, gx), place, after)


def split_kernel(place_ref, *refs):
    states, (kept_ref, got_ref, own_ref, send_ref) = refs[:NZ], refs[NZ:]
    z, first = place_ref[2], place_ref[3] == 0
    for k in range(NZ):
        head = (z - k + NZ) % NZ
        early = jnp.where(first, kept_ref[head], got_ref[head])
        state = states[k][...]
        moved = (
            gate_of(early) * state - mm(state, early[:DK]) + early[DK : 2 * DK].astype(F32)
        )
        own_ref[head] = jnp.where(first, state, moved)
        send_ref[head] = jnp.where(first, moved, state)


def split_pass(place, states, kept, got, after):
    outs = (shape(GROUP, DK, DK),) * 2
    return single(split_kernel, outs, (*states, kept, got), place, after)


def two_parts(array):
    high = array.astype(BF)
    return high, (array - high.astype(F32)).astype(BF)


def select(theirs_ref, mine_ref, h):
    return jnp.where(pl.program_id(0) == 0, theirs_ref[h], mine_ref[h])


def norm_kernel(
    place_ref, got_ref, own_ref, car_ref, loc_ref, gn_ref,
    norm_ref, s_ref, do_ref, sent_ref, kept_ref,
):
    first = pl.program_id(0) == 0
    for h in range(GROUP):
        state, carried = select(got_ref, own_ref, h).astype(BF), car_ref[h]
        s_ref[h] = state
        head = loc_ref[h] + mm_nt(carried, state)
        scale = lax.rsqrt(lane_sum(head * head) * (1.0 / DK) + EPS)
        normed = head * scale
        norm_ref[:, h * DK : (h + 1) * DK] = normed.astype(BF)
        grad = gn_ref[:, h * DK : (h + 1) * DK]
        inner = lane_sum(grad * normed) * (1.0 / DK)
        back = scale * (grad - normed * inner)
        do_ref[h] = back
        both = mm_tn(jnp.concatenate(two_parts(back), axis=1), carried)
        direct = both[:DV] + both[DV:]

        @pl.when(first)
        def _():
            sent_ref[h] = direct

        @pl.when(jnp.logical_not(first))
        def _():
            kept_ref[h] = direct


def norm_pass(place, got, own, carried, local, grad_normed):
    heads = 2 * KEYS
    half = shape(GROUP, DK, DK)
    return call(
        norm_kernel,
        (
            shape(TOK, heads * DK, dtype=BF),
            shape(heads, DK, DK, dtype=BF),
            shape(heads, TOK, DK),
            half,
            half,
        ),
        (2,),
        [
            whole(got),
            whole(own),
            heads_spec(TOK, DK),
            heads_spec(TOK, DK),
            wide_spec(2 * DK),
        ],
        (wide_spec(2 * DK), heads_spec(DK, DK), heads_spec(TOK, DK), whole(half), whole(half)),
        (got, own, carried, local, grad_normed),
        SHORT,
        prefetch=place,
    )


def middle_kernel(
    place_ref, q_ref, k_ref, v_ref, c_ref, cols_ref, s_ref, do_ref, p_ref, x_ref, wu_ref,
    dq_ref, u_ref, dk_ref, e_ref, y_ref, dcc_ref, dcr_ref,
):
    inclusive = iota((TOK, TOK), 0) >= iota((TOK, TOK), 1)
    lane = iota((TOK, DK), 1)
    sub = iota((8, TOK), 0)
    for i in range(2):
        j = key_head(i, place_ref)
        unit, _ = unit_keys(k_ref[:, i * DK : (i + 1) * DK])
        low = unit.astype(BF)
        query = q_ref[:, i * DK : (i + 1) * DK]
        wide = query.astype(F32)
        cols = cols_ref[i]
        down = jnp.zeros((TOK, DK), F32)
        across = jnp.zeros((8, TOK), F32)
        pair_sum = jnp.zeros((TOK, TOK), F32)
        grad_query = jnp.zeros((TOK, DK), F32)
        for a in range(2):
            h = 2 * i + a
            c_col = cols[:, a : a + 1]
            growth = jnp.exp(c_col)
            state, attend = s_ref[h], p_ref[h]
            back, rest = two_parts(do_ref[h])
            update = (wu_ref[h, :, DK:].astype(F32) - mm_nt(wu_ref[h, :, :DK], state)).astype(BF)
            u_ref[h] = update
            pairs = mm_nt(back, update) + mm_nt(rest, update)
            ratio = jnp.exp(jnp.minimum(c_col - c_ref[pl.ds(2 * j + a, 1), :], 0.0))
            pair_sum += jnp.where(inclusive, pairs * ratio, 0.0)
            shares = pairs * attend.astype(F32)
            reached = growth * (mm(back, state) + mm(rest, state))
            grad_query += reached
            down = jnp.where(lane == a, lane_sum(shares) + lane_sum(reached * wide), down)
            across = jnp.where(sub == a, -jnp.sum(shares, axis=0, keepdims=True), across)
            e_ref[h] = mm_tn(x_ref[h], mm_tn(attend, back))
            value = v_ref[:, h * DK : (h + 1) * DK].astype(F32)
            y_ref[h] = (value - growth * mm_nt(low, state)).astype(BF)
        pair_low = pair_sum.astype(BF)
        dq_ref[:, i * DK : (i + 1) * DK] = grad_query + mm(pair_low, low)
        dk_ref[:, i * DK : (i + 1) * DK] = mm_tn(pair_low, query)
        dcc_ref[i] = down
        dcr_ref[i] = across


def middle_pass(place, query, key, value, cums, cols, state, back, attend, inverse, wu):
    heads = 2 * KEYS
    return call(
        middle_kernel,
        (
            shape(TOK, KEYS * DK),
            shape(heads, TOK, DK, dtype=BF),
            shape(TOK, KEYS * DK),
            shape(heads, TOK, DK),
            shape(heads, TOK, DK, dtype=BF),
            shape(KEYS, TOK, DK),
            shape(KEYS, 8, TOK),
        ),
        (2,),
        [
            wide_spec(DK),
            wide_spec(DK),
            wide_spec(2 * DK),
            whole(cums),
            lead_spec(TOK, DK),
            heads_spec(DK, DK),
            heads_spec(TOK, DK),
            heads_spec(TOK, TOK),
            heads_spec(TOK, TOK),
            heads_spec(TOK, 2 * DK),
        ],
        (
            wide_spec(DK),
            heads_spec(TOK, DK),
            wide_spec(DK),
            heads_spec(TOK, DK),
            heads_spec(TOK, DK),
            lead_spec(TOK, DK),
            lead_spec(8, TOK),
        ),
        (query, key, value, cums, cols, state, back, attend, inverse, wu),
        2 * LONG,
        prefetch=place,
    )


def join_kernel(place_ref, kept_ref, got_ref, dkept_ref, dgot_ref, *out_refs):
    z, first = place_ref[2], place_ref[3] == 0
    for k in range(NZ):
        head = (z + k) % NZ
        early = jnp.where(first, kept_ref[head], got_ref[head])
        before = jnp.where(first, dkept_ref[head], dgot_ref[head])
        after = jnp.where(first, dgot_ref[head], dkept_ref[head])
        out_refs[k][...] = gate_of(early) * after - mm_nt(after, early[:DK]) + before


def join_pass(place, kept, got, dkept, dgot, after):
    outs = (shape(DK, DK),) * NZ
    return single(join_kernel, outs, (kept, got, dkept, dgot), place, after)


def later_kernel(place_ref, *refs):
    parts, (row_ref, d_ref, tot_ref, line_ref) = refs[:NZ], refs[NZ:]
    z = place_ref[2]
    for k in range(NZ):
        line_ref[(z - k + NZ) % NZ] = parts[k][...]
    total = jnp.zeros((DK, DK), F32)
    for i in reversed(range(NZ)):
        d_ref[i] = total
        block = row_ref[i]
        total = gate_of(block) * total - mm_nt(total, block[:DK]) + line_ref[i]
    tot_ref[...] = total


def later_pass(place, parts, row, after):
    outs = (shape(NZ, DK, DK), shape(DK, DK), shape(NZ, DK, DK))
    return single(later_kernel, outs, (*parts, row), place, after)


def leave_kernel(
    place_ref, one_ref, two_ref, three_ref, g1_ref, g2_ref, g3_ref, ns_ref, gs_ref, d_ref, *out_refs
):
    here, z = place_ref[1], place_ref[2]
    total = jnp.zeros((DK, DK), F32)
    for ahead, ref, grad in ((3, one_ref, g3_ref), (2, two_ref, g2_ref), (1, three_ref, g1_ref)):
        block = ref[...]
        moved = gate_of(block) * total - mm_nt(total, block[:DK]) + grad[...]
        total = jnp.where(here + ahead < NY, moved, total)
    for k in range(NZ):
        i = (z + k) % NZ
        out_refs[k][...] = gs_ref[pl.ds(i, 1), :] * total - mm_nt(total, ns_ref[i]) + d_ref[i]


def leave_pass(place, totals, grads, ns, gs, directs, after):
    outs = (shape(DK, DK),) * NZ
    return single(leave_kernel, outs, (*totals, *grads, ns, gs, directs), place, after)


def part_kernel(place_ref, *refs):
    grads, (kept_ref, got_ref, dkept_ref, dgot_ref, own_ref, send_ref) = refs[:NZ], refs[NZ:]
    z, first = place_ref[2], place_ref[3] == 0
    for k in range(NZ):
        head = (z - k + NZ) % NZ
        late = jnp.where(first, got_ref[head], kept_ref[head])
        direct = jnp.where(first, dgot_ref[head], dkept_ref[head])
        grad = grads[k][...]
        moved = gate_of(late) * grad - mm_nt(grad, late[:DK]) + direct
        own_ref[head] = jnp.where(first, moved, grad)
        send_ref[head] = jnp.where(first, grad, moved)


def part_pass(place, grads, kept, got, dkept, dgot, after):
    outs = (shape(GROUP, DK, DK),) * 2
    return single(part_kernel, outs, (*grads, kept, got, dkept, dgot), place, after)


def last_kernel(
    place_ref, k_ref, c_ref, cols_ref, s_ref, ggot_ref, gown_ref, e_ref, y_ref, u_ref, xz_ref,
    dk0_ref, dcc_ref, dcr_ref, dv_ref, dk_ref, db_ref, dd_ref,
):
    strict = iota((TOK, TOK), 0) > iota((TOK, TOK), 1)
    last = iota((TOK, 1), 0) == TOK - 1
    lane = iota((TOK, DK), 1)
    sub = iota((8, TOK), 0)
    for i in range(2):
        j = key_head(i, place_ref)
        unit, rate = unit_keys(k_ref[:, i * DK : (i + 1) * DK])
        low = unit.astype(BF)
        gram = mm_nt(low, low)
        cols = cols_ref[i]
        down = jnp.zeros((TOK, DK), F32)
        pair_sum = jnp.zeros((TOK, TOK), F32)
        grad_key = dk0_ref[:, i * DK : (i + 1) * DK]
        across = []
        for a in range(2):
            h = 2 * i + a
            c_col, beta_col = cols[:, a : a + 1], cols[:, 2 + a : 3 + a]
            growth = jnp.exp(c_col)
            end = c_col[TOK - 1 : TOK, :]
            state, later, update = s_ref[h], select(ggot_ref, gown_ref, h), u_ref[h]
            error = e_ref[h] + mm_nt(xz_ref[h], later)
            ratio = jnp.exp(jnp.minimum(c_col - c_ref[pl.ds(2 * j + a, 1), :], 0.0))
            pairs = jnp.where(strict, -mm_nt(error, update) * ratio, 0.0)
            shares = pairs * gram
            row_share = lane_sum(shares)
            across.append(jnp.sum(beta_col * shares, axis=0, keepdims=True))
            pair_sum += beta_col * pairs
            grad_value = beta_col * error
            dv_ref[:, h * DK : (h + 1) * DK] = grad_value
            reached = growth * mm(grad_value, state)
            tail = jnp.exp(end - c_col) * mm(update, later)
            grad_key += tail - reached
            tail_share = lane_sum(tail * unit)
            gate_share = jnp.exp(end) * jnp.sum(
                lane_sum(state.astype(F32) * later.astype(F32)), axis=0, keepdims=True
            )
            total = jnp.sum(tail_share, axis=0, keepdims=True) + gate_share
            grad_cum = beta_col * row_share - lane_sum(reached * unit) - tail_share
            grad_cum += jnp.where(last, total, 0.0)
            grad_beta = row_share + lane_sum(error * y_ref[h].astype(F32))
            down = jnp.where(lane == a, grad_cum, jnp.where(lane == 2 + a, grad_beta, down))
        pair_low = pair_sum.astype(BF)
        grad_key += mm(pair_low, low) + mm_tn(pair_low, low)
        dk_ref[:, i * DK : (i + 1) * DK] = rate * (grad_key - unit * lane_sum(unit * grad_key))
        turned = jnp.transpose(down + jnp.where(lane < 2, dcc_ref[i], 0.0))[:8]
        cum = turned + dcr_ref[i]
        for a in range(2):
            cum = jnp.where(sub == a, cum - across[a], cum)
        decayed = suffix_lanes(cum)
        for a in range(2):
            dd_ref[pl.ds(2 * j + a, 1), :] = decayed[a : a + 1]
            db_ref[pl.ds(2 * j + a, 1), :] = turned[2 + a : 3 + a]


def last_pass(place, key, cums, cols, state, got, own, error, y, update, xz, dk0, dcc, dcr, after):
    heads = 2 * KEYS
    return call(
        last_kernel,
        (
            shape(TOK, heads * DK),
            shape(TOK, KEYS * DK),
            shape(heads, TOK),
            shape(heads, TOK),
        ),
        (2,),
        [
            wide_spec(DK),
            whole(cums),
            lead_spec(TOK, DK),
            heads_spec(DK, DK),
            whole(got),
            whole(own),
            heads_spec(TOK, DK),
            heads_spec(TOK, DK),
            heads_spec(TOK, DK),
            heads_spec(TOK, DK),
            wide_spec(DK),
            lead_spec(TOK, DK),
            lead_spec(8, TOK),
        ],
        (wide_spec(2 * DK), wide_spec(DK), whole(cums), whole(cums)),
        (key, cums, cols, state, got, own, error, y, update, xz, dk0, dcc, dcr),
        SHORT,
        prefetch=place,
        after=after,
    )


def back_kernel(place_ref, cot_ref, w_ref, out_ref):
    part = mm(cot_ref[0], w_ref[...])

    @pl.when(pl.program_id(0) == 0)
    def _():
        out_ref[...] = part

    @pl.when(pl.program_id(0) > 0)
    def _():
        out_ref[...] += part


def back_pass(place, cot, weight, after):
    depth, wide = cot.shape[2], weight.shape[1]
    out = shape(TOK, wide)
    return call(
        back_kernel,
        (out,),
        (NH,),
        [
            pl.BlockSpec((1, TOK, depth), lambda k, place: (k, 0, 0)),
            pl.BlockSpec((depth, wide), lambda k, place: ((place[0] + k) % NH, 0)),
        ],
        (whole(out),),
        (cot, weight),
        LONG,
        prefetch=place,
        after=after,
    )[0]


def mix_kernel(place_ref, norm_ref, w_ref, out_ref):
    out_ref[0] = mm_nt(norm_ref[...], w_ref[...]).astype(BF)


def mix_pass(place, normed, weight, after):
    depth = weight.shape[0] // NH
    out = shape(NH, TOK, depth, dtype=BF)
    return call(
        mix_kernel,
        (out,),
        (NH,),
        [
            whole(normed),
            pl.BlockSpec((depth, weight.shape[1]), lambda k, place: ((place[0] + k) % NH, 0)),
        ],
        (pl.BlockSpec((1, TOK, depth), lambda k, place: (k, 0, 0)),),
        (normed, weight),
        LONG,
        prefetch=place,
        after=after,
    )[0]


def outer_kernel(place_ref, cot_ref, norm_ref, mine_ref, other_ref):
    here, core = place_ref[2], place_ref[3]
    rows = mine_ref.shape[2]
    for k in range(NZ):
        start = pl.multiple_of(((here + k) % NZ) * 2 * rows, 2 * rows)
        part = mm_tn(cot_ref[0, :, pl.ds(start, 2 * rows)], norm_ref[...]).astype(BF)
        first = core == 0
        mine_ref[0, k] = jnp.where(first, part[:rows], part[rows:])
        other_ref[0, k] = jnp.where(first, part[rows:], part[:rows])


def outer_pass(place, cot, normed, after):
    rows = cot.shape[2] // (NZ * NC)
    out = shape(NY, NZ, rows, normed.shape[1], dtype=BF)
    spec = pl.BlockSpec((1, NZ, rows, normed.shape[1]), lambda k, place: (k, 0, 0, 0))
    return call(
        outer_kernel,
        (out, out),
        (NY,),
        [
            pl.BlockSpec(
                (1, TOK, cot.shape[2]), lambda k, place: ((place[1] + k - place[0] + NH) % NH, 0, 0)
            ),
            whole(normed),
        ],
        (spec, spec),
        (cot, normed),
        LONG,
        prefetch=place,
        after=after,
    )


def blend_kernel(place_ref, mine_ref, other_ref, *out_refs):
    wide = mine_ref.shape[3] // 2
    for y in range(NY):
        for z in range(NZ):
            total = (mine_ref[y, z].astype(F32) + other_ref[y, z].astype(F32)).astype(BF)
            out_refs[z][y] = total[:, :wide]
            out_refs[NZ + y][z] = total[:, wide:]


def blend_pass(place, mine, other, after):
    rows, cols = mine.shape[2:]
    outs = (shape(NY, rows, cols // 2, dtype=BF),) * NZ + (shape(NZ, rows, cols // 2, dtype=BF),) * NY
    parts = single(blend_kernel, outs, (mine, other), place, after, LONG)
    return parts[:NZ], parts[NZ:]


def sum_kernel(place_ref, *refs):
    ins, outs = refs[: NZ + NY], refs[NZ + NY :]
    for y in range(NY):
        outs[y][...] = sum(ins[z][y].astype(F32) for z in range(NZ)).astype(BF)
    for z in range(NZ):
        outs[NY + z][...] = sum(ins[NZ + y][z].astype(F32) for y in range(NY)).astype(BF)


def sum_pass(place, left, right, after):
    outs = (shape(*left[0].shape[1:], dtype=BF),) * (NY + NZ)
    parts = single(sum_kernel, outs, (*left, *right), place, after)
    return parts[:NY], parts[NY:]


def shift(array, axis, count, step):
    return lax.ppermute(array, axis, [(i, (i + step) % count) for i in range(count)])


def spread(parts, axis, count, sign=1):
    return [parts[0]] + [shift(parts[k], axis, count, sign * k) for k in range(1, count)]


def scatter_stage(parts, axis, count):
    return sum(part.astype(F32) for part in spread(parts, axis, count))


def swap(array):
    return lax.ppermute(array, "c", [(0, 1), (1, 0)])


def body(query, key, value, beta, decay, wo_start, wo_end, curve_index, cotangent):
    place = jnp.stack([lax.axis_index(a) for a in ("head", "y", "z", "c")]).astype(jnp.int32)
    position = curve_index[0].astype(F32) / (CURVE_POINTS - 1)
    weight_local = (
        (1.0 - position) * wo_start.astype(F32) + position * wo_end.astype(F32)
    ).astype(BF)
    weight = lax.all_gather(weight_local, RING, axis=0, tiled=True)
    cot = jnp.stack([cotangent] + [shift(cotangent, "head", NH, -k) for k in range(1, NH)])

    sent, kept, inverse, wu, cums, cols = pre_pass(place, key, value, beta, decay)
    got = swap(sent)
    parts = spread(pair_pass(place, kept, got), "z", NZ)
    attend, carried, local, xz = attend_pass(
        place, query, key, cums, cols, inverse, wu, (parts[0],)
    )
    row, nx, bx, gx, total = prefix_pass(place, parts, (xz,))
    totals = [shift(total, "y", NY, k) for k in range(1, NY)]
    ns, gs = suffix_pass(place, row)
    states = spread(enter_pass(place, totals, nx, bx, gx, (ns,)), "z", NZ)
    grad_normed = back_pass(place, cot, weight, (ns,))
    own, send = split_pass(place, states, kept, got, (grad_normed,))
    normed, state, back, dsent, dkept = norm_pass(
        place, swap(send), own, carried, local, grad_normed
    )

    dgot = swap(dsent)
    grad_parts = spread(join_pass(place, kept, got, dkept, dgot, ()), "z", NZ)
    mine, other = outer_pass(place, cot, normed, (dgot,))
    theirs = swap(other)
    mixes = mix_pass(place, normed, weight, (grad_parts[0],))
    suffixes, grad_total, _ = later_pass(place, grad_parts, row, (mixes,))
    grads = [shift(grad_total, "y", NY, -k) for k in range(1, NY)]
    grad_query, update, dk0, error, y, dcc, dcr = middle_pass(
        place, query, key, value, cums, cols, state, back, attend, inverse, wu
    )
    laters = spread(leave_pass(place, totals, grads, ns, gs, suffixes, (dk0,)), "z", NZ)
    left, right = blend_pass(place, mine, theirs, (laters[0],))
    left, right = spread(left, "z", NZ), spread(right, "y", NY)
    gown, gsend = part_pass(place, laters, kept, got, dkept, dgot, (left[0],))
    ggot = swap(gsend)

    grad_value, grad_key, grad_beta, grad_decay = last_pass(
        place, key, cums, cols, state, ggot, gown, error, y, update, xz, dk0, dcc, dcr, ()
    )
    mixes, grad_beta = lax.optimization_barrier((mixes, grad_beta))
    mixed = scatter_stage([mixes[k] for k in range(NH)], "head", NH).astype(BF)
    left, right = sum_pass(place, left, right, (grad_beta,))
    left, right = scatter_stage(left, "y", NY), scatter_stage(right, "z", NZ)
    grad_weight = jnp.concatenate([left, right], axis=-1)
    return (
        mixed,
        grad_query,
        grad_key,
        grad_value,
        grad_beta,
        grad_decay,
        (1.0 - position) * grad_weight,
        position * grad_weight,
    )


def solution(mesh):
    fine = Mesh(mesh.devices.reshape(NY, NZ, NC, NH), ("y", "z", "c", "head"))
    rows, flipped = P(RING, "head"), P("head", RING)
    return jax.shard_map(
        body,
        mesh=fine,
        in_specs=(rows, rows, rows, flipped, flipped, rows, rows, P(), rows),
        out_specs=(rows, rows, rows, rows, flipped, flipped, rows, rows),
        check_vma=False,
    )
```
